128 devices in a mesh: dev: 128 (over y, x, z, core).
Axes of the slice: x: 4, y: 4, z: 4, core: 2. Of those that a mesh axis runs over, the one named last changes fastest.
Arguments:
- params: float32 [59, 655360], P(None, 'dev'), as said below
- requests: int32 [128, 128, 40], P('dev'), may hold values from 0 to 5119, as said below
- tile_slots: int32 [2048, 512], P('dev'), may hold values from 0 to 5119, as said below
- tile_count: int32 [2048], P('dev'), may hold values from 128 to 512, as said below
- tile_place: int32 [2048], P('dev'), may hold values from 0 to 8159, as said below
- target: float32 [2048, 3, 256], P('dev'), may hold values from 0 to 1
Outputs:
- rendered: float32 [2048, 3, 256], P('dev')
- gradient: float32 [59, 655360], P(None, 'dev')
The draws below stay inside these ranges and needn't reach their ends.
Inputs may be any that keep to these rules, and one draw needn't show every extreme that they name: requests[d, p, c] is a row (0 to 5119) of owner p's Gaussians; for each owner the lists of all devices name each of its rows exactly once. `tile_slots`: entries k < tile_count of a tile are rows of its device's received block, in front-to-back order; entries beyond hold 0; over the 16 tiles of a device every received row is listed exactly once. `tile_count`: the counts of one device's tiles sum to 5120. `tile_place`: all entries are distinct. `params`: row 2 lies between 2 and 8; row 6 between 0.5 and 1.5; rows 7 to 9 between -1 and 1.
All inputs are finite; a program needn't handle non-finite values.
Results may differ from the reference program's by a relative error of at most 0.0003.
Values sent between devices are 32-bit elements; how exact they have to be, the bound alone decides.
A program may use at most 128 MiB of HBM per device.

```python
import jax
import jax.numpy as jnp
from jax import lax

PARAMS = 59
TILE_DEV = 16
M = 320
K_MAX = 512
G_DEV = 5120
GAUSS = 655360
CAP = 40
TILES = 2048
N_DEV = 128


def layout(key):
    owner_key, order_key, count_key, device_key, pair_key, place_key, shuffle_key = jax.random.split(key, 7)
    owner_order = jax.vmap(lambda subkey: jax.random.permutation(subkey, G_DEV))(jax.random.split(owner_key, N_DEV)).astype(jnp.int32)
    requests = owner_order.reshape(N_DEV, N_DEV, CAP).transpose(1, 0, 2)
    list_order = jax.vmap(lambda subkey: jax.random.permutation(subkey, G_DEV))(jax.random.split(order_key, N_DEV)).astype(jnp.int32)
    limit = K_MAX - M
    offsets = jax.random.randint(count_key, (N_DEV, TILE_DEV // 2), -limit, limit + 1, dtype=jnp.int32)
    forced_device = jax.random.randint(device_key, (), 0, N_DEV, dtype=jnp.int32)
    forced_pair = jax.random.randint(pair_key, (), 0, TILE_DEV // 2, dtype=jnp.int32)
    offsets = offsets.at[forced_device, forced_pair].set(limit)
    counts = jnp.stack([M + offsets, M - offsets], axis=-1).reshape(N_DEV, TILE_DEV).astype(jnp.int32)
    starts = jnp.cumsum(counts, axis=1).astype(jnp.int32) - counts
    steps_along = jnp.arange(K_MAX, dtype=jnp.int32)
    spots = starts[:, :, None] + steps_along[None, None, :]
    present = steps_along[None, None, :] < counts[:, :, None]
    picked = jax.vmap(lambda order, spot: order[jnp.clip(spot, 0, G_DEV - 1)])(list_order, spots)
    slots = jnp.where(present, picked, 0).astype(jnp.int32)
    middle = 1 + jax.random.permutation(place_key, 8158).astype(jnp.int32)
    chosen = jnp.concatenate([jnp.array([0, 8159], jnp.int32), middle[:TILES - 2]])
    places = jax.random.permutation(shuffle_key, chosen).astype(jnp.int32)
    return (requests, owner_order, list_order, counts, starts, slots, places)


def draw_requests(key, part):
    return layout(key)[0]


def draw_tile_slots(key, part):
    return layout(key)[5].reshape(TILES, K_MAX)


def draw_tile_count(key, part):
    return layout(key)[3].reshape(TILES)


def draw_tile_place(key, part):
    return layout(key)[6]


def draw_params(key, part):
    requests, owner_order, list_order, counts, starts, slots, places = layout(key)
    key = jax.random.fold_in(key, 11)
    keys = jax.random.split(key, 9)
    series = jnp.arange(G_DEV, dtype=jnp.int32)
    owner_inverse = jax.vmap(lambda order: jnp.zeros((G_DEV,), jnp.int32).at[order].set(series))(owner_order)
    list_inverse = jax.vmap(lambda order: jnp.zeros((G_DEV,), jnp.int32).at[order].set(series))(list_order)
    requester = owner_inverse // CAP
    block_row = jnp.arange(N_DEV, dtype=jnp.int32)[:, None] * CAP + owner_inverse % CAP
    position = list_inverse[requester, block_row]
    tile_index = jnp.sum((position[:, :, None] >= starts[requester]).astype(jnp.int32), axis=-1) - 1
    image_tile = places[requester * TILE_DEV + tile_index]
    shape = (N_DEV, G_DEV)
    depth = 2.0 + 6.0 * (position.astype(jnp.float32) + 0.5 * jax.random.uniform(keys[0], shape)) / G_DEV
    screen_x = 16.0 * (image_tile % 120).astype(jnp.float32) + 16.0 * jax.random.uniform(keys[1], shape)
    screen_y = 16.0 * (image_tile // 120).astype(jnp.float32) + 16.0 * jax.random.uniform(keys[2], shape)
    mean_x = (screen_x - 960.0) * depth / 1200.0
    mean_y = (screen_y - 540.0) * depth / 1200.0
    log_scales = jnp.log(depth / 1200.0)[None] + jax.random.uniform(keys[3], (3,) + shape, minval=0.0, maxval=1.6)
    real_part = jax.random.uniform(keys[4], (1,) + shape, minval=0.5, maxval=1.5)
    imag_part = jax.random.uniform(keys[5], (3,) + shape, minval=-1.0, maxval=1.0)
    opacity = jax.random.uniform(keys[6], (1,) + shape, minval=-5.0, maxval=-2.5)
    base_colour = 0.6 * jax.random.normal(keys[7], (3,) + shape)
    higher = 0.25 * jax.random.normal(keys[8], (45,) + shape)
    rows = jnp.concatenate([mean_x[None], mean_y[None], depth[None], log_scales, real_part, imag_part, opacity, base_colour, higher], axis=0)
    return rows.reshape(PARAMS, N_DEV * G_DEV).astype(jnp.float32)


def block_scale(key, dims, shards, low, top_value):
    def one(dim, parts):
        draws = jax.random.uniform(jax.random.fold_in(jax.random.fold_in(key, 6), dim), (parts,), jnp.float32, low / len(shards), top_value / len(shards))
        return jnp.repeat(jnp.exp(draws), dims[dim] // parts).reshape((-1,) + (1,) * (len(dims) - dim - 1))

    level = one(*shards[0])
    for cut in shards[1:]:
        level = level * one(*cut)
    return level


def setup_inputs(seed: int = 0) -> dict:
    seeds = jax.random.split(jax.random.key(seed), 7)
    return {
        "params": draw_params(jax.random.fold_in(seeds[6], 71), 0),
        "requests": draw_requests(jax.random.fold_in(seeds[6], 71), 0),
        "tile_slots": draw_tile_slots(jax.random.fold_in(seeds[6], 71), 0),
        "tile_count": draw_tile_count(jax.random.fold_in(seeds[6], 71), 0),
        "tile_place": draw_tile_place(jax.random.fold_in(seeds[6], 71), 0),
        "target": jnp.clip(1.0 * jax.random.uniform(seeds[5], (TILES, 3, 256), jnp.float32) ** block_scale(seeds[5], (TILES, 3, 256), ((0, 128),), -0.2, 0.2), 0.0, 1.0),
    }


FOCAL_LENGTH = 1200.0
CENTER_X = 960.0
CENTER_Y = 540.0
DILATION = 0.3
BAND_ZERO = 0.28209479177387814
BAND_ONE = 0.4886025119029199
BAND_TWO = (1.0925484305920792, -1.0925484305920792, 0.31539156525252005, -1.0925484305920792, 0.5462742152960396)
BAND_THREE = (-0.5900435899266435, 2.890611442640554, -0.4570457994644658, 0.3731763325901154, -0.4570457994644658, 1.445305721320277, -0.5900435899266435)

def harmonics(facing_x, facing_y, facing_z):
    square_x = facing_x * facing_x
    square_y = facing_y * facing_y
    square_z = facing_z * facing_z
    terms = [BAND_ZERO * jnp.ones_like(facing_x), -BAND_ONE * facing_y, BAND_ONE * facing_z, -BAND_ONE * facing_x, BAND_TWO[0] * facing_x * facing_y, BAND_TWO[1] * facing_y * facing_z, BAND_TWO[2] * (2.0 * square_z - square_x - square_y), BAND_TWO[3] * facing_x * facing_z, BAND_TWO[4] * (square_x - square_y), BAND_THREE[0] * facing_y * (3.0 * square_x - square_y), BAND_THREE[1] * facing_x * facing_y * facing_z, BAND_THREE[2] * facing_y * (4.0 * square_z - square_x - square_y), BAND_THREE[3] * facing_z * (2.0 * square_z - 3.0 * square_x - 3.0 * square_y), BAND_THREE[4] * facing_x * (4.0 * square_z - square_x - square_y), BAND_THREE[5] * facing_z * (square_x - square_y), BAND_THREE[6] * facing_x * (square_x - 3.0 * square_y)]
    return jnp.stack(terms)

def project(gauss_rows):
    mean_x, mean_y, mean_z = (gauss_rows[0], gauss_rows[1], gauss_rows[2])
    scales = jnp.exp(gauss_rows[3:6])
    quaternion = gauss_rows[6:10] / jnp.sqrt(lax.optimization_barrier(jnp.sum(gauss_rows[6:10] * gauss_rows[6:10], axis=0)))
    real_w, imag_x, imag_y, imag_z = (quaternion[0], quaternion[1], quaternion[2], quaternion[3])
    rotation = [[1.0 - 2.0 * (imag_y * imag_y + imag_z * imag_z), 2.0 * (imag_x * imag_y - real_w * imag_z), 2.0 * (imag_x * imag_z + real_w * imag_y)], [2.0 * (imag_x * imag_y + real_w * imag_z), 1.0 - 2.0 * (imag_x * imag_x + imag_z * imag_z), 2.0 * (imag_y * imag_z - real_w * imag_x)], [2.0 * (imag_x * imag_z - real_w * imag_y), 2.0 * (imag_y * imag_z + real_w * imag_x), 1.0 - 2.0 * (imag_x * imag_x + imag_y * imag_y)]]
    spread = [[rotation[first][second] * scales[second] for second in range(3)] for first in range(3)]
    inverse_z = 1.0 / mean_z
    jac_diag = FOCAL_LENGTH * inverse_z
    jac_xz = -FOCAL_LENGTH * mean_x * inverse_z * inverse_z
    jac_yz = -FOCAL_LENGTH * mean_y * inverse_z * inverse_z
    across = [jac_diag * spread[0][second] + jac_xz * spread[2][second] for second in range(3)]
    upward = [jac_diag * spread[1][second] + jac_yz * spread[2][second] for second in range(3)]
    cov_xx = across[0] * across[0] + across[1] * across[1] + across[2] * across[2] + DILATION
    cov_xy = across[0] * upward[0] + across[1] * upward[1] + across[2] * upward[2]
    cov_yy = upward[0] * upward[0] + upward[1] * upward[1] + upward[2] * upward[2] + DILATION
    determinant = cov_xx * cov_yy - cov_xy * cov_xy
    screen_x = FOCAL_LENGTH * mean_x * inverse_z + CENTER_X
    screen_y = FOCAL_LENGTH * mean_y * inverse_z + CENTER_Y
    distance = jnp.sqrt(mean_x * mean_x + mean_y * mean_y + mean_z * mean_z)
    basis = harmonics(mean_x / distance, mean_y / distance, mean_z / distance)
    coeffs = gauss_rows[11:59].reshape(16, 3, -1)
    colours = jnp.maximum(lax.optimization_barrier(jnp.sum(basis[:, None, :] * coeffs, axis=0)) + 0.5, 0.0)
    shape_rows = jnp.stack([screen_x, screen_y, cov_yy / determinant, -cov_xy / determinant, cov_xx / determinant, jax.nn.sigmoid(gauss_rows[10])])
    return jnp.concatenate([shape_rows, colours], axis=0)

def shade(attributes, present, pixel_x, pixel_y):
    delta_x = pixel_x[None, :] - attributes[0][:, None]
    delta_y = pixel_y[None, :] - attributes[1][:, None]
    exponent = -0.5 * (attributes[2][:, None] * delta_x * delta_x + attributes[4][:, None] * delta_y * delta_y) - attributes[3][:, None] * delta_x * delta_y
    coverage = (attributes[5] * present)[:, None] * jnp.exp(exponent)
    remain = jnp.cumprod(1.0 - coverage, axis=0)
    transmit = jnp.concatenate([jnp.ones_like(remain[:1]), remain[:-1]], axis=0)
    weights = coverage * transmit
    return jnp.einsum('ck,kp->cp', attributes[6:9], weights, precision=lax.Precision.HIGHEST)

def render_tiles(screen, tile_slots, tile_count, tile_place, target):
    list_length = tile_slots.shape[1]
    pixels = jnp.arange(256, dtype=jnp.int32)

    def one_tile(inputs):
        slot_rows, listed, image_tile, target_tile = inputs
        attributes = jnp.take(screen, slot_rows, axis=1)
        present = (jnp.arange(list_length, dtype=jnp.int32) < listed).astype(screen.dtype)
        pixel_x = (16 * (image_tile % 120) + pixels % 16).astype(jnp.float32) + 0.5
        pixel_y = (16 * (image_tile // 120) + pixels // 16).astype(jnp.float32) + 0.5
        colours, pullback = jax.vjp(lambda attrib: shade(attrib, present, pixel_x, pixel_y), attributes)
        attr_grad, = pullback((colours - target_tile) / 256.0)
        return (colours, attr_grad)
    colours, slot_grads = lax.map(one_tile, (tile_slots, tile_count, tile_place, target))
    rows_total = screen.shape[0]
    screen_grad = jnp.zeros_like(screen).at[:, tile_slots.reshape(-1)].add(slot_grads.transpose(1, 0, 2).reshape(rows_total, -1))
    return (colours, screen_grad)

def reference(params, requests, tile_slots, tile_count, tile_place, target):
    owners = jnp.arange(N_DEV, dtype=jnp.int32)

    def one_device(inputs):
        wanted, slots, listed, places, goals = inputs
        global_rows = (owners[:, None] * G_DEV + wanted).reshape(-1)
        received = jnp.take(params, global_rows, axis=1)
        screen, pullback = jax.vjp(project, received)
        colours, screen_grad = render_tiles(screen, slots, listed, places, goals)
        row_grads, = pullback(screen_grad)
        return (colours, row_grads)
    colours, row_grads = lax.map(one_device, (requests, tile_slots.reshape(N_DEV, TILE_DEV, K_MAX), tile_count.reshape(N_DEV, TILE_DEV), tile_place.reshape(N_DEV, TILE_DEV), target.reshape(N_DEV, TILE_DEV, 3, 256)))
    all_rows = (owners[None, :, None] * G_DEV + requests).reshape(-1)
    gradient = jnp.zeros((PARAMS, GAUSS), jnp.float32).at[:, all_rows].add(row_grads.transpose(1, 0, 2).reshape(PARAMS, -1))
    return (colours.reshape(TILES, 3, 256), gradient)
```

```python
import functools

import jax
import jax.numpy as jnp
from jax import lax
from jax.experimental import pallas as pl
from jax.experimental.pallas import tpu as pltpu
from jax.sharding import PartitionSpec as P

FOCAL = 1200.0
CENTER_X = 960.0
CENTER_Y = 540.0
DILATION = 0.3
BAND_ZERO = 0.28209479177387814
BAND_ONE = 0.4886025119029199
BAND_TWO = (
    1.0925484305920792,
    -1.0925484305920792,
    0.31539156525252005,
    -1.0925484305920792,
    0.5462742152960396,
)
BAND_THREE = (
    -0.5900435899266435,
    2.890611442640554,
    -0.4570457994644658,
    0.3731763325901154,
    -0.4570457994644658,
    1.445305721320277,
    -0.5900435899266435,
)
LOG2_E = 1.4426950408889634

DEVICES = 128
OWNED = 5120
CAP = 40
PARAMS = 59
BLOCKS = OWNED // 128
TILES = 16
SLOTS = 512
SEG = 46
SEG_PAD = 48
SEGS = 12
GROUP = 8
PASSES = 32 // GROUP
F32 = jnp.float32
I32 = jnp.int32
VMEM_LIMIT = 48 * 1024 * 1024


def project(rows):
    x, y, z = rows[0], rows[1], rows[2]
    scales = [jnp.exp(rows[3 + k]) for k in range(3)]
    norm = jnp.sqrt(rows[6] * rows[6] + rows[7] * rows[7] + rows[8] * rows[8] + rows[9] * rows[9])
    qw, qx, qy, qz = (rows[6 + k] / norm for k in range(4))
    rotation = [
        [1.0 - 2.0 * (qy * qy + qz * qz), 2.0 * (qx * qy - qw * qz), 2.0 * (qx * qz + qw * qy)],
        [2.0 * (qx * qy + qw * qz), 1.0 - 2.0 * (qx * qx + qz * qz), 2.0 * (qy * qz - qw * qx)],
        [2.0 * (qx * qz - qw * qy), 2.0 * (qy * qz + qw * qx), 1.0 - 2.0 * (qx * qx + qy * qy)],
    ]
    spread = [[rotation[i][k] * scales[k] for k in range(3)] for i in range(3)]
    inverse_z = 1.0 / z
    diag = FOCAL * inverse_z
    jac_xz = -FOCAL * x * inverse_z * inverse_z
    jac_yz = -FOCAL * y * inverse_z * inverse_z
    across = [diag * spread[0][k] + jac_xz * spread[2][k] for k in range(3)]
    upward = [diag * spread[1][k] + jac_yz * spread[2][k] for k in range(3)]
    cov_xx = across[0] * across[0] + across[1] * across[1] + across[2] * across[2] + DILATION
    cov_xy = across[0] * upward[0] + across[1] * upward[1] + across[2] * upward[2]
    cov_yy = upward[0] * upward[0] + upward[1] * upward[1] + upward[2] * upward[2] + DILATION
    determinant = cov_xx * cov_yy - cov_xy * cov_xy
    distance = jnp.sqrt(x * x + y * y + z * z)
    fx, fy, fz = x / distance, y / distance, z / distance
    xx, yy, zz = fx * fx, fy * fy, fz * fz
    basis = [
        None,
        -BAND_ONE * fy,
        BAND_ONE * fz,
        -BAND_ONE * fx,
        BAND_TWO[0] * fx * fy,
        BAND_TWO[1] * fy * fz,
        BAND_TWO[2] * (2.0 * zz - xx - yy),
        BAND_TWO[3] * fx * fz,
        BAND_TWO[4] * (xx - yy),
        BAND_THREE[0] * fy * (3.0 * xx - yy),
        BAND_THREE[1] * fx * fy * fz,
        BAND_THREE[2] * fy * (4.0 * zz - xx - yy),
        BAND_THREE[3] * fz * (2.0 * zz - 3.0 * xx - 3.0 * yy),
        BAND_THREE[4] * fx * (4.0 * zz - xx - yy),
        BAND_THREE[5] * fz * (xx - yy),
        BAND_THREE[6] * fx * (xx - 3.0 * yy),
    ]
    colours = []
    for channel in range(3):
        total = BAND_ZERO * rows[11 + channel]
        for k in range(1, 16):
            total = total + basis[k] * rows[11 + 3 * k + channel]
        colours.append(jnp.maximum(total + 0.5, 0.0))
    return [
        FOCAL * x * inverse_z + CENTER_X,
        FOCAL * y * inverse_z + CENTER_Y,
        cov_yy / determinant,
        -cov_xy / determinant,
        cov_xx / determinant,
        1.0 / (1.0 + jnp.exp(-rows[10])),
        *colours,
    ]


def load_rows(params_ref, group):
    columns = pl.ds(pl.multiple_of(group * 1024, 1024), 1024)
    return [params_ref[row : row + 1, columns].reshape(8, 128) for row in range(PARAMS)]


def project_kernel(params_ref, screen_ref, ninth_ref):
    def one_group(group, carry):
        screen = project(load_rows(params_ref, group))
        for row in range(8):
            screen_ref[pl.ds(pl.multiple_of(group * 8, 8), 8), row, :] = screen[row]
        ninth_ref[group] = screen[8]
        return carry

    lax.fori_loop(0, OWNED // 1024, one_group, 0)


def gather(source_ref, ninth_ref, block_ref, lane_ref, out_ref, out_ninth_ref, targets, sources):
    sublane = lax.broadcasted_iota(I32, (8, 128), 0)

    def one_row(row, carry):
        lane = jnp.broadcast_to(lane_ref[pl.ds(row, 1), :], (8, 128))
        block = jnp.broadcast_to(block_ref[pl.ds(row, 1), :], (8, 128))
        total = jnp.zeros((8, 128), F32)
        for source in range(sources):
            picked = jnp.take_along_axis(source_ref[source], lane, axis=1)
            total = jnp.where(block == source, picked, total)
        out_ref[row] = total
        place = block - sublane
        total = jnp.zeros((8, 128), F32)
        for source in range((sources + 7) // 8):
            picked = jnp.take_along_axis(ninth_ref[source], lane, axis=1)
            total = jnp.where(place == 8 * source, picked, total)
        out_ninth_ref[pl.ds(row, 1), :] = jnp.sum(total, axis=0, keepdims=True)
        return carry

    lax.fori_loop(0, targets, one_row, 0)


def invert(block_ref, lane_ref, left_ref, right_ref, row_ref, col_ref, rows, blocks):
    iota_lane = lax.broadcasted_iota(I32, (1, 128), 1).astype(F32)
    iota_block = lax.broadcasted_iota(I32, (blocks, 128), 0)
    iota_sub = lax.broadcasted_iota(I32, (128, 128), 0)

    def one_row(row, carry):
        columns = pl.ds(pl.multiple_of(row * 128, 128), 128)
        here = iota_block == block_ref[pl.ds(row, 1), :]
        value = jnp.full((1, 128), 0.0, F32) + row.astype(F32)
        left_ref[0:blocks, columns] = jnp.where(here, value, 0.0).astype(jnp.bfloat16)
        left_ref[blocks : 2 * blocks, columns] = jnp.where(here, iota_lane, 0.0).astype(
            jnp.bfloat16
        )
        right_ref[:, columns] = jnp.where(
            iota_sub == lane_ref[pl.ds(row, 1), :], 1.0, 0.0
        ).astype(jnp.bfloat16)
        return carry

    lax.fori_loop(0, rows, one_row, 0)
    found = lax.dot_general(
        left_ref[...], right_ref[...], (((1,), (1,)), ((), ())), preferred_element_type=F32
    )
    row_ref[...] = (found[0:blocks] + 0.5).astype(I32)
    col_ref[...] = (found[blocks : 2 * blocks] + 0.5).astype(I32)


def pack_messages(rows_ref, ninth_ref, out_ref):
    flat = rows_ref[...].reshape(CAP * 8, 128)
    out_ref[:, 0, :] = flat[0:128].T
    out_ref[:, 1, :] = flat[128:256].T
    last = jnp.concatenate(
        [flat[256:320], ninth_ref[...], jnp.zeros((128 - 64 - CAP, 128), F32)], axis=0
    )
    out_ref[:, 2, :] = last.T
    out_ref[:, 3, :] = jnp.zeros((128, 128), F32)


def unpack_messages(message_ref, rows_ref, ninth_ref):
    rows_ref[0:16] = message_ref[:, 0, :].T.reshape(16, 8, 128)
    rows_ref[16:32] = message_ref[:, 1, :].T.reshape(16, 8, 128)
    last = message_ref[:, 2, :].T
    rows_ref[32:40] = last[0:64].reshape(8, 8, 128)
    ninth_ref[...] = last[64 : 64 + CAP].reshape(CAP // 8, 8, 128)


def wanted_tables(wanted_ref, block_ref, lane_ref):
    wide = jnp.concatenate(
        [wanted_ref[...].astype(F32), jnp.zeros((DEVICES, 128 - CAP), F32)], axis=1
    )
    wanted = wide.T[0:CAP].astype(I32)
    block_ref[...] = wanted >> 7
    lane_ref[...] = wanted & 127


def send_kernel(
    wanted_ref, screen_ref, ninth_ref, message_ref, row_ref, col_ref,
    block_ref, lane_ref, out_ref, out_ninth_ref, left_ref, right_ref,
):
    wanted_tables(wanted_ref, block_ref, lane_ref)
    gather(screen_ref, ninth_ref, block_ref, lane_ref, out_ref, out_ninth_ref, CAP, BLOCKS)
    pack_messages(out_ref, out_ninth_ref, message_ref)
    invert(block_ref, lane_ref, left_ref, right_ref, row_ref, col_ref, CAP, BLOCKS)


def lane_map(count_ref, place_ref):
    lane = lax.broadcasted_iota(I32, (1, 128), 1)
    tile = jnp.full((1, 128), -1, I32)
    segment = jnp.zeros((1, 128), I32)
    segments = jnp.zeros((1, 128), I32)
    count = jnp.zeros((1, 128), I32)
    origin_x = jnp.zeros((1, 128), I32)
    origin_y = jnp.zeros((1, 128), I32)
    base = jnp.int32(0)
    for index in range(TILES):
        listed = count_ref[0, index]
        place = place_ref[0, index]
        used = lax.div(listed + (SEG - 1), SEG)
        inside = (lane >= base) & (lane < base + used)
        place_y = lax.div(place, 120)
        tile = jnp.where(inside, index, tile)
        segment = jnp.where(inside, lane - base, segment)
        segments = jnp.where(inside, used, segments)
        count = jnp.where(inside, listed, count)
        origin_x = jnp.where(inside, 16 * (place - 120 * place_y), origin_x)
        origin_y = jnp.where(inside, 16 * place_y, origin_y)
        base = base + used
    return tile, segment, segments, count, origin_x, origin_y


def index_kernel(
    count_ref, place_ref, slots_ref,
    block_ref, lane_ref, row_ref, col_ref, lanes_ref, all_ref, left_ref, right_ref,
):
    tile, segment, segments, count, origin_x, origin_y = lane_map(count_ref, place_ref)
    lanes_ref[0:1] = tile
    lanes_ref[1:2] = segment
    lanes_ref[2:3] = segments
    lanes_ref[3:4] = count
    lanes_ref[4:5] = origin_x
    lanes_ref[5:6] = origin_y
    lanes_ref[6:8] = jnp.zeros((2, 128), I32)
    slots = slots_ref[...]
    owner = ((slots.astype(F32) + 0.5) * (1.0 / CAP)).astype(I32)
    within = slots - owner * CAP
    pick = jnp.where(
        lax.broadcasted_iota(I32, (TILES, 128), 0) == tile, 1.0, 0.0
    ).astype(jnp.bfloat16)
    contract = (((0,), (0,)), ((), ()))
    step = lax.broadcasted_iota(I32, (SEG_PAD, 128), 0)
    live = (step < SEG) & (step + segment * SEG < count)
    for values, out in ((within, block_ref), (owner, lane_ref)):
        all_ref[0:SLOTS] = lax.dot_general(
            values.astype(F32).astype(jnp.bfloat16), pick, contract, preferred_element_type=F32
        )
        all_ref[SLOTS:] = jnp.zeros_like(all_ref[SLOTS:])
        total = jnp.zeros((SEG_PAD, 128), F32)
        for part in range(SEGS):
            rows = all_ref[part * SEG : part * SEG + SEG_PAD]
            total = jnp.where(segment == part, rows, total)
        out[...] = jnp.where(live, (total + 0.5).astype(I32), -1)
    invert(block_ref, lane_ref, left_ref, right_ref, row_ref, col_ref, SEG, CAP)


def render_kernel(
    message_ref, block_ref, lane_ref, row_ref, col_ref, lanes_ref, target_ref,
    rendered_ref, gradient_ref,
    source_ref, source_ninth_ref, rows_ref, ninth_ref, pre_ref, alpha_ref, weight_ref,
    trans_ref, colour_ref, behind_ref, moment_ref, grad_ref, grad_ninth_ref,
    back_ref, back_ninth_ref,
):
    unpack_messages(message_ref, source_ref, source_ninth_ref)
    safe_lane_ref = lane_ref
    gather(
        source_ref, source_ninth_ref, block_ref, safe_lane_ref, rows_ref, ninth_ref, SEG, CAP
    )
    tile = lanes_ref[0:1]
    segment = lanes_ref[1:2]
    segments = lanes_ref[2:3]
    origin_x = lanes_ref[4:5].astype(F32)
    origin_y = lanes_ref[5:6].astype(F32)
    sub = lax.broadcasted_iota(I32, (8, 128), 0).astype(F32) + 0.5

    def wide(row):
        return jnp.broadcast_to(row, (8, 128))

    def prepare(step, carry):
        attrs = rows_ref[step]
        screen_x = attrs[0:1] - origin_x
        screen_y = attrs[1:2] - origin_y
        curve_x = wide(-0.5 * LOG2_E * attrs[2:3])
        curve_xy = wide(-LOG2_E * attrs[3:4])
        for half in range(2):
            delta = (sub + 8.0 * half) - wide(screen_x)
            pre_ref[step, half] = curve_x * delta * delta
            pre_ref[step, 2 + half] = curve_xy * delta
            pre_ref[step, 9 + half] = delta
        pre_ref[step, 4] = wide(screen_y)
        pre_ref[step, 5] = wide(-0.5 * LOG2_E * attrs[4:5])
        pre_ref[step, 6] = wide(attrs[5:6])
        pre_ref[step, 7] = wide(attrs[6:7])
        pre_ref[step, 8] = wide(attrs[7:8])
        pre_ref[step, 11] = wide(ninth_ref[pl.ds(step, 1), :])
        return carry

    lax.fori_loop(0, SEG, prepare, 0)

    def forward_pass(index, carry):
        first_v = (index * (GROUP // 2)).astype(F32) + 0.5

        def one_step(step, state):
            trans, red, green, blue = (list(part) for part in state)
            opacity, screen_y, curve_y = pre_ref[step, 6], pre_ref[step, 4], pre_ref[step, 5]
            colours = (pre_ref[step, 7], pre_ref[step, 8], pre_ref[step, 11])
            for pair in range(GROUP // 2):
                delta_y = (first_v + float(pair)) - screen_y
                bend = curve_y * delta_y * delta_y
                for half in range(2):
                    k = 2 * pair + half
                    power = pre_ref[step, half] + (bend + pre_ref[step, 2 + half] * delta_y)
                    alpha = opacity * jnp.exp2(power)
                    weight = alpha * trans[k]
                    trans[k] = trans[k] - weight
                    red[k] = red[k] + colours[0] * weight
                    green[k] = green[k] + colours[1] * weight
                    blue[k] = blue[k] + colours[2] * weight
                    alpha_ref[index, step, k] = alpha
                    weight_ref[index, step, k] = weight
            return tuple(trans), tuple(red), tuple(green), tuple(blue)

        ones = tuple(jnp.ones((8, 128), F32) for _ in range(GROUP))
        zeros = tuple(jnp.zeros((8, 128), F32) for _ in range(GROUP))
        state = lax.fori_loop(0, SEG, one_step, (ones, zeros, zeros, zeros))
        for k in range(GROUP):
            rows = pl.ds(pl.multiple_of((index * GROUP + k) * 8, 8), 8)
            trans_ref[rows, :] = state[0][k]
            for channel in range(3):
                colour_ref[channel, rows, :] = state[1 + channel][k]
        return carry

    lax.fori_loop(0, PASSES, forward_pass, 0)

    through = trans_ref[...]
    start = jnp.where(segment == 0, 1.0, pltpu.roll(through, 1, 1))
    for shift in (1, 2, 4, 8):
        start = start * jnp.where(segment >= shift, pltpu.roll(start, shift, 1), 1.0)
    pick = jnp.where(lax.broadcasted_iota(I32, (TILES, 128), 0) == tile, 1.0, 0.0)
    behind = jnp.zeros((256, 128), F32)
    for channel in range(3):
        image = lax.dot_general(
            pick, colour_ref[channel] * start, (((1,), (1,)), ((), ())),
            preferred_element_type=F32, precision=lax.Precision.HIGHEST,
        )
        rendered_ref[:, channel, :] = image
        error = (image - target_ref[:, channel, :]) * (1.0 / 256.0)
        spread = lax.dot_general(
            error, pick, (((0,), (0,)), ((), ())),
            preferred_element_type=F32, precision=lax.Precision.HIGHEST,
        )
        behind = behind + spread * colour_ref[channel]
        colour_ref[channel] = spread * start
    left = segments - 1 - segment
    factor = jnp.where(left >= 1, pltpu.roll(through, 127, 1), 0.0)
    behind = jnp.where(left >= 1, pltpu.roll(behind, 127, 1), 0.0)
    for shift in (1, 2, 4, 8):
        reach = left >= shift
        behind = behind + factor * jnp.where(reach, pltpu.roll(behind, 128 - shift, 1), 0.0)
        factor = factor * jnp.where(reach, pltpu.roll(factor, 128 - shift, 1), 0.0)
    behind_ref[...] = behind * start

    def clear(step, carry):
        for row in range(9):
            moment_ref[step, row] = jnp.zeros((8, 128), F32)
        return carry

    lax.fori_loop(0, SEG, clear, 0)

    def backward_pass(index, carry):
        first_v = (index * (GROUP // 2)).astype(F32) + 0.5
        rows = [pl.ds(pl.multiple_of((index * GROUP + k) * 8, 8), 8) for k in range(GROUP)]
        errors = [[colour_ref[channel, rows[k], :] for channel in range(3)] for k in range(GROUP)]

        def one_step(count, state):
            step = SEG - 1 - count
            state = list(state)
            screen_y = pre_ref[step, 4]
            colours = (pre_ref[step, 7], pre_ref[step, 8], pre_ref[step, 11])
            sums = [moment_ref[step, row] for row in range(9)]
            for pair in range(GROUP // 2):
                delta_y = (first_v + float(pair)) - screen_y
                for half in range(2):
                    k = 2 * pair + half
                    alpha = alpha_ref[index, step, k]
                    weight = weight_ref[index, step, k]
                    shade = (
                        colours[0] * errors[k][0]
                        + colours[1] * errors[k][1]
                        + colours[2] * errors[k][2]
                    )
                    gap = shade - state[k]
                    state[k] = state[k] + alpha * gap
                    slope = weight * gap
                    slope_y = slope * delta_y
                    sums[3 * half] = sums[3 * half] + slope
                    sums[3 * half + 1] = sums[3 * half + 1] + slope_y
                    sums[3 * half + 2] = sums[3 * half + 2] + slope_y * delta_y
                    for channel in range(3):
                        sums[6 + channel] = sums[6 + channel] + weight * errors[k][channel]
            for row in range(9):
                moment_ref[step, row] = sums[row]
            return tuple(state)

        lax.fori_loop(0, SEG, one_step, tuple(behind_ref[rows[k], :] for k in range(GROUP)))
        return carry

    lax.fori_loop(0, PASSES, backward_pass, 0)

    def finish(step, carry):
        delta = [pre_ref[step, 9], pre_ref[step, 10]]
        sums = [moment_ref[step, row] for row in range(9)]
        flat = [sums[0], sums[3]]
        tilt = [sums[1], sums[4]]
        bend = [sums[2], sums[5]]
        side = [flat[half] * delta[half] for half in range(2)]

        def total(register):
            return jnp.sum(register, axis=0, keepdims=True)

        m00 = total(flat[0] + flat[1])
        m10 = total(side[0] + side[1])
        m01 = total(tilt[0] + tilt[1])
        m20 = total(side[0] * delta[0] + side[1] * delta[1])
        m11 = total(tilt[0] * delta[0] + tilt[1] * delta[1])
        m02 = total(bend[0] + bend[1])
        attrs = rows_ref[step]
        conic_a, conic_b, conic_c = attrs[2:3], attrs[3:4], attrs[4:5]
        grad_ref[step] = jnp.concatenate(
            [
                conic_a * m10 + conic_b * m01,
                conic_b * m10 + conic_c * m01,
                -0.5 * m20,
                -m11,
                -0.5 * m02,
                m00,
                total(sums[6]),
                total(sums[7]),
            ],
            axis=0,
        )
        ninth_ref[pl.ds(step, 1), :] = total(sums[8])
        return carry

    lax.fori_loop(0, SEG, finish, 0)
    ninth_ref[SEG:SEG_PAD] = jnp.zeros((SEG_PAD - SEG, 128), F32)
    grad_ninth_ref[...] = ninth_ref[...].reshape(SEG_PAD // 8, 8, 128)
    gather(grad_ref, grad_ninth_ref, row_ref, col_ref, back_ref, back_ninth_ref, CAP, SEG)
    pack_messages(back_ref, back_ninth_ref, gradient_ref)


def pullback_kernel(
    message_ref, row_ref, col_ref, params_ref, gradient_ref,
    source_ref, source_ninth_ref, rows_ref, ninth_ref,
):
    unpack_messages(message_ref, source_ref, source_ninth_ref)
    gather(source_ref, source_ninth_ref, row_ref, col_ref, rows_ref, ninth_ref, BLOCKS, CAP)

    def one_group(group, carry):
        columns = pl.ds(pl.multiple_of(group * 1024, 1024), 1024)
        eight = pl.ds(pl.multiple_of(group * 8, 8), 8)
        rows = load_rows(params_ref, group)
        screen_grad = [rows_ref[eight, row, :] for row in range(8)] + [ninth_ref[eight, :]]
        screen, pullback = jax.vjp(project, rows)
        by_logit = screen_grad[5] * (1.0 / (1.0 + jnp.exp(rows[10])))
        screen_grad[5] = jnp.zeros_like(by_logit)
        (grads,) = pullback(screen_grad)
        grads[10] = by_logit
        for row in range(PARAMS):
            gradient_ref[row : row + 1, columns] = grads[row].reshape(1, 1024)
        return carry

    lax.fori_loop(0, OWNED // 1024, one_group, 0)


def shape(dims, dtype=F32):
    return jax.ShapeDtypeStruct(dims, dtype)


def call(kernel, outs, scratch, name, smem=0, operands=0):
    params = pltpu.CompilerParams(vmem_limit_bytes=VMEM_LIMIT)
    specs = [pl.BlockSpec(memory_space=pltpu.SMEM)] * smem
    specs += [pl.BlockSpec(memory_space=pltpu.VMEM)] * (operands - smem)
    return pl.pallas_call(
        kernel,
        out_shape=outs,
        in_specs=specs,
        out_specs=[pl.BlockSpec(memory_space=pltpu.VMEM)] * len(outs),
        scratch_shapes=scratch,
        compiler_params=params,
        name=name,
    )


MESSAGE = (DEVICES, 4, 128)
TABLE = (CAP, 128)
EIGHT = (CAP, 8, 128)
NINE = (CAP // 8, 8, 128)


def exchange(messages):
    return lax.all_to_all(messages, "dev", split_axis=0, concat_axis=0, tiled=True)


def exchange_requests(requests):
    return lax.all_to_all(requests, "dev", split_axis=1, concat_axis=0, tiled=True)


def local(params, requests, tile_slots, tile_count, tile_place, target):
    vmem = pltpu.VMEM
    wanted = exchange_requests(requests).reshape(DEVICES, CAP)
    screen, ninth = call(
        project_kernel, [shape(EIGHT), shape(NINE)], [], "project", operands=1
    )(params)
    messages, owner_row, owner_col = call(
        send_kernel,
        [shape(MESSAGE), shape(TABLE, I32), shape(TABLE, I32)],
        [
            vmem(TABLE, I32), vmem(TABLE, I32), vmem(EIGHT, F32), vmem(TABLE, F32),
            vmem((2 * BLOCKS, CAP * 128), jnp.bfloat16), vmem((128, CAP * 128), jnp.bfloat16),
        ],
        "send",
        operands=3,
    )(wanted, screen, ninth)
    received = exchange(messages)
    steps = (SEG_PAD, 128)
    block, lane, slot_row, slot_col, lanes = call(
        index_kernel,
        [
            shape(steps, I32), shape(steps, I32), shape(TABLE, I32), shape(TABLE, I32),
            shape((8, 128), I32),
        ],
        [
            vmem((SEGS * SEG + 8, 128), F32),
            vmem((2 * CAP, SEG * 128), jnp.bfloat16), vmem((128, SEG * 128), jnp.bfloat16),
        ],
        "index",
        smem=2,
        operands=3,
    )(tile_count.reshape(1, TILES), tile_place.reshape(1, TILES), tile_slots)
    rendered, gradients = call(
        render_kernel,
        [shape((TILES, 3, 256)), shape(MESSAGE)],
        [
            vmem(EIGHT, F32), vmem(NINE, F32),
            vmem((SEG, 8, 128), F32), vmem(steps, F32),
            vmem((SEG, 12, 8, 128), F32),
            vmem((PASSES, SEG, GROUP, 8, 128), F32), vmem((PASSES, SEG, GROUP, 8, 128), F32),
            vmem((256, 128), F32), vmem((3, 256, 128), F32), vmem((256, 128), F32),
            vmem((SEG, 9, 8, 128), F32),
            vmem((SEG, 8, 128), F32), vmem((SEG_PAD // 8, 8, 128), F32),
            vmem(EIGHT, F32), vmem(TABLE, F32),
        ],
        "render",
        operands=7,
    )(received, block, lane, slot_row, slot_col, lanes, target)
    returned = exchange(gradients)
    (gradient,) = call(
        pullback_kernel,
        [shape((PARAMS, OWNED))],
        [vmem(EIGHT, F32), vmem(NINE, F32), vmem(EIGHT, F32), vmem(TABLE, F32)],
        "pullback",
        operands=4,
    )(returned, owner_row, owner_col, params)
    return rendered, gradient


def solution(mesh):
    in_specs = (
        P(None, "dev"),
        P("dev", None, None),
        P("dev", None),
        P("dev"),
        P("dev"),
        P("dev", None, None),
    )
    out_specs = (P("dev", None, None), P(None, "dev"))
    return jax.shard_map(local, mesh=mesh, in_specs=in_specs, out_specs=out_specs, check_vma=False)
```

```python
import functools

import jax
import jax.numpy as jnp
from jax import lax
from jax.experimental import pallas as pl
from jax.experimental.pallas import tpu as pltpu
from jax.sharding import PartitionSpec as P

FOCAL = 1200.0
CENTER_X = 960.0
CENTER_Y = 540.0
DILATION = 0.3
BAND_ZERO = 0.28209479177387814
BAND_ONE = 0.4886025119029199
BAND_TWO = (
    1.0925484305920792,
    -1.0925484305920792,
    0.31539156525252005,
    -1.0925484305920792,
    0.5462742152960396,
)
BAND_THREE = (
    -0.5900435899266435,
    2.890611442640554,
    -0.4570457994644658,
    0.3731763325901154,
    -0.4570457994644658,
    1.445305721320277,
    -0.5900435899266435,
)
LOG2_E = 1.4426950408889634

DEVICES = 128
OWNED = 5120
CAP = 40
PARAMS = 59
BLOCKS = OWNED // 128
TILES = 16
SLOTS = 512
SEG = 46
SEG_PAD = 48
SEGS = 12
GROUP = 8
PASSES = 32 // GROUP
STEP_UNROLL = 2
BACK_UNROLL = 2
SHORT_UNROLL = 23
BF16 = jnp.bfloat16
F32 = jnp.float32
I32 = jnp.int32
VMEM_LIMIT = 48 * 1024 * 1024


def project(rows):
    x, y, z = rows[0], rows[1], rows[2]
    scales = [jnp.exp(rows[3 + k]) for k in range(3)]
    norm = jnp.sqrt(rows[6] * rows[6] + rows[7] * rows[7] + rows[8] * rows[8] + rows[9] * rows[9])
    qw, qx, qy, qz = (rows[6 + k] / norm for k in range(4))
    rotation = [
        [1.0 - 2.0 * (qy * qy + qz * qz), 2.0 * (qx * qy - qw * qz), 2.0 * (qx * qz + qw * qy)],
        [2.0 * (qx * qy + qw * qz), 1.0 - 2.0 * (qx * qx + qz * qz), 2.0 * (qy * qz - qw * qx)],
        [2.0 * (qx * qz - qw * qy), 2.0 * (qy * qz + qw * qx), 1.0 - 2.0 * (qx * qx + qy * qy)],
    ]
    spread = [[rotation[i][k] * scales[k] for k in range(3)] for i in range(3)]
    inverse_z = 1.0 / z
    diag = FOCAL * inverse_z
    jac_xz = -FOCAL * x * inverse_z * inverse_z
    jac_yz = -FOCAL * y * inverse_z * inverse_z
    across = [diag * spread[0][k] + jac_xz * spread[2][k] for k in range(3)]
    upward = [diag * spread[1][k] + jac_yz * spread[2][k] for k in range(3)]
    cov_xx = across[0] * across[0] + across[1] * across[1] + across[2] * across[2] + DILATION
    cov_xy = across[0] * upward[0] + across[1] * upward[1] + across[2] * upward[2]
    cov_yy = upward[0] * upward[0] + upward[1] * upward[1] + upward[2] * upward[2] + DILATION
    determinant = cov_xx * cov_yy - cov_xy * cov_xy
    distance = jnp.sqrt(x * x + y * y + z * z)
    fx, fy, fz = x / distance, y / distance, z / distance
    xx, yy, zz = fx * fx, fy * fy, fz * fz
    basis = [
        None,
        -BAND_ONE * fy,
        BAND_ONE * fz,
        -BAND_ONE * fx,
        BAND_TWO[0] * fx * fy,
        BAND_TWO[1] * fy * fz,
        BAND_TWO[2] * (2.0 * zz - xx - yy),
        BAND_TWO[3] * fx * fz,
        BAND_TWO[4] * (xx - yy),
        BAND_THREE[0] * fy * (3.0 * xx - yy),
        BAND_THREE[1] * fx * fy * fz,
        BAND_THREE[2] * fy * (4.0 * zz - xx - yy),
        BAND_THREE[3] * fz * (2.0 * zz - 3.0 * xx - 3.0 * yy),
        BAND_THREE[4] * fx * (4.0 * zz - xx - yy),
        BAND_THREE[5] * fz * (xx - yy),
        BAND_THREE[6] * fx * (xx - 3.0 * yy),
    ]
    colours = []
    for channel in range(3):
        total = BAND_ZERO * rows[11 + channel]
        for k in range(1, 16):
            total = total + basis[k] * rows[11 + 3 * k + channel]
        colours.append(jnp.maximum(total + 0.5, 0.0))
    return [
        FOCAL * x * inverse_z + CENTER_X,
        FOCAL * y * inverse_z + CENTER_Y,
        cov_yy / determinant,
        -cov_xy / determinant,
        cov_xx / determinant,
        1.0 / (1.0 + jnp.exp(-rows[10])),
        *colours,
    ]


def load_rows(params_ref, group):
    columns = pl.ds(pl.multiple_of(group * 1024, 1024), 1024)
    return [params_ref[row : row + 1, columns].reshape(8, 128) for row in range(PARAMS)]


def project_kernel(params_ref, screen_ref, ninth_ref):
    def one_group(group, carry):
        screen = project(load_rows(params_ref, group))
        for row in range(8):
            screen_ref[pl.ds(pl.multiple_of(group * 8, 8), 8), row, :] = screen[row]
        ninth_ref[group] = screen[8]
        return carry

    lax.fori_loop(0, OWNED // 1024, one_group, 0)


def repeat(count, unroll, body, state):
    def turn(index, state):
        for part in range(unroll):
            state = body(index * unroll + part, state)
        return state

    return lax.fori_loop(0, count // unroll, turn, state)


def gather(
    source_ref, ninth_ref, block_ref, lane_ref, out_ref, out_ninth_ref, split_ref,
    targets, sources, by_matmul, by_lanes,
):
    half = sources // 2
    eights = half * 8
    height = eights + 24
    width = 128 * by_matmul
    ninth = ninth_ref[...].reshape(-1, 128)
    rest = jnp.concatenate(
        [
            jnp.concatenate([ninth[0:half], ninth[half:sources]], axis=1),
            jnp.zeros((24 - half, 256), F32),
        ],
        axis=0,
    )
    main = jnp.concatenate(
        [
            source_ref[0:half].reshape(eights, 128),
            source_ref[half:sources].reshape(eights, 128),
        ],
        axis=1,
    )
    for part in range(3):
        for values, start in ((main, 0), (rest, eights)):
            rounded = values.astype(BF16)
            split_ref[part * height + start : part * height + start + values.shape[0]] = rounded
        main = main - main.astype(BF16).astype(F32)
        rest = rest - rest.astype(BF16).astype(F32)
    iota = lax.broadcasted_iota(I32, (256, width), 0).astype(F32).astype(BF16)
    sublane_rest = lax.broadcasted_iota(I32, (24, width), 0)
    sublane = lax.broadcasted_iota(I32, (8, 128), 0)

    def turn(index, carry):
        base = index * (by_matmul + by_lanes)
        rows = [pl.ds(base + k, 1) for k in range(by_matmul)]
        block = jnp.concatenate([block_ref[row, :] for row in rows], axis=1)
        lane = jnp.concatenate([lane_ref[row, :] for row in rows], axis=1)
        upper = jnp.where(block >= half, 1, 0)
        key = jnp.broadcast_to((lane + 128 * upper).astype(F32), (16, width)).astype(BF16)
        place = block - half * upper
        match = jnp.concatenate([key] * 16, axis=0) == iota
        pick = jnp.where(match, jnp.ones((), BF16), jnp.zeros((), BF16))
        parts = lax.dot_general(
            split_ref[...], pick, (((1,), (0,)), ((), ())), preferred_element_type=F32
        )
        for k in range(by_lanes):
            row = base + by_matmul + k
            lane = jnp.broadcast_to(lane_ref[pl.ds(row, 1), :], (8, 128))
            block = jnp.broadcast_to(block_ref[pl.ds(row, 1), :], (8, 128))
            total = jnp.zeros((8, 128), F32)
            for source in range(sources):
                picked = jnp.take_along_axis(
                    source_ref[source], lane, axis=1, mode="promise_in_bounds"
                )
                total = jnp.where(block == source, picked, total)
            out_ref[row] = total
            offset = block - sublane
            total = jnp.zeros((8, 128), F32)
            for source in range((sources + 7) // 8):
                picked = jnp.take_along_axis(
                    ninth_ref[source], lane, axis=1, mode="promise_in_bounds"
                )
                total = jnp.where(offset == 8 * source, picked, total)
            out_ninth_ref[pl.ds(row, 1), :] = jnp.sum(total, axis=0, keepdims=True)
        values = (parts[0:height] + parts[height : 2 * height]) + parts[2 * height : 3 * height]
        wide = jnp.broadcast_to(place, (8, width))
        total = jnp.zeros((8, width), F32)
        for source in range(half):
            total = jnp.where(wide == source, values[8 * source : 8 * source + 8], total)
        last = jnp.sum(
            jnp.where(sublane_rest == place, values[eights:height], 0.0), axis=0, keepdims=True
        )
        for k in range(by_matmul):
            out_ref[base + k] = total[:, 128 * k : 128 * k + 128]
            out_ninth_ref[pl.ds(base + k, 1), :] = last[:, 128 * k : 128 * k + 128]
        return carry

    lax.fori_loop(0, targets // (by_matmul + by_lanes), turn, 0)


def invert(block_ref, lane_ref, left_ref, right_ref, row_ref, col_ref, rows, blocks):
    iota_lane = lax.broadcasted_iota(I32, (1, 128), 1).astype(F32)
    iota_block = lax.broadcasted_iota(I32, (blocks, 128), 0)
    iota_sub = lax.broadcasted_iota(I32, (128, 128), 0)

    def one_row(row, carry):
        columns = pl.ds(pl.multiple_of(row * 128, 128), 128)
        here = iota_block == block_ref[pl.ds(row, 1), :]
        value = jnp.full((1, 128), 0.0, F32) + row.astype(F32)
        left_ref[0:blocks, columns] = jnp.where(here, value, 0.0).astype(BF16)
        left_ref[blocks : 2 * blocks, columns] = jnp.where(here, iota_lane, 0.0).astype(
            BF16
        )
        right_ref[:, columns] = jnp.where(
            iota_sub == lane_ref[pl.ds(row, 1), :], 1.0, 0.0
        ).astype(BF16)
        return carry

    repeat(rows, 2, one_row, 0)
    found = lax.dot_general(
        left_ref[...], right_ref[...], (((1,), (1,)), ((), ())), preferred_element_type=F32
    )
    row_ref[...] = (found[0:blocks] + 0.5).astype(I32)
    col_ref[...] = (found[blocks : 2 * blocks] + 0.5).astype(I32)


def pack_messages(rows_ref, ninth_ref, out_ref):
    flat = rows_ref[...].reshape(CAP * 8, 128)
    out_ref[:, 0, :] = flat[0:128].T
    out_ref[:, 1, :] = flat[128:256].T
    last = jnp.concatenate(
        [flat[256:320], ninth_ref[...], jnp.zeros((128 - 64 - CAP, 128), F32)], axis=0
    )
    out_ref[:, 2, :] = last.T
    out_ref[:, 3, :] = jnp.zeros((128, 128), F32)


def unpack_messages(message_ref, rows_ref, ninth_ref):
    rows_ref[0:16] = message_ref[:, 0, :].T.reshape(16, 8, 128)
    rows_ref[16:32] = message_ref[:, 1, :].T.reshape(16, 8, 128)
    last = message_ref[:, 2, :].T
    rows_ref[32:40] = last[0:64].reshape(8, 8, 128)
    ninth_ref[...] = last[64 : 64 + CAP].reshape(CAP // 8, 8, 128)


def wanted_tables(wanted_ref, block_ref, lane_ref):
    wide = jnp.concatenate(
        [wanted_ref[...].astype(F32), jnp.zeros((DEVICES, 128 - CAP), F32)], axis=1
    )
    wanted = wide.T[0:CAP].astype(I32)
    block_ref[...] = wanted >> 7
    lane_ref[...] = wanted & 127


def send_kernel(
    wanted_ref, screen_ref, ninth_ref, message_ref, block_ref, lane_ref,
    out_ref, out_ninth_ref, split_ref,
):
    wanted_tables(wanted_ref, block_ref, lane_ref)
    gather(
        screen_ref, ninth_ref, block_ref, lane_ref, out_ref, out_ninth_ref, split_ref,
        CAP, BLOCKS, 10, 10,
    )
    pack_messages(out_ref, out_ninth_ref, message_ref)


def invert_kernel(block_ref, lane_ref, row_ref, col_ref, left_ref, right_ref):
    invert(block_ref, lane_ref, left_ref, right_ref, row_ref, col_ref, CAP, BLOCKS)


def lane_map(count_ref, place_ref):
    lane = lax.broadcasted_iota(I32, (1, 128), 1)
    tile = jnp.full((1, 128), -1, I32)
    segment = jnp.zeros((1, 128), I32)
    segments = jnp.zeros((1, 128), I32)
    count = jnp.zeros((1, 128), I32)
    origin_x = jnp.zeros((1, 128), I32)
    origin_y = jnp.zeros((1, 128), I32)
    base = jnp.int32(0)
    for index in range(TILES):
        listed = count_ref[0, index]
        place = place_ref[0, index]
        used = lax.div(listed + (SEG - 1), SEG)
        inside = (lane >= base) & (lane < base + used)
        place_y = lax.div(place, 120)
        tile = jnp.where(inside, index, tile)
        segment = jnp.where(inside, lane - base, segment)
        segments = jnp.where(inside, used, segments)
        count = jnp.where(inside, listed, count)
        origin_x = jnp.where(inside, 16 * (place - 120 * place_y), origin_x)
        origin_y = jnp.where(inside, 16 * place_y, origin_y)
        base = base + used
    return tile, segment, segments, count, origin_x, origin_y


def index_kernel(
    count_ref, place_ref, slots_ref,
    block_ref, lane_ref, row_ref, col_ref, lanes_ref, all_ref, left_ref, right_ref,
):
    tile, segment, segments, count, origin_x, origin_y = lane_map(count_ref, place_ref)
    lanes_ref[0:1] = tile
    lanes_ref[1:2] = segment
    lanes_ref[2:3] = segments
    lanes_ref[3:4] = count
    lanes_ref[4:5] = origin_x
    lanes_ref[5:6] = origin_y
    lanes_ref[6:8] = jnp.zeros((2, 128), I32)
    slots = slots_ref[...]
    owner = ((slots.astype(F32) + 0.5) * (1.0 / CAP)).astype(I32)
    within = slots - owner * CAP
    pick = jnp.where(
        lax.broadcasted_iota(I32, (TILES, 128), 0) == tile, 1.0, 0.0
    ).astype(BF16)
    contract = (((0,), (0,)), ((), ()))
    step = lax.broadcasted_iota(I32, (SEG_PAD, 128), 0)
    live = (step < SEG) & (step + segment * SEG < count)
    for values, out, unused in ((within, block_ref, -1), (owner, lane_ref, 0)):
        all_ref[0:SLOTS] = lax.dot_general(
            values.astype(F32).astype(BF16), pick, contract, preferred_element_type=F32
        )
        all_ref[SLOTS:] = jnp.zeros_like(all_ref[SLOTS:])
        total = jnp.zeros((SEG_PAD, 128), F32)
        for part in range(SEGS):
            rows = all_ref[part * SEG : part * SEG + SEG_PAD]
            total = jnp.where(segment == part, rows, total)
        out[...] = jnp.where(live, (total + 0.5).astype(I32), unused)
    invert(block_ref, lane_ref, left_ref, right_ref, row_ref, col_ref, SEG, CAP)


def render_kernel(
    message_ref, block_ref, lane_ref, row_ref, col_ref, lanes_ref, target_ref,
    rendered_ref, gradient_ref,
    source_ref, source_ninth_ref, rows_ref, ninth_ref, pre_ref, alpha_ref, weight_ref,
    trans_ref, colour_ref, behind_ref, moment_ref, grad_ref, grad_ninth_ref,
    back_ref, back_ninth_ref, split_ref, split_back_ref,
):
    unpack_messages(message_ref, source_ref, source_ninth_ref)
    gather(
        source_ref, source_ninth_ref, block_ref, lane_ref, rows_ref, ninth_ref, split_ref,
        SEG, CAP, 12, 11,
    )
    tile = lanes_ref[0:1]
    segment = lanes_ref[1:2]
    segments = lanes_ref[2:3]
    origin_x = lanes_ref[4:5].astype(F32)
    origin_y = lanes_ref[5:6].astype(F32)
    sub = lax.broadcasted_iota(I32, (8, 128), 0).astype(F32) + 0.5

    def wide(row):
        return jnp.broadcast_to(row, (8, 128))

    def prepare(step, carry):
        attrs = rows_ref[step]
        screen_x = attrs[0:1] - origin_x
        screen_y = attrs[1:2] - origin_y
        curve_x = wide(-0.5 * LOG2_E * attrs[2:3])
        curve_xy = wide(-LOG2_E * attrs[3:4])
        for half in range(2):
            delta = (sub + 8.0 * half) - wide(screen_x)
            pre_ref[step, half] = curve_x * delta * delta
            pre_ref[step, 2 + half] = curve_xy * delta
            pre_ref[step, 9 + half] = delta
        pre_ref[step, 4] = wide(screen_y)
        pre_ref[step, 5] = wide(-0.5 * LOG2_E * attrs[4:5])
        pre_ref[step, 6] = wide(attrs[5:6])
        pre_ref[step, 7] = wide(attrs[6:7])
        pre_ref[step, 8] = wide(attrs[7:8])
        pre_ref[step, 11] = wide(ninth_ref[pl.ds(step, 1), :])
        return carry

    repeat(SEG, SHORT_UNROLL, prepare, 0)

    for index in range(PASSES):
        first_v = index * (GROUP // 2) + 0.5

        def one_step(step, state):
            trans, red, green, blue = (list(part) for part in state)
            opacity, screen_y, curve_y = pre_ref[step, 6], pre_ref[step, 4], pre_ref[step, 5]
            colours = (pre_ref[step, 7], pre_ref[step, 8], pre_ref[step, 11])
            for pair in range(GROUP // 2):
                delta_y = (first_v + float(pair)) - screen_y
                bend = curve_y * delta_y * delta_y
                for half in range(2):
                    k = 2 * pair + half
                    power = pre_ref[step, half] + (bend + pre_ref[step, 2 + half] * delta_y)
                    alpha = opacity * jnp.exp2(power)
                    weight = alpha * trans[k]
                    trans[k] = trans[k] - weight
                    red[k] = red[k] + colours[0] * weight
                    green[k] = green[k] + colours[1] * weight
                    blue[k] = blue[k] + colours[2] * weight
                    alpha_ref[index, step, k] = alpha
                    weight_ref[index, step, k] = weight
            return tuple(trans), tuple(red), tuple(green), tuple(blue)

        ones = tuple(jnp.ones((8, 128), F32) for _ in range(GROUP))
        zeros = tuple(jnp.zeros((8, 128), F32) for _ in range(GROUP))
        state = repeat(SEG, STEP_UNROLL, one_step, (ones, zeros, zeros, zeros))
        for k in range(GROUP):
            rows = pl.ds((index * GROUP + k) * 8, 8)
            trans_ref[rows, :] = state[0][k]
            for channel in range(3):
                colour_ref[channel, rows, :] = state[1 + channel][k]

    through = trans_ref[...]
    start = jnp.where(segment == 0, 1.0, pltpu.roll(through, 1, 1))
    for shift in (1, 2, 4, 8):
        start = start * jnp.where(segment >= shift, pltpu.roll(start, shift, 1), 1.0)
    pick = jnp.where(lax.broadcasted_iota(I32, (TILES, 128), 0) == tile, 1.0, 0.0)
    behind = jnp.zeros((256, 128), F32)
    for channel in range(3):
        image = lax.dot_general(
            pick, colour_ref[channel] * start, (((1,), (1,)), ((), ())),
            preferred_element_type=F32, precision=lax.Precision.HIGHEST,
        )
        rendered_ref[:, channel, :] = image
        error = (image - target_ref[:, channel, :]) * (1.0 / 256.0)
        spread = lax.dot_general(
            error, pick, (((0,), (0,)), ((), ())),
            preferred_element_type=F32, precision=lax.Precision.HIGHEST,
        )
        behind = behind + spread * colour_ref[channel]
        colour_ref[channel] = spread * start
    left = segments - 1 - segment
    factor = jnp.where(left >= 1, pltpu.roll(through, 127, 1), 0.0)
    behind = jnp.where(left >= 1, pltpu.roll(behind, 127, 1), 0.0)
    for shift in (1, 2, 4, 8):
        reach = left >= shift
        behind = behind + factor * jnp.where(reach, pltpu.roll(behind, 128 - shift, 1), 0.0)
        factor = factor * jnp.where(reach, pltpu.roll(factor, 128 - shift, 1), 0.0)
    behind_ref[...] = behind * start

    for index in range(PASSES):
        first_v = index * (GROUP // 2) + 0.5
        rows = [pl.ds((index * GROUP + k) * 8, 8) for k in range(GROUP)]
        errors = [[colour_ref[channel, rows[k], :] for channel in range(3)] for k in range(GROUP)]

        def one_step(count, state):
            step = SEG - 1 - count
            state = list(state)
            screen_y = pre_ref[step, 4]
            colours = (pre_ref[step, 7], pre_ref[step, 8], pre_ref[step, 11])
            sums = [moment_ref[step, row] if index else None for row in range(9)]

            def add(row, value):
                sums[row] = value if sums[row] is None else sums[row] + value

            for pair in range(GROUP // 2):
                delta_y = (first_v + float(pair)) - screen_y
                for half in range(2):
                    k = 2 * pair + half
                    alpha = alpha_ref[index, step, k]
                    weight = weight_ref[index, step, k]
                    shade = (
                        colours[0] * errors[k][0]
                        + colours[1] * errors[k][1]
                        + colours[2] * errors[k][2]
                    )
                    gap = shade - state[k]
                    state[k] = state[k] + alpha * gap
                    slope = weight * gap
                    slope_y = slope * delta_y
                    add(3 * half, slope)
                    add(3 * half + 1, slope_y)
                    add(3 * half + 2, slope_y * delta_y)
                    for channel in range(3):
                        add(6 + channel, weight * errors[k][channel])
            for row in range(9):
                moment_ref[step, row] = sums[row]
            return tuple(state)

        repeat(
            SEG, BACK_UNROLL, one_step, tuple(behind_ref[rows[k], :] for k in range(GROUP))
        )

    def finish(step, carry):
        delta = [pre_ref[step, 9], pre_ref[step, 10]]
        sums = [moment_ref[step, row] for row in range(9)]
        flat = [sums[0], sums[3]]
        tilt = [sums[1], sums[4]]
        bend = [sums[2], sums[5]]
        side = [flat[half] * delta[half] for half in range(2)]

        def total(register):
            return jnp.sum(register, axis=0, keepdims=True)

        m00 = total(flat[0] + flat[1])
        m10 = total(side[0] + side[1])
        m01 = total(tilt[0] + tilt[1])
        m20 = total(side[0] * delta[0] + side[1] * delta[1])
        m11 = total(tilt[0] * delta[0] + tilt[1] * delta[1])
        m02 = total(bend[0] + bend[1])
        attrs = rows_ref[step]
        conic_a, conic_b, conic_c = attrs[2:3], attrs[3:4], attrs[4:5]
        grad_ref[step] = jnp.concatenate(
            [
                conic_a * m10 + conic_b * m01,
                conic_b * m10 + conic_c * m01,
                -0.5 * m20,
                -m11,
                -0.5 * m02,
                m00,
                total(sums[6]),
                total(sums[7]),
            ],
            axis=0,
        )
        ninth_ref[pl.ds(step, 1), :] = total(sums[8])
        return carry

    repeat(SEG, SHORT_UNROLL, finish, 0)
    ninth_ref[SEG:SEG_PAD] = jnp.zeros((SEG_PAD - SEG, 128), F32)
    grad_ninth_ref[...] = ninth_ref[...].reshape(SEG_PAD // 8, 8, 128)
    gather(
        grad_ref, grad_ninth_ref, row_ref, col_ref, back_ref, back_ninth_ref, split_back_ref,
        CAP, SEG, 10, 10,
    )
    pack_messages(back_ref, back_ninth_ref, gradient_ref)


def pullback_kernel(
    message_ref, row_ref, col_ref, params_ref, gradient_ref,
    source_ref, source_ninth_ref, rows_ref, ninth_ref, split_ref,
):
    unpack_messages(message_ref, source_ref, source_ninth_ref)
    gather(
        source_ref, source_ninth_ref, row_ref, col_ref, rows_ref, ninth_ref, split_ref,
        BLOCKS, CAP, 10, 10,
    )

    def one_group(group, carry):
        columns = pl.ds(pl.multiple_of(group * 1024, 1024), 1024)
        eight = pl.ds(pl.multiple_of(group * 8, 8), 8)
        rows = load_rows(params_ref, group)
        screen_grad = [rows_ref[eight, row, :] for row in range(8)] + [ninth_ref[eight, :]]
        screen, pullback = jax.vjp(project, rows)
        by_logit = screen_grad[5] * (1.0 / (1.0 + jnp.exp(rows[10])))
        screen_grad[5] = jnp.zeros_like(by_logit)
        (grads,) = pullback(screen_grad)
        grads[10] = by_logit
        for row in range(PARAMS):
            gradient_ref[row : row + 1, columns] = grads[row].reshape(1, 1024)
        return carry

    lax.fori_loop(0, OWNED // 1024, one_group, 0)


def shape(dims, dtype=F32):
    return jax.ShapeDtypeStruct(dims, dtype)


def call(kernel, outs, scratch, name, smem=0, operands=0):
    params = pltpu.CompilerParams(vmem_limit_bytes=VMEM_LIMIT)
    specs = [pl.BlockSpec(memory_space=pltpu.SMEM)] * smem
    specs += [pl.BlockSpec(memory_space=pltpu.VMEM)] * (operands - smem)
    return pl.pallas_call(
        kernel,
        out_shape=outs,
        in_specs=specs,
        out_specs=[pl.BlockSpec(memory_space=pltpu.VMEM)] * len(outs),
        scratch_shapes=scratch,
        compiler_params=params,
        name=name,
    )


SPLIT = (3 * (CAP // 2 * 8 + 24), 256)
SPLIT_BACK = (3 * (SEG // 2 * 8 + 24), 256)
MESSAGE = (DEVICES, 4, 128)
TABLE = (CAP, 128)
EIGHT = (CAP, 8, 128)
NINE = (CAP // 8, 8, 128)


def exchange(messages):
    return lax.all_to_all(messages, "dev", split_axis=0, concat_axis=0, tiled=True)


def exchange_requests(requests):
    return lax.all_to_all(requests, "dev", split_axis=1, concat_axis=0, tiled=True)


def local(params, requests, tile_slots, tile_count, tile_place, target):
    vmem = pltpu.VMEM
    wanted = exchange_requests(requests).reshape(DEVICES, CAP)
    screen, ninth = call(
        project_kernel, [shape(EIGHT), shape(NINE)], [], "project", operands=1
    )(params)
    messages, wanted_block, wanted_lane = call(
        send_kernel,
        [shape(MESSAGE), shape(TABLE, I32), shape(TABLE, I32)],
        [vmem(EIGHT, F32), vmem(TABLE, F32), vmem(SPLIT, BF16)],
        "send",
        operands=3,
    )(wanted, screen, ninth)
    received = exchange(messages)
    owner_row, owner_col = call(
        invert_kernel,
        [shape(TABLE, I32), shape(TABLE, I32)],
        [vmem((2 * BLOCKS, CAP * 128), BF16), vmem((128, CAP * 128), BF16)],
        "invert",
        operands=2,
    )(wanted_block, wanted_lane)
    steps = (SEG_PAD, 128)
    block, lane, slot_row, slot_col, lanes = call(
        index_kernel,
        [
            shape(steps, I32), shape(steps, I32), shape(TABLE, I32), shape(TABLE, I32),
            shape((8, 128), I32),
        ],
        [
            vmem((SEGS * SEG + 8, 128), F32),
            vmem((2 * CAP, SEG * 128), BF16), vmem((128, SEG * 128), BF16),
        ],
        "index",
        smem=2,
        operands=3,
    )(tile_count.reshape(1, TILES), tile_place.reshape(1, TILES), tile_slots)
    rendered, gradients = call(
        render_kernel,
        [shape((TILES, 3, 256)), shape(MESSAGE)],
        [
            vmem(EIGHT, F32), vmem(NINE, F32),
            vmem((SEG, 8, 128), F32), vmem(steps, F32),
            vmem((SEG, 12, 8, 128), F32),
            vmem((PASSES, SEG, GROUP, 8, 128), F32), vmem((PASSES, SEG, GROUP, 8, 128), F32),
            vmem((256, 128), F32), vmem((3, 256, 128), F32), vmem((256, 128), F32),
            vmem((SEG, 9, 8, 128), F32),
            vmem((SEG, 8, 128), F32), vmem((SEG_PAD // 8, 8, 128), F32),
            vmem(EIGHT, F32), vmem(TABLE, F32), vmem(SPLIT, BF16), vmem(SPLIT_BACK, BF16),
        ],
        "render",
        operands=7,
    )(received, block, lane, slot_row, slot_col, lanes, target)
    returned = exchange(gradients)
    (gradient,) = call(
        pullback_kernel,
        [shape((PARAMS, OWNED))],
        [
            vmem(EIGHT, F32), vmem(NINE, F32), vmem(EIGHT, F32), vmem(TABLE, F32),
            vmem(SPLIT, BF16),
        ],
        "pullback",
        operands=4,
    )(returned, owner_row, owner_col, params)
    return rendered, gradient


def solution(mesh):
    in_specs = (
        P(None, "dev"),
        P("dev", None, None),
        P("dev", None),
        P("dev"),
        P("dev"),
        P("dev", None, None),
    )
    out_specs = (P("dev", None, None), P(None, "dev"))
    return jax.shard_map(local, mesh=mesh, in_specs=in_specs, out_specs=out_specs, check_vma=False)
```

```python
import functools

import jax
import jax.numpy as jnp
from jax import lax
from jax.experimental import pallas as pl
from jax.experimental.pallas import tpu as pltpu
from jax.sharding import PartitionSpec as P

FOCAL = 1200.0
CENTER_X = 960.0
CENTER_Y = 540.0
DILATION = 0.3
BAND_ZERO = 0.28209479177387814
BAND_ONE = 0.4886025119029199
BAND_TWO = (
    1.0925484305920792,
    -1.0925484305920792,
    0.31539156525252005,
    -1.0925484305920792,
    0.5462742152960396,
)
BAND_THREE = (
    -0.5900435899266435,
    2.890611442640554,
    -0.4570457994644658,
    0.3731763325901154,
    -0.4570457994644658,
    1.445305721320277,
    -0.5900435899266435,
)
LOG2_E = 1.4426950408889634

DEVICES = 128
OWNED = 5120
CAP = 40
PARAMS = 59
BLOCKS = OWNED // 128
TILES = 16
SLOTS = 512
SEG = 46
SEG_PAD = 48
SEGS = 12
GROUP = 8
PASSES = 32 // GROUP
STEP_UNROLL = 2
BACK_UNROLL = 2
SHORT_UNROLL = 23
BF16 = jnp.bfloat16
MESH_ID = pl.DeviceIdType.MESH
F32 = jnp.float32
I32 = jnp.int32
VMEM_LIMIT = 48 * 1024 * 1024


def project(rows):
    x, y, z = rows[0], rows[1], rows[2]
    scales = [jnp.exp(rows[3 + k]) for k in range(3)]
    norm = jnp.sqrt(rows[6] * rows[6] + rows[7] * rows[7] + rows[8] * rows[8] + rows[9] * rows[9])
    qw, qx, qy, qz = (rows[6 + k] / norm for k in range(4))
    rotation = [
        [1.0 - 2.0 * (qy * qy + qz * qz), 2.0 * (qx * qy - qw * qz), 2.0 * (qx * qz + qw * qy)],
        [2.0 * (qx * qy + qw * qz), 1.0 - 2.0 * (qx * qx + qz * qz), 2.0 * (qy * qz - qw * qx)],
        [2.0 * (qx * qz - qw * qy), 2.0 * (qy * qz + qw * qx), 1.0 - 2.0 * (qx * qx + qy * qy)],
    ]
    spread = [[rotation[i][k] * scales[k] for k in range(3)] for i in range(3)]
    inverse_z = 1.0 / z
    diag = FOCAL * inverse_z
    jac_xz = -FOCAL * x * inverse_z * inverse_z
    jac_yz = -FOCAL * y * inverse_z * inverse_z
    across = [diag * spread[0][k] + jac_xz * spread[2][k] for k in range(3)]
    upward = [diag * spread[1][k] + jac_yz * spread[2][k] for k in range(3)]
    cov_xx = across[0] * across[0] + across[1] * across[1] + across[2] * across[2] + DILATION
    cov_xy = across[0] * upward[0] + across[1] * upward[1] + across[2] * upward[2]
    cov_yy = upward[0] * upward[0] + upward[1] * upward[1] + upward[2] * upward[2] + DILATION
    determinant = cov_xx * cov_yy - cov_xy * cov_xy
    distance = jnp.sqrt(x * x + y * y + z * z)
    fx, fy, fz = x / distance, y / distance, z / distance
    xx, yy, zz = fx * fx, fy * fy, fz * fz
    basis = [
        None,
        -BAND_ONE * fy,
        BAND_ONE * fz,
        -BAND_ONE * fx,
        BAND_TWO[0] * fx * fy,
        BAND_TWO[1] * fy * fz,
        BAND_TWO[2] * (2.0 * zz - xx - yy),
        BAND_TWO[3] * fx * fz,
        BAND_TWO[4] * (xx - yy),
        BAND_THREE[0] * fy * (3.0 * xx - yy),
        BAND_THREE[1] * fx * fy * fz,
        BAND_THREE[2] * fy * (4.0 * zz - xx - yy),
        BAND_THREE[3] * fz * (2.0 * zz - 3.0 * xx - 3.0 * yy),
        BAND_THREE[4] * fx * (4.0 * zz - xx - yy),
        BAND_THREE[5] * fz * (xx - yy),
        BAND_THREE[6] * fx * (xx - 3.0 * yy),
    ]
    colours = []
    for channel in range(3):
        total = BAND_ZERO * rows[11 + channel]
        for k in range(1, 16):
            total = total + basis[k] * rows[11 + 3 * k + channel]
        colours.append(jnp.maximum(total + 0.5, 0.0))
    return [
        FOCAL * x * inverse_z + CENTER_X,
        FOCAL * y * inverse_z + CENTER_Y,
        cov_yy / determinant,
        -cov_xy / determinant,
        cov_xx / determinant,
        1.0 / (1.0 + jnp.exp(-rows[10])),
        *colours,
    ]


def load_rows(params_ref, group):
    columns = pl.ds(pl.multiple_of(group * 1024, 1024), 1024)
    return [params_ref[row : row + 1, columns].reshape(8, 128) for row in range(PARAMS)]


def project_all(params_ref, screen_ref, ninth_ref):
    def one_group(group, carry):
        screen = project(load_rows(params_ref, group))
        for row in range(8):
            screen_ref[pl.ds(pl.multiple_of(group * 8, 8), 8), row, :] = screen[row]
        ninth_ref[group] = screen[8]
        return carry

    lax.fori_loop(0, OWNED // 1024, one_group, 0)


def repeat(count, unroll, body, state):
    def turn(index, state):
        for part in range(unroll):
            state = body(index * unroll + part, state)
        return state

    return lax.fori_loop(0, count // unroll, turn, state)


def gather(
    source_ref, ninth_ref, block_ref, lane_ref, out_ref, out_ninth_ref, split_ref,
    targets, sources, by_matmul, by_lanes,
):
    half = sources // 2
    eights = half * 8
    height = eights + 24
    width = 128 * by_matmul
    ninth = ninth_ref[...].reshape(-1, 128)
    rest = jnp.concatenate(
        [
            jnp.concatenate([ninth[0:half], ninth[half:sources]], axis=1),
            jnp.zeros((24 - half, 256), F32),
        ],
        axis=0,
    )
    main = jnp.concatenate(
        [
            source_ref[0:half].reshape(eights, 128),
            source_ref[half:sources].reshape(eights, 128),
        ],
        axis=1,
    )
    for part in range(3):
        for values, start in ((main, 0), (rest, eights)):
            rounded = values.astype(BF16)
            split_ref[part * height + start : part * height + start + values.shape[0]] = rounded
        main = main - main.astype(BF16).astype(F32)
        rest = rest - rest.astype(BF16).astype(F32)
    iota = lax.broadcasted_iota(I32, (256, width), 0).astype(F32).astype(BF16)
    sublane_rest = lax.broadcasted_iota(I32, (24, width), 0)
    sublane = lax.broadcasted_iota(I32, (8, 128), 0)

    def turn(index, carry):
        base = index * (by_matmul + by_lanes)
        rows = [pl.ds(base + k, 1) for k in range(by_matmul)]
        block = jnp.concatenate([block_ref[row, :] for row in rows], axis=1)
        lane = jnp.concatenate([lane_ref[row, :] for row in rows], axis=1)
        upper = jnp.where(block >= half, 1, 0)
        key = jnp.broadcast_to((lane + 128 * upper).astype(F32), (16, width)).astype(BF16)
        place = block - half * upper
        match = jnp.concatenate([key] * 16, axis=0) == iota
        pick = jnp.where(match, jnp.ones((), BF16), jnp.zeros((), BF16))
        parts = lax.dot_general(
            split_ref[...], pick, (((1,), (0,)), ((), ())), preferred_element_type=F32
        )
        for k in range(by_lanes):
            row = base + by_matmul + k
            lane = jnp.broadcast_to(lane_ref[pl.ds(row, 1), :], (8, 128))
            block = jnp.broadcast_to(block_ref[pl.ds(row, 1), :], (8, 128))
            total = jnp.zeros((8, 128), F32)
            for source in range(sources):
                picked = jnp.take_along_axis(
                    source_ref[source], lane, axis=1, mode="promise_in_bounds"
                )
                total = jnp.where(block == source, picked, total)
            out_ref[row] = total
            offset = block - sublane
            total = jnp.zeros((8, 128), F32)
            for source in range((sources + 7) // 8):
                picked = jnp.take_along_axis(
                    ninth_ref[source], lane, axis=1, mode="promise_in_bounds"
                )
                total = jnp.where(offset == 8 * source, picked, total)
            out_ninth_ref[pl.ds(row, 1), :] = jnp.sum(total, axis=0, keepdims=True)
        values = (parts[0:height] + parts[height : 2 * height]) + parts[2 * height : 3 * height]
        wide = jnp.broadcast_to(place, (8, width))
        total = jnp.zeros((8, width), F32)
        for source in range(half):
            total = jnp.where(wide == source, values[8 * source : 8 * source + 8], total)
        last = jnp.sum(
            jnp.where(sublane_rest == place, values[eights:height], 0.0), axis=0, keepdims=True
        )
        for k in range(by_matmul):
            out_ref[base + k] = total[:, 128 * k : 128 * k + 128]
            out_ninth_ref[pl.ds(base + k, 1), :] = last[:, 128 * k : 128 * k + 128]
        return carry

    lax.fori_loop(0, targets // (by_matmul + by_lanes), turn, 0)


def invert(block_ref, lane_ref, left_ref, right_ref, row_ref, col_ref, rows, blocks):
    iota_lane = lax.broadcasted_iota(I32, (1, 128), 1).astype(F32)
    iota_block = lax.broadcasted_iota(I32, (blocks, 128), 0)
    iota_sub = lax.broadcasted_iota(I32, (128, 128), 0)

    def one_row(row, carry):
        columns = pl.ds(pl.multiple_of(row * 128, 128), 128)
        here = iota_block == block_ref[pl.ds(row, 1), :]
        value = jnp.full((1, 128), 0.0, F32) + row.astype(F32)
        left_ref[0:blocks, columns] = jnp.where(here, value, 0.0).astype(BF16)
        left_ref[blocks : 2 * blocks, columns] = jnp.where(here, iota_lane, 0.0).astype(
            BF16
        )
        right_ref[:, columns] = jnp.where(
            iota_sub == lane_ref[pl.ds(row, 1), :], 1.0, 0.0
        ).astype(BF16)
        return carry

    repeat(rows, 2, one_row, 0)
    found = lax.dot_general(
        left_ref[...], right_ref[...], (((1,), (1,)), ((), ())), preferred_element_type=F32
    )
    row_ref[...] = (found[0:blocks] + 0.5).astype(I32)
    col_ref[...] = (found[blocks : 2 * blocks] + 0.5).astype(I32)


def pack_messages(rows_ref, ninth_ref, out_ref):
    flat = rows_ref[...].reshape(CAP * 8, 128)
    out_ref[:, 0, :] = flat[0:128].T
    out_ref[:, 1, :] = flat[128:256].T
    last = jnp.concatenate(
        [flat[256:320], ninth_ref[...], jnp.zeros((128 - 64 - CAP, 128), F32)], axis=0
    )
    out_ref[:, 2, :] = last.T
    out_ref[:, 3, :] = jnp.zeros((128, 128), F32)


def unpack_messages(message_ref, rows_ref, ninth_ref):
    rows_ref[0:16] = message_ref[:, 0, :].T.reshape(16, 8, 128)
    rows_ref[16:32] = message_ref[:, 1, :].T.reshape(16, 8, 128)
    last = message_ref[:, 2, :].T
    rows_ref[32:40] = last[0:64].reshape(8, 8, 128)
    ninth_ref[...] = last[64 : 64 + CAP].reshape(CAP // 8, 8, 128)


def greet(me):
    barrier = pltpu.get_barrier_semaphore()

    def one(turn, carry):
        pl.semaphore_signal(
            barrier, inc=1, device_id=(lax.rem(me + turn, DEVICES),), device_id_type=MESH_ID
        )
        return carry

    lax.fori_loop(1, DEVICES, one, 0)


def await_greetings():
    pl.semaphore_wait(pltpu.get_barrier_semaphore(), DEVICES - 1)


def send_all(source_ref, landing_ref, send_sem, receive_sem, own_sem, me):
    def one(turn, carry):
        peer = lax.rem(me + turn, DEVICES)
        pltpu.make_async_remote_copy(
            src_ref=source_ref.at[peer],
            dst_ref=landing_ref.at[me],
            send_sem=send_sem,
            recv_sem=receive_sem,
            device_id=(peer,),
            device_id_type=MESH_ID,
        ).start()
        return carry

    lax.fori_loop(1, DEVICES, one, 0)
    pltpu.make_async_copy(source_ref.at[me], landing_ref.at[me], own_sem).start()


def await_all(source_ref, landing_ref, send_sem, receive_sem, own_sem, me):
    others = pl.ds(0, DEVICES - 1)
    pltpu.make_async_copy(source_ref.at[me], landing_ref.at[me], own_sem).wait()
    pltpu.make_async_copy(landing_ref.at[others], landing_ref.at[others], receive_sem).wait()
    pltpu.make_async_copy(source_ref.at[others], source_ref.at[others], send_sem).wait()


def wanted_tables(wanted_ref, block_ref, lane_ref):
    wanted = wanted_ref[:, 0, :].astype(F32).T[0:CAP].astype(I32)
    block_ref[...] = wanted >> 7
    lane_ref[...] = wanted & 127


def lane_map(count_ref, place_ref):
    lane = lax.broadcasted_iota(I32, (1, 128), 1)
    tile = jnp.full((1, 128), -1, I32)
    segment = jnp.zeros((1, 128), I32)
    segments = jnp.zeros((1, 128), I32)
    count = jnp.zeros((1, 128), I32)
    origin_x = jnp.zeros((1, 128), I32)
    origin_y = jnp.zeros((1, 128), I32)
    base = jnp.int32(0)
    for index in range(TILES):
        listed = count_ref[0, index]
        place = place_ref[0, index]
        used = lax.div(listed + (SEG - 1), SEG)
        inside = (lane >= base) & (lane < base + used)
        place_y = lax.div(place, 120)
        tile = jnp.where(inside, index, tile)
        segment = jnp.where(inside, lane - base, segment)
        segments = jnp.where(inside, used, segments)
        count = jnp.where(inside, listed, count)
        origin_x = jnp.where(inside, 16 * (place - 120 * place_y), origin_x)
        origin_y = jnp.where(inside, 16 * place_y, origin_y)
        base = base + used
    return tile, segment, segments, count, origin_x, origin_y


def index_tables(
    count_ref, place_ref, slots_ref,
    block_ref, lane_ref, row_ref, col_ref, lanes_ref, all_ref, left_ref, right_ref,
):
    tile, segment, segments, count, origin_x, origin_y = lane_map(count_ref, place_ref)
    lanes_ref[0:1] = tile
    lanes_ref[1:2] = segment
    lanes_ref[2:3] = segments
    lanes_ref[3:4] = count
    lanes_ref[4:5] = origin_x
    lanes_ref[5:6] = origin_y
    lanes_ref[6:8] = jnp.zeros((2, 128), I32)
    slots = slots_ref[...]
    owner = ((slots.astype(F32) + 0.5) * (1.0 / CAP)).astype(I32)
    within = slots - owner * CAP
    pick = jnp.where(
        lax.broadcasted_iota(I32, (TILES, 128), 0) == tile, 1.0, 0.0
    ).astype(BF16)
    contract = (((0,), (0,)), ((), ()))
    step = lax.broadcasted_iota(I32, (SEG_PAD, 128), 0)
    live = (step < SEG) & (step + segment * SEG < count)
    for values, out, unused in ((within, block_ref, -1), (owner, lane_ref, 0)):
        all_ref[0:SLOTS] = lax.dot_general(
            values.astype(F32).astype(BF16), pick, contract, preferred_element_type=F32
        )
        all_ref[SLOTS:] = jnp.zeros_like(all_ref[SLOTS:])
        total = jnp.zeros((SEG_PAD, 128), F32)
        for part in range(SEGS):
            rows = all_ref[part * SEG : part * SEG + SEG_PAD]
            total = jnp.where(segment == part, rows, total)
        out[...] = jnp.where(live, (total + 0.5).astype(I32), unused)
    invert(block_ref, lane_ref, left_ref, right_ref, row_ref, col_ref, SEG, CAP)


def fetch_kernel(
    requests_ref, params_ref, count_ref, place_ref, slots_ref,
    source_ref, source_ninth_ref, block_ref, lane_ref, row_ref, col_ref, lanes_ref,
    wanted_block_ref, wanted_lane_ref,
    request_ref, wanted_ref, vmem_params_ref, screen_ref, ninth_ref, out_ref, out_ninth_ref,
    split_ref, message_ref, landing_ref, all_ref, left_ref, right_ref,
    params_sem, request_send_sem, request_sem, request_own_sem, send_sem, receive_sem, own_sem,
):
    me = lax.axis_index("dev")
    load = pltpu.make_async_copy(params_ref, vmem_params_ref, params_sem)
    load.start()
    greet(me)
    request_ref[:, 0, :] = jnp.concatenate(
        [requests_ref[0], jnp.zeros((DEVICES, 128 - CAP), I32)], axis=1
    )
    await_greetings()
    request_sems = (request_send_sem, request_sem, request_own_sem, me)
    send_all(request_ref, wanted_ref, *request_sems)
    load.wait()
    project_all(vmem_params_ref, screen_ref, ninth_ref)
    index_tables(
        count_ref, place_ref, slots_ref,
        block_ref, lane_ref, row_ref, col_ref, lanes_ref, all_ref, left_ref, right_ref,
    )
    await_all(request_ref, wanted_ref, *request_sems)
    wanted_tables(wanted_ref, wanted_block_ref, wanted_lane_ref)
    gather(
        screen_ref, ninth_ref, wanted_block_ref, wanted_lane_ref, out_ref, out_ninth_ref,
        split_ref, CAP, BLOCKS, 10, 10,
    )
    pack_messages(out_ref, out_ninth_ref, message_ref)
    sems = (send_sem, receive_sem, own_sem, me)
    send_all(message_ref, landing_ref, *sems)
    await_all(message_ref, landing_ref, *sems)
    unpack_messages(landing_ref, source_ref, source_ninth_ref)


def return_kernel(
    message_ref, block_ref, lane_ref, source_ref, source_ninth_ref, row_ref, col_ref,
    landing_ref, left_ref, right_ref, send_sem, receive_sem, own_sem,
):
    me = lax.axis_index("dev")
    greet(me)
    await_greetings()
    sems = (send_sem, receive_sem, own_sem, me)
    send_all(message_ref, landing_ref, *sems)
    invert(block_ref, lane_ref, left_ref, right_ref, row_ref, col_ref, CAP, BLOCKS)
    await_all(message_ref, landing_ref, *sems)
    unpack_messages(landing_ref, source_ref, source_ninth_ref)


def render_kernel(
    source_ref, source_ninth_ref, block_ref, lane_ref, row_ref, col_ref, lanes_ref, target_ref,
    rendered_ref, gradient_ref,
    rows_ref, ninth_ref, pre_ref, alpha_ref, weight_ref,
    trans_ref, colour_ref, behind_ref, moment_ref, grad_ref, grad_ninth_ref,
    back_ref, back_ninth_ref, split_ref, split_back_ref,
):
    gather(
        source_ref, source_ninth_ref, block_ref, lane_ref, rows_ref, ninth_ref, split_ref,
        SEG, CAP, 12, 11,
    )
    tile = lanes_ref[0:1]
    segment = lanes_ref[1:2]
    segments = lanes_ref[2:3]
    origin_x = lanes_ref[4:5].astype(F32)
    origin_y = lanes_ref[5:6].astype(F32)
    sub = lax.broadcasted_iota(I32, (8, 128), 0).astype(F32) + 0.5

    def wide(row):
        return jnp.broadcast_to(row, (8, 128))

    def prepare(step, carry):
        attrs = rows_ref[step]
        screen_x = attrs[0:1] - origin_x
        screen_y = attrs[1:2] - origin_y
        curve_x = wide(-0.5 * LOG2_E * attrs[2:3])
        curve_xy = wide(-LOG2_E * attrs[3:4])
        for half in range(2):
            delta = (sub + 8.0 * half) - wide(screen_x)
            pre_ref[step, half] = curve_x * delta * delta
            pre_ref[step, 2 + half] = curve_xy * delta
            pre_ref[step, 9 + half] = delta
        pre_ref[step, 4] = wide(screen_y)
        pre_ref[step, 5] = wide(-0.5 * LOG2_E * attrs[4:5])
        pre_ref[step, 6] = wide(attrs[5:6])
        pre_ref[step, 7] = wide(attrs[6:7])
        pre_ref[step, 8] = wide(attrs[7:8])
        pre_ref[step, 11] = wide(ninth_ref[pl.ds(step, 1), :])
        return carry

    repeat(SEG, SHORT_UNROLL, prepare, 0)

    for index in range(PASSES):
        first_v = index * (GROUP // 2) + 0.5

        def one_step(step, state):
            trans, red, green, blue = (list(part) for part in state)
            opacity, screen_y, curve_y = pre_ref[step, 6], pre_ref[step, 4], pre_ref[step, 5]
            colours = (pre_ref[step, 7], pre_ref[step, 8], pre_ref[step, 11])
            for pair in range(GROUP // 2):
                delta_y = (first_v + float(pair)) - screen_y
                bend = curve_y * delta_y * delta_y
                for half in range(2):
                    k = 2 * pair + half
                    power = pre_ref[step, half] + (bend + pre_ref[step, 2 + half] * delta_y)
                    alpha = opacity * jnp.exp2(power)
                    weight = alpha * trans[k]
                    trans[k] = trans[k] - weight
                    red[k] = red[k] + colours[0] * weight
                    green[k] = green[k] + colours[1] * weight
                    blue[k] = blue[k] + colours[2] * weight
                    alpha_ref[index, step, k] = alpha
                    weight_ref[index, step, k] = weight
            return tuple(trans), tuple(red), tuple(green), tuple(blue)

        ones = tuple(jnp.ones((8, 128), F32) for _ in range(GROUP))
        zeros = tuple(jnp.zeros((8, 128), F32) for _ in range(GROUP))
        state = repeat(SEG, STEP_UNROLL, one_step, (ones, zeros, zeros, zeros))
        for k in range(GROUP):
            rows = pl.ds((index * GROUP + k) * 8, 8)
            trans_ref[rows, :] = state[0][k]
            for channel in range(3):
                colour_ref[channel, rows, :] = state[1 + channel][k]

    through = trans_ref[...]
    start = jnp.where(segment == 0, 1.0, pltpu.roll(through, 1, 1))
    for shift in (1, 2, 4, 8):
        start = start * jnp.where(segment >= shift, pltpu.roll(start, shift, 1), 1.0)
    pick = jnp.where(lax.broadcasted_iota(I32, (TILES, 128), 0) == tile, 1.0, 0.0)
    behind = jnp.zeros((256, 128), F32)
    for channel in range(3):
        image = lax.dot_general(
            pick, colour_ref[channel] * start, (((1,), (1,)), ((), ())),
            preferred_element_type=F32, precision=lax.Precision.HIGHEST,
        )
        rendered_ref[:, channel, :] = image
        error = (image - target_ref[:, channel, :]) * (1.0 / 256.0)
        spread = lax.dot_general(
            error, pick, (((0,), (0,)), ((), ())),
            preferred_element_type=F32, precision=lax.Precision.HIGHEST,
        )
        behind = behind + spread * colour_ref[channel]
        colour_ref[channel] = spread * start
    left = segments - 1 - segment
    factor = jnp.where(left >= 1, pltpu.roll(through, 127, 1), 0.0)
    behind = jnp.where(left >= 1, pltpu.roll(behind, 127, 1), 0.0)
    for shift in (1, 2, 4, 8):
        reach = left >= shift
        behind = behind + factor * jnp.where(reach, pltpu.roll(behind, 128 - shift, 1), 0.0)
        factor = factor * jnp.where(reach, pltpu.roll(factor, 128 - shift, 1), 0.0)
    behind_ref[...] = behind * start

    for index in range(PASSES):
        first_v = index * (GROUP // 2) + 0.5
        rows = [pl.ds((index * GROUP + k) * 8, 8) for k in range(GROUP)]
        errors = [[colour_ref[channel, rows[k], :] for channel in range(3)] for k in range(GROUP)]

        def one_step(count, state):
            step = SEG - 1 - count
            state = list(state)
            screen_y = pre_ref[step, 4]
            colours = (pre_ref[step, 7], pre_ref[step, 8], pre_ref[step, 11])
            sums = [moment_ref[step, row] if index else None for row in range(9)]

            def add(row, value):
                sums[row] = value if sums[row] is None else sums[row] + value

            for pair in range(GROUP // 2):
                delta_y = (first_v + float(pair)) - screen_y
                for half in range(2):
                    k = 2 * pair + half
                    alpha = alpha_ref[index, step, k]
                    weight = weight_ref[index, step, k]
                    shade = (
                        colours[0] * errors[k][0]
                        + colours[1] * errors[k][1]
                        + colours[2] * errors[k][2]
                    )
                    gap = shade - state[k]
                    state[k] = state[k] + alpha * gap
                    slope = weight * gap
                    slope_y = slope * delta_y
                    add(3 * half, slope)
                    add(3 * half + 1, slope_y)
                    add(3 * half + 2, slope_y * delta_y)
                    for channel in range(3):
                        add(6 + channel, weight * errors[k][channel])
            for row in range(9):
                moment_ref[step, row] = sums[row]
            return tuple(state)

        repeat(
            SEG, BACK_UNROLL, one_step, tuple(behind_ref[rows[k], :] for k in range(GROUP))
        )

    def finish(step, carry):
        delta = [pre_ref[step, 9], pre_ref[step, 10]]
        sums = [moment_ref[step, row] for row in range(9)]
        flat = [sums[0], sums[3]]
        tilt = [sums[1], sums[4]]
        bend = [sums[2], sums[5]]
        side = [flat[half] * delta[half] for half in range(2)]

        def total(register):
            return jnp.sum(register, axis=0, keepdims=True)

        m00 = total(flat[0] + flat[1])
        m10 = total(side[0] + side[1])
        m01 = total(tilt[0] + tilt[1])
        m20 = total(side[0] * delta[0] + side[1] * delta[1])
        m11 = total(tilt[0] * delta[0] + tilt[1] * delta[1])
        m02 = total(bend[0] + bend[1])
        attrs = rows_ref[step]
        conic_a, conic_b, conic_c = attrs[2:3], attrs[3:4], attrs[4:5]
        grad_ref[step] = jnp.concatenate(
            [
                conic_a * m10 + conic_b * m01,
                conic_b * m10 + conic_c * m01,
                -0.5 * m20,
                -m11,
                -0.5 * m02,
                m00,
                total(sums[6]),
                total(sums[7]),
            ],
            axis=0,
        )
        ninth_ref[pl.ds(step, 1), :] = total(sums[8])
        return carry

    repeat(SEG, SHORT_UNROLL, finish, 0)
    ninth_ref[SEG:SEG_PAD] = jnp.zeros((SEG_PAD - SEG, 128), F32)
    grad_ninth_ref[...] = ninth_ref[...].reshape(SEG_PAD // 8, 8, 128)
    gather(
        grad_ref, grad_ninth_ref, row_ref, col_ref, back_ref, back_ninth_ref, split_back_ref,
        CAP, SEG, 10, 10,
    )
    pack_messages(back_ref, back_ninth_ref, gradient_ref)


def pullback_kernel(
    source_ref, source_ninth_ref, row_ref, col_ref, params_ref, gradient_ref,
    rows_ref, ninth_ref, split_ref,
):
    gather(
        source_ref, source_ninth_ref, row_ref, col_ref, rows_ref, ninth_ref, split_ref,
        BLOCKS, CAP, 10, 10,
    )

    def one_group(group, carry):
        columns = pl.ds(pl.multiple_of(group * 1024, 1024), 1024)
        eight = pl.ds(pl.multiple_of(group * 8, 8), 8)
        rows = load_rows(params_ref, group)
        screen_grad = [rows_ref[eight, row, :] for row in range(8)] + [ninth_ref[eight, :]]
        screen, pullback = jax.vjp(project, rows)
        by_logit = screen_grad[5] * (1.0 / (1.0 + jnp.exp(rows[10])))
        screen_grad[5] = jnp.zeros_like(by_logit)
        (grads,) = pullback(screen_grad)
        grads[10] = by_logit
        for row in range(PARAMS):
            gradient_ref[row : row + 1, columns] = grads[row].reshape(1, 1024)
        return carry

    lax.fori_loop(0, OWNED // 1024, one_group, 0)


def shape(dims, dtype=F32):
    return jax.ShapeDtypeStruct(dims, dtype)


def call(kernel, outs, specs, scratch, name, collective=None):
    params = {"vmem_limit_bytes": VMEM_LIMIT}
    if collective is not None:
        params.update(collective_id=collective, has_side_effects=True)
    spaces = {"v": pltpu.VMEM, "s": pltpu.SMEM, "h": pl.ANY}
    return pl.pallas_call(
        kernel,
        out_shape=outs,
        in_specs=[pl.BlockSpec(memory_space=spaces[kind]) for kind in specs],
        out_specs=[pl.BlockSpec(memory_space=pltpu.VMEM)] * len(outs),
        scratch_shapes=scratch,
        compiler_params=pltpu.CompilerParams(**params),
        name=name,
    )


SPLIT = (3 * (CAP // 2 * 8 + 24), 256)
SPLIT_BACK = (3 * (SEG // 2 * 8 + 24), 256)
MESSAGE = (DEVICES, 4, 128)
REQUEST = (DEVICES, 1, 128)
TABLE = (CAP, 128)
STEPS = (SEG_PAD, 128)
EIGHT = (CAP, 8, 128)
NINE = (CAP // 8, 8, 128)


def local(params, requests, tile_slots, tile_count, tile_place, target):
    vmem = pltpu.VMEM
    sems = [pltpu.SemaphoreType.DMA] * 3
    source, source_ninth, block, lane, slot_row, slot_col, lanes, wanted_block, wanted_lane = call(
        fetch_kernel,
        [
            shape(EIGHT), shape(NINE), shape(STEPS, I32), shape(STEPS, I32), shape(TABLE, I32),
            shape(TABLE, I32), shape((8, 128), I32), shape(TABLE, I32), shape(TABLE, I32),
        ],
        "vhssv",
        [
            vmem(REQUEST, I32), vmem(REQUEST, I32), vmem((PARAMS, OWNED), F32),
            vmem(EIGHT, F32), vmem(NINE, F32), vmem(EIGHT, F32), vmem(TABLE, F32),
            vmem(SPLIT, BF16), vmem(MESSAGE, F32), vmem(MESSAGE, F32),
            vmem((SEGS * SEG + 8, 128), F32),
            vmem((2 * CAP, SEG * 128), BF16), vmem((128, SEG * 128), BF16),
            pltpu.SemaphoreType.DMA, *sems, *sems,
        ],
        "fetch",
        0,
    )(requests, params, tile_count.reshape(1, TILES), tile_place.reshape(1, TILES), tile_slots)
    rendered, gradients = call(
        render_kernel,
        [shape((TILES, 3, 256)), shape(MESSAGE)],
        "vvvvvvvv",
        [
            vmem((SEG, 8, 128), F32), vmem(STEPS, F32),
            vmem((SEG, 12, 8, 128), F32),
            vmem((PASSES, SEG, GROUP, 8, 128), F32), vmem((PASSES, SEG, GROUP, 8, 128), F32),
            vmem((256, 128), F32), vmem((3, 256, 128), F32), vmem((256, 128), F32),
            vmem((SEG, 9, 8, 128), F32),
            vmem((SEG, 8, 128), F32), vmem((SEG_PAD // 8, 8, 128), F32),
            vmem(EIGHT, F32), vmem(TABLE, F32), vmem(SPLIT, BF16), vmem(SPLIT_BACK, BF16),
        ],
        "render",
    )(source, source_ninth, block, lane, slot_row, slot_col, lanes, target)
    back, back_ninth, owner_row, owner_col = call(
        return_kernel,
        [shape(EIGHT), shape(NINE), shape(TABLE, I32), shape(TABLE, I32)],
        "vvv",
        [
            vmem(MESSAGE, F32),
            vmem((2 * BLOCKS, CAP * 128), BF16), vmem((128, CAP * 128), BF16),
            *sems,
        ],
        "return",
        1,
    )(gradients, wanted_block, wanted_lane)
    (gradient,) = call(
        pullback_kernel,
        [shape((PARAMS, OWNED))],
        "vvvvv",
        [vmem(EIGHT, F32), vmem(TABLE, F32), vmem(SPLIT, BF16)],
        "pullback",
    )(back, back_ninth, owner_row, owner_col, params)
    return rendered, gradient


def solution(mesh):
    in_specs = (
        P(None, "dev"),
        P("dev", None, None),
        P("dev", None),
        P("dev"),
        P("dev"),
        P("dev", None, None),
    )
    out_specs = (P("dev", None, None), P(None, "dev"))
    return jax.shard_map(local, mesh=mesh, in_specs=in_specs, out_specs=out_specs, check_vma=False)
```

```python
import functools

import jax
import jax.numpy as jnp
from jax import lax
from jax.experimental import pallas as pl
from jax.experimental.pallas import tpu as pltpu
from jax.sharding import PartitionSpec as P

FOCAL = 1200.0
CENTER_X = 960.0
CENTER_Y = 540.0
DILATION = 0.3
BAND_ZERO = 0.28209479177387814
BAND_ONE = 0.4886025119029199
BAND_TWO = (
    1.0925484305920792,
    -1.0925484305920792,
    0.31539156525252005,
    -1.0925484305920792,
    0.5462742152960396,
)
BAND_THREE = (
    -0.5900435899266435,
    2.890611442640554,
    -0.4570457994644658,
    0.3731763325901154,
    -0.4570457994644658,
    1.445305721320277,
    -0.5900435899266435,
)
LOG2_E = 1.4426950408889634

DEVICES = 128
OWNED = 5120
CAP = 40
PARAMS = 59
BLOCKS = OWNED // 128
TILES = 16
SLOTS = 512
SEG = 46
SEG_PAD = 48
SEGS = 12
GROUP = 8
PASSES = 32 // GROUP
STEP_UNROLL = 2
BACK_UNROLL = 2
SHORT_UNROLL = 23
BF16 = jnp.bfloat16
MESH_ID = pl.DeviceIdType.MESH
F32 = jnp.float32
I32 = jnp.int32
VMEM_LIMIT = 64 * 1000 * 1000


def project(rows):
    x, y, z = rows[0], rows[1], rows[2]
    scales = [jnp.exp(rows[3 + k]) for k in range(3)]
    norm = jnp.sqrt(rows[6] * rows[6] + rows[7] * rows[7] + rows[8] * rows[8] + rows[9] * rows[9])
    qw, qx, qy, qz = (rows[6 + k] / norm for k in range(4))
    rotation = [
        [1.0 - 2.0 * (qy * qy + qz * qz), 2.0 * (qx * qy - qw * qz), 2.0 * (qx * qz + qw * qy)],
        [2.0 * (qx * qy + qw * qz), 1.0 - 2.0 * (qx * qx + qz * qz), 2.0 * (qy * qz - qw * qx)],
        [2.0 * (qx * qz - qw * qy), 2.0 * (qy * qz + qw * qx), 1.0 - 2.0 * (qx * qx + qy * qy)],
    ]
    spread = [[rotation[i][k] * scales[k] for k in range(3)] for i in range(3)]
    inverse_z = 1.0 / z
    diag = FOCAL * inverse_z
    jac_xz = -FOCAL * x * inverse_z * inverse_z
    jac_yz = -FOCAL * y * inverse_z * inverse_z
    across = [diag * spread[0][k] + jac_xz * spread[2][k] for k in range(3)]
    upward = [diag * spread[1][k] + jac_yz * spread[2][k] for k in range(3)]
    cov_xx = across[0] * across[0] + across[1] * across[1] + across[2] * across[2] + DILATION
    cov_xy = across[0] * upward[0] + across[1] * upward[1] + across[2] * upward[2]
    cov_yy = upward[0] * upward[0] + upward[1] * upward[1] + upward[2] * upward[2] + DILATION
    determinant = cov_xx * cov_yy - cov_xy * cov_xy
    distance = jnp.sqrt(x * x + y * y + z * z)
    fx, fy, fz = x / distance, y / distance, z / distance
    xx, yy, zz = fx * fx, fy * fy, fz * fz
    basis = [
        None,
        -BAND_ONE * fy,
        BAND_ONE * fz,
        -BAND_ONE * fx,
        BAND_TWO[0] * fx * fy,
        BAND_TWO[1] * fy * fz,
        BAND_TWO[2] * (2.0 * zz - xx - yy),
        BAND_TWO[3] * fx * fz,
        BAND_TWO[4] * (xx - yy),
        BAND_THREE[0] * fy * (3.0 * xx - yy),
        BAND_THREE[1] * fx * fy * fz,
        BAND_THREE[2] * fy * (4.0 * zz - xx - yy),
        BAND_THREE[3] * fz * (2.0 * zz - 3.0 * xx - 3.0 * yy),
        BAND_THREE[4] * fx * (4.0 * zz - xx - yy),
        BAND_THREE[5] * fz * (xx - yy),
        BAND_THREE[6] * fx * (xx - 3.0 * yy),
    ]
    colours = []
    for channel in range(3):
        total = BAND_ZERO * rows[11 + channel]
        for k in range(1, 16):
            total = total + basis[k] * rows[11 + 3 * k + channel]
        colours.append(jnp.maximum(total + 0.5, 0.0))
    return [
        FOCAL * x * inverse_z + CENTER_X,
        FOCAL * y * inverse_z + CENTER_Y,
        cov_yy / determinant,
        -cov_xy / determinant,
        cov_xx / determinant,
        1.0 / (1.0 + jnp.exp(-rows[10])),
        *colours,
    ]


def load_rows(params_ref, columns):
    return [params_ref[row : row + 1, columns].reshape(8, 128) for row in range(PARAMS)]


def project_all(params_ref, screen_ref, ninth_ref):
    def one_group(group, carry):
        screen = project(
            load_rows(params_ref, pl.ds(pl.multiple_of(group * 1024, 1024), 1024))
        )
        for row in range(8):
            screen_ref[pl.ds(pl.multiple_of(group * 8, 8), 8), row, :] = screen[row]
        ninth_ref[group] = screen[8]
        return carry

    lax.fori_loop(0, OWNED // 1024, one_group, 0)


def repeat(count, unroll, body, state):
    def turn(index, state):
        for part in range(unroll):
            state = body(index * unroll + part, state)
        return state

    return lax.fori_loop(0, count // unroll, turn, state)


def gather(
    source_ref, ninth_ref, block_ref, lane_ref, out_ref, out_ninth_ref, split_ref,
    targets, sources, by_matmul, by_lanes,
):
    half = sources // 2
    eights = half * 8
    height = eights + 24
    width = 128 * by_matmul
    ninth = ninth_ref[...].reshape(-1, 128)
    rest = jnp.concatenate(
        [
            jnp.concatenate([ninth[0:half], ninth[half:sources]], axis=1),
            jnp.zeros((24 - half, 256), F32),
        ],
        axis=0,
    )
    main = jnp.concatenate(
        [
            source_ref[0:half].reshape(eights, 128),
            source_ref[half:sources].reshape(eights, 128),
        ],
        axis=1,
    )
    for part in range(3):
        for values, start in ((main, 0), (rest, eights)):
            rounded = values.astype(BF16)
            split_ref[part * height + start : part * height + start + values.shape[0]] = rounded
        main = main - main.astype(BF16).astype(F32)
        rest = rest - rest.astype(BF16).astype(F32)
    iota = lax.broadcasted_iota(I32, (256, width), 0).astype(F32).astype(BF16)
    sublane_rest = lax.broadcasted_iota(I32, (24, width), 0)
    sublane = lax.broadcasted_iota(I32, (8, 128), 0)

    def turn(index, carry):
        base = index * (by_matmul + by_lanes)
        rows = [pl.ds(base + k, 1) for k in range(by_matmul)]
        block = jnp.concatenate([block_ref[row, :] for row in rows], axis=1)
        lane = jnp.concatenate([lane_ref[row, :] for row in rows], axis=1)
        upper = jnp.where(block >= half, 1, 0)
        key = jnp.broadcast_to((lane + 128 * upper).astype(F32), (16, width)).astype(BF16)
        place = block - half * upper
        match = jnp.concatenate([key] * 16, axis=0) == iota
        pick = jnp.where(match, jnp.ones((), BF16), jnp.zeros((), BF16))
        parts = lax.dot_general(
            split_ref[...], pick, (((1,), (0,)), ((), ())), preferred_element_type=F32
        )
        for k in range(by_lanes):
            row = base + by_matmul + k
            lane = jnp.broadcast_to(lane_ref[pl.ds(row, 1), :], (8, 128))
            block = jnp.broadcast_to(block_ref[pl.ds(row, 1), :], (8, 128))
            total = jnp.zeros((8, 128), F32)
            for source in range(sources):
                picked = jnp.take_along_axis(
                    source_ref[source], lane, axis=1, mode="promise_in_bounds"
                )
                total = jnp.where(block == source, picked, total)
            out_ref[row] = total
            offset = block - sublane
            total = jnp.zeros((8, 128), F32)
            for source in range((sources + 7) // 8):
                picked = jnp.take_along_axis(
                    ninth_ref[source], lane, axis=1, mode="promise_in_bounds"
                )
                total = jnp.where(offset == 8 * source, picked, total)
            out_ninth_ref[pl.ds(row, 1), :] = jnp.sum(total, axis=0, keepdims=True)
        values = (parts[0:height] + parts[height : 2 * height]) + parts[2 * height : 3 * height]
        wide = jnp.broadcast_to(place, (8, width))
        total = jnp.zeros((8, width), F32)
        for source in range(half):
            total = jnp.where(wide == source, values[8 * source : 8 * source + 8], total)
        last = jnp.sum(
            jnp.where(sublane_rest == place, values[eights:height], 0.0), axis=0, keepdims=True
        )
        for k in range(by_matmul):
            out_ref[base + k] = total[:, 128 * k : 128 * k + 128]
            out_ninth_ref[pl.ds(base + k, 1), :] = last[:, 128 * k : 128 * k + 128]
        return carry

    lax.fori_loop(0, targets // (by_matmul + by_lanes), turn, 0)


def invert(block_ref, lane_ref, left_ref, right_ref, row_ref, col_ref, rows, blocks):
    iota_lane = lax.broadcasted_iota(I32, (1, 128), 1).astype(F32)
    iota_block = lax.broadcasted_iota(I32, (blocks, 128), 0)
    iota_sub = lax.broadcasted_iota(I32, (128, 128), 0)

    def one_row(row, carry):
        columns = pl.ds(pl.multiple_of(row * 128, 128), 128)
        here = iota_block == block_ref[pl.ds(row, 1), :]
        value = jnp.full((1, 128), 0.0, F32) + row.astype(F32)
        left_ref[0:blocks, columns] = jnp.where(here, value, 0.0).astype(BF16)
        left_ref[blocks : 2 * blocks, columns] = jnp.where(here, iota_lane, 0.0).astype(
            BF16
        )
        right_ref[:, columns] = jnp.where(
            iota_sub == lane_ref[pl.ds(row, 1), :], 1.0, 0.0
        ).astype(BF16)
        return carry

    repeat(rows, 2, one_row, 0)
    found = lax.dot_general(
        left_ref[...], right_ref[...], (((1,), (1,)), ((), ())), preferred_element_type=F32
    )
    row_ref[...] = (found[0:blocks] + 0.5).astype(I32)
    col_ref[...] = (found[blocks : 2 * blocks] + 0.5).astype(I32)


def pack_messages(rows_ref, ninth_ref, out_ref):
    flat = rows_ref[...].reshape(CAP * 8, 128)
    out_ref[:, 0, :] = flat[0:128].T
    out_ref[:, 1, :] = flat[128:256].T
    last = jnp.concatenate(
        [flat[256:320], ninth_ref[...], jnp.zeros((128 - 64 - CAP, 128), F32)], axis=0
    )
    out_ref[:, 2, :] = last.T


def unpack_messages(message_ref, rows_ref, ninth_ref):
    rows_ref[0:16] = message_ref[:, 0, :].T.reshape(16, 8, 128)
    rows_ref[16:32] = message_ref[:, 1, :].T.reshape(16, 8, 128)
    last = message_ref[:, 2, :].T
    rows_ref[32:40] = last[0:64].reshape(8, 8, 128)
    ninth_ref[...] = last[64 : 64 + CAP].reshape(CAP // 8, 8, 128)


def greet(me):
    barrier = pltpu.get_barrier_semaphore()

    def one(turn, carry):
        pl.semaphore_signal(
            barrier, inc=1, device_id=(lax.rem(me + turn, DEVICES),), device_id_type=MESH_ID
        )
        return carry

    lax.fori_loop(1, DEVICES, one, 0)


def await_greetings():
    pl.semaphore_wait(pltpu.get_barrier_semaphore(), DEVICES - 1)


def send_all(source_ref, landing_ref, send_sem, receive_sem, own_sem, me):
    def one(turn, carry):
        peer = lax.rem(me + turn, DEVICES)
        pltpu.make_async_remote_copy(
            src_ref=source_ref.at[peer],
            dst_ref=landing_ref.at[me],
            send_sem=send_sem,
            recv_sem=receive_sem,
            device_id=(peer,),
            device_id_type=MESH_ID,
        ).start()
        return carry

    lax.fori_loop(1, DEVICES, one, 0)
    pltpu.make_async_copy(source_ref.at[me], landing_ref.at[me], own_sem).start()


def await_all(source_ref, landing_ref, send_sem, receive_sem, own_sem, me):
    others = pl.ds(0, DEVICES - 1)
    pltpu.make_async_copy(source_ref.at[me], landing_ref.at[me], own_sem).wait()
    pltpu.make_async_copy(landing_ref.at[others], landing_ref.at[others], receive_sem).wait()
    pltpu.make_async_copy(source_ref.at[others], source_ref.at[others], send_sem).wait()


def wanted_tables(wanted_ref, block_ref, lane_ref):
    wanted = wanted_ref[:, 0, :].astype(F32).T[0:CAP].astype(I32)
    block_ref[...] = wanted >> 7
    lane_ref[...] = wanted & 127


def lane_map(count_ref, place_ref):
    lane = lax.broadcasted_iota(I32, (1, 128), 1)
    tile = jnp.full((1, 128), -1, I32)
    segment = jnp.zeros((1, 128), I32)
    segments = jnp.zeros((1, 128), I32)
    count = jnp.zeros((1, 128), I32)
    origin_x = jnp.zeros((1, 128), I32)
    origin_y = jnp.zeros((1, 128), I32)
    base = jnp.int32(0)
    for index in range(TILES):
        listed = count_ref[index]
        place = place_ref[index]
        used = lax.div(listed + (SEG - 1), SEG)
        inside = (lane >= base) & (lane < base + used)
        place_y = lax.div(place, 120)
        tile = jnp.where(inside, index, tile)
        segment = jnp.where(inside, lane - base, segment)
        segments = jnp.where(inside, used, segments)
        count = jnp.where(inside, listed, count)
        origin_x = jnp.where(inside, 16 * (place - 120 * place_y), origin_x)
        origin_y = jnp.where(inside, 16 * place_y, origin_y)
        base = base + used
    return tile, segment, segments, count, origin_x, origin_y


def index_tables(
    count_ref, place_ref, slots_ref,
    block_ref, lane_ref, row_ref, col_ref, lanes_ref, all_ref, left_ref, right_ref,
):
    tile, segment, segments, count, origin_x, origin_y = lane_map(count_ref, place_ref)
    lanes_ref[0:1] = tile
    lanes_ref[1:2] = segment
    lanes_ref[2:3] = segments
    lanes_ref[3:4] = count
    lanes_ref[4:5] = origin_x
    lanes_ref[5:6] = origin_y
    lanes_ref[6:8] = jnp.zeros((2, 128), I32)
    slots = slots_ref[...]
    owner = ((slots.astype(F32) + 0.5) * (1.0 / CAP)).astype(I32)
    within = slots - owner * CAP
    pick = jnp.where(
        lax.broadcasted_iota(I32, (TILES, 128), 0) == tile, 1.0, 0.0
    ).astype(BF16)
    contract = (((0,), (0,)), ((), ()))
    step = lax.broadcasted_iota(I32, (SEG_PAD, 128), 0)
    live = (step < SEG) & (step + segment * SEG < count)
    for values, out, unused in ((within, block_ref, -1), (owner, lane_ref, 0)):
        all_ref[0:SLOTS] = lax.dot_general(
            values.astype(F32).astype(BF16), pick, contract, preferred_element_type=F32
        )
        all_ref[SLOTS:] = jnp.zeros_like(all_ref[SLOTS:])
        total = jnp.zeros((SEG_PAD, 128), F32)
        for part in range(SEGS):
            rows = all_ref[part * SEG : part * SEG + SEG_PAD]
            total = jnp.where(segment == part, rows, total)
        out[...] = jnp.where(live, (total + 0.5).astype(I32), unused)
    invert(block_ref, lane_ref, left_ref, right_ref, row_ref, col_ref, SEG, CAP)


def render(
    source_ref, source_ninth_ref, block_ref, lane_ref, row_ref, col_ref, lanes_ref, target_ref,
    rendered_ref, gradient_ref,
    rows_ref, ninth_ref, pre_ref, alpha_ref, weight_ref,
    trans_ref, colour_ref, behind_ref, moment_ref, grad_ref, grad_ninth_ref,
    back_ref, back_ninth_ref, split_ref, split_back_ref,
):
    gather(
        source_ref, source_ninth_ref, block_ref, lane_ref, rows_ref, ninth_ref, split_ref,
        SEG, CAP, 12, 11,
    )
    tile = lanes_ref[0:1]
    segment = lanes_ref[1:2]
    segments = lanes_ref[2:3]
    origin_x = lanes_ref[4:5].astype(F32)
    origin_y = lanes_ref[5:6].astype(F32)
    sub = lax.broadcasted_iota(I32, (8, 128), 0).astype(F32) + 0.5

    def wide(row):
        return jnp.broadcast_to(row, (8, 128))

    def prepare(step, carry):
        attrs = rows_ref[step]
        screen_x = attrs[0:1] - origin_x
        screen_y = attrs[1:2] - origin_y
        curve_x = wide(-0.5 * LOG2_E * attrs[2:3])
        curve_xy = wide(-LOG2_E * attrs[3:4])
        for half in range(2):
            delta = (sub + 8.0 * half) - wide(screen_x)
            pre_ref[step, half] = curve_x * delta * delta
            pre_ref[step, 2 + half] = curve_xy * delta
            pre_ref[step, 9 + half] = delta
        pre_ref[step, 4] = wide(screen_y)
        pre_ref[step, 5] = wide(-0.5 * LOG2_E * attrs[4:5])
        pre_ref[step, 6] = wide(attrs[5:6])
        pre_ref[step, 7] = wide(attrs[6:7])
        pre_ref[step, 8] = wide(attrs[7:8])
        pre_ref[step, 11] = wide(ninth_ref[pl.ds(step, 1), :])
        return carry

    repeat(SEG, SHORT_UNROLL, prepare, 0)

    for index in range(PASSES):
        first_v = index * (GROUP // 2) + 0.5

        def one_step(step, state):
            trans, red, green, blue = (list(part) for part in state)
            opacity, screen_y, curve_y = pre_ref[step, 6], pre_ref[step, 4], pre_ref[step, 5]
            colours = (pre_ref[step, 7], pre_ref[step, 8], pre_ref[step, 11])
            for pair in range(GROUP // 2):
                delta_y = (first_v + float(pair)) - screen_y
                bend = curve_y * delta_y * delta_y
                for half in range(2):
                    k = 2 * pair + half
                    power = pre_ref[step, half] + (bend + pre_ref[step, 2 + half] * delta_y)
                    alpha = opacity * jnp.exp2(power)
                    weight = alpha * trans[k]
                    trans[k] = trans[k] - weight
                    red[k] = red[k] + colours[0] * weight
                    green[k] = green[k] + colours[1] * weight
                    blue[k] = blue[k] + colours[2] * weight
                    alpha_ref[index, step, k] = alpha
                    weight_ref[index, step, k] = weight
            return tuple(trans), tuple(red), tuple(green), tuple(blue)

        ones = tuple(jnp.ones((8, 128), F32) for _ in range(GROUP))
        zeros = tuple(jnp.zeros((8, 128), F32) for _ in range(GROUP))
        state = repeat(SEG, STEP_UNROLL, one_step, (ones, zeros, zeros, zeros))
        for k in range(GROUP):
            rows = pl.ds((index * GROUP + k) * 8, 8)
            trans_ref[rows, :] = state[0][k]
            for channel in range(3):
                colour_ref[channel, rows, :] = state[1 + channel][k]

    through = trans_ref[...]
    start = jnp.where(segment == 0, 1.0, pltpu.roll(through, 1, 1))
    for shift in (1, 2, 4, 8):
        start = start * jnp.where(segment >= shift, pltpu.roll(start, shift, 1), 1.0)
    pick = jnp.where(lax.broadcasted_iota(I32, (TILES, 128), 0) == tile, 1.0, 0.0)
    behind = jnp.zeros((256, 128), F32)
    for channel in range(3):
        image = lax.dot_general(
            pick, colour_ref[channel] * start, (((1,), (1,)), ((), ())),
            preferred_element_type=F32, precision=lax.Precision.HIGHEST,
        )
        rendered_ref[channel] = image
        error = (image - target_ref[channel]) * (1.0 / 256.0)
        spread = lax.dot_general(
            error, pick, (((0,), (0,)), ((), ())),
            preferred_element_type=F32, precision=lax.Precision.HIGHEST,
        )
        behind = behind + spread * colour_ref[channel]
        colour_ref[channel] = spread * start
    left = segments - 1 - segment
    factor = jnp.where(left >= 1, pltpu.roll(through, 127, 1), 0.0)
    behind = jnp.where(left >= 1, pltpu.roll(behind, 127, 1), 0.0)
    for shift in (1, 2, 4, 8):
        reach = left >= shift
        behind = behind + factor * jnp.where(reach, pltpu.roll(behind, 128 - shift, 1), 0.0)
        factor = factor * jnp.where(reach, pltpu.roll(factor, 128 - shift, 1), 0.0)
    behind_ref[...] = behind * start

    for index in range(PASSES):
        first_v = index * (GROUP // 2) + 0.5
        rows = [pl.ds((index * GROUP + k) * 8, 8) for k in range(GROUP)]
        errors = [[colour_ref[channel, rows[k], :] for channel in range(3)] for k in range(GROUP)]

        def one_step(count, state):
            step = SEG - 1 - count
            state = list(state)
            screen_y = pre_ref[step, 4]
            colours = (pre_ref[step, 7], pre_ref[step, 8], pre_ref[step, 11])
            sums = [moment_ref[step, row] if index else None for row in range(9)]

            def add(row, value):
                sums[row] = value if sums[row] is None else sums[row] + value

            for pair in range(GROUP // 2):
                delta_y = (first_v + float(pair)) - screen_y
                for half in range(2):
                    k = 2 * pair + half
                    alpha = alpha_ref[index, step, k]
                    weight = weight_ref[index, step, k]
                    shade = (
                        colours[0] * errors[k][0]
                        + colours[1] * errors[k][1]
                        + colours[2] * errors[k][2]
                    )
                    gap = shade - state[k]
                    state[k] = state[k] + alpha * gap
                    slope = weight * gap
                    slope_y = slope * delta_y
                    add(3 * half, slope)
                    add(3 * half + 1, slope_y)
                    add(3 * half + 2, slope_y * delta_y)
                    for channel in range(3):
                        add(6 + channel, weight * errors[k][channel])
            for row in range(9):
                moment_ref[step, row] = sums[row]
            return tuple(state)

        repeat(
            SEG, BACK_UNROLL, one_step, tuple(behind_ref[rows[k], :] for k in range(GROUP))
        )

    def finish(step, carry):
        delta = [pre_ref[step, 9], pre_ref[step, 10]]
        sums = [moment_ref[step, row] for row in range(9)]
        flat = [sums[0], sums[3]]
        tilt = [sums[1], sums[4]]
        bend = [sums[2], sums[5]]
        side = [flat[half] * delta[half] for half in range(2)]

        def total(register):
            return jnp.sum(register, axis=0, keepdims=True)

        m00 = total(flat[0] + flat[1])
        m10 = total(side[0] + side[1])
        m01 = total(tilt[0] + tilt[1])
        m20 = total(side[0] * delta[0] + side[1] * delta[1])
        m11 = total(tilt[0] * delta[0] + tilt[1] * delta[1])
        m02 = total(bend[0] + bend[1])
        attrs = rows_ref[step]
        conic_a, conic_b, conic_c = attrs[2:3], attrs[3:4], attrs[4:5]
        grad_ref[step] = jnp.concatenate(
            [
                conic_a * m10 + conic_b * m01,
                conic_b * m10 + conic_c * m01,
                -0.5 * m20,
                -m11,
                -0.5 * m02,
                m00,
                total(sums[6]),
                total(sums[7]),
            ],
            axis=0,
        )
        ninth_ref[pl.ds(step, 1), :] = total(sums[8])
        return carry

    repeat(SEG, SHORT_UNROLL, finish, 0)
    ninth_ref[SEG:SEG_PAD] = jnp.zeros((SEG_PAD - SEG, 128), F32)
    grad_ninth_ref[...] = ninth_ref[...].reshape(SEG_PAD // 8, 8, 128)
    gather(
        grad_ref, grad_ninth_ref, row_ref, col_ref, back_ref, back_ninth_ref, split_back_ref,
        CAP, SEG, 10, 10,
    )
    pack_messages(back_ref, back_ninth_ref, gradient_ref)


def step_kernel(
    requests_ref, params_ref, count_ref, place_ref, slots_ref, target_ref,
    far_rendered_ref, far_back_ref, far_back_ninth_ref, far_owner_row_ref, far_owner_col_ref,
    rendered_ref, back_ref, back_ninth_ref, owner_row_ref, owner_col_ref, store_sem,
    here_requests_ref, here_params_ref, here_count_ref, here_place_ref, here_slots_ref,
    here_target_ref, load_sem,
    request_ref, wanted_ref, wanted_block_ref, wanted_lane_ref, request_send, request_receive,
    request_own,
    screen_ref, ninth_ref, out_ref, out_ninth_ref, split_ref, left_ref, right_ref,
    all_ref, slot_left_ref, slot_right_ref, block_ref, lane_ref, row_ref, col_ref, lanes_ref,
    message_ref, landing_ref, send_sem, receive_sem, own_sem, source_ref, source_ninth_ref,
    reply_ref, reply_landing_ref, reply_send, reply_receive, reply_own,
    *render_refs,
):
    me = lax.axis_index("dev")
    loads = [
        pltpu.make_async_copy(far, near, load_sem.at[index])
        for index, (far, near) in enumerate(
            (
                (requests_ref, here_requests_ref),
                (params_ref, here_params_ref),
                (count_ref, here_count_ref),
                (place_ref, here_place_ref),
                (slots_ref, here_slots_ref),
                (target_ref, here_target_ref),
            )
        )
    ]
    for load in loads:
        load.start()
    greet(me)
    loads[0].wait()
    wide = jnp.concatenate(
        [here_requests_ref[...].astype(F32), jnp.zeros((128 - CAP, DEVICES), F32)], axis=0
    )
    request_ref[:, 0, :] = wide.T.astype(I32)
    await_greetings()
    request_sems = (request_send, request_receive, request_own, me)
    send_all(request_ref, wanted_ref, *request_sems)
    for load in loads[1:]:
        load.wait()
    project_all(here_params_ref, screen_ref, ninth_ref)
    index_tables(
        here_count_ref, here_place_ref, here_slots_ref,
        block_ref, lane_ref, row_ref, col_ref, lanes_ref, all_ref, slot_left_ref, slot_right_ref,
    )
    await_all(request_ref, wanted_ref, *request_sems)
    wanted_tables(wanted_ref, wanted_block_ref, wanted_lane_ref)
    gather(
        screen_ref, ninth_ref, wanted_block_ref, wanted_lane_ref, out_ref, out_ninth_ref,
        split_ref, CAP, BLOCKS, 10, 10,
    )
    pack_messages(out_ref, out_ninth_ref, message_ref)
    sems = (send_sem, receive_sem, own_sem, me)
    send_all(message_ref, landing_ref, *sems)
    invert(
        wanted_block_ref, wanted_lane_ref, left_ref, right_ref, owner_row_ref, owner_col_ref,
        CAP, BLOCKS,
    )
    await_all(message_ref, landing_ref, *sems)
    unpack_messages(landing_ref, source_ref, source_ninth_ref)
    render(
        source_ref, source_ninth_ref, block_ref, lane_ref, row_ref, col_ref, lanes_ref,
        here_target_ref, rendered_ref, reply_ref, *render_refs,
    )
    reply_sems = (reply_send, reply_receive, reply_own, me)
    send_all(reply_ref, reply_landing_ref, *reply_sems)
    stores = [
        pltpu.make_async_copy(near, far, store_sem.at[index])
        for index, (near, far) in enumerate(
            (
                (rendered_ref, far_rendered_ref),
                (owner_row_ref, far_owner_row_ref),
                (owner_col_ref, far_owner_col_ref),
                (back_ref, far_back_ref),
                (back_ninth_ref, far_back_ninth_ref),
            )
        )
    ]
    for store in stores[:3]:
        store.start()
    await_all(reply_ref, reply_landing_ref, *reply_sems)
    unpack_messages(reply_landing_ref, back_ref, back_ninth_ref)
    for store in stores[3:]:
        store.start()
    for store in stores:
        store.wait()


def pullback_kernel(
    far_source_ref, far_ninth_ref, far_row_ref, far_col_ref, image_ref, params_ref,
    rendered_ref, gradient_ref,
    source_ref, source_ninth_ref, row_ref, col_ref,
    rows_ref, ninth_ref, split_ref, here_params_ref, here_gradient_ref, load_sem, store_sem,
):
    loads = [
        pltpu.make_async_copy(far, near, load_sem.at[index])
        for index, (far, near) in enumerate(
            (
                (far_source_ref, source_ref),
                (far_ninth_ref, source_ninth_ref),
                (far_row_ref, row_ref),
                (far_col_ref, col_ref),
                (params_ref, here_params_ref),
                (image_ref, rendered_ref),
            )
        )
    ]
    for load in loads:
        load.start()
    for load in loads[:4]:
        load.wait()
    gather(
        source_ref, source_ninth_ref, row_ref, col_ref, rows_ref, ninth_ref, split_ref,
        BLOCKS, CAP, 10, 10,
    )
    loads[4].wait()
    stores = []
    for group in range(OWNED // 1024):
        columns = pl.ds(group * 1024, 1024)
        eight = pl.ds(group * 8, 8)
        rows = load_rows(here_params_ref, columns)
        screen_grad = [rows_ref[eight, row, :] for row in range(8)] + [ninth_ref[eight, :]]
        screen, pullback = jax.vjp(project, rows)
        by_logit = screen_grad[5] * (1.0 / (1.0 + jnp.exp(rows[10])))
        screen_grad[5] = jnp.zeros_like(by_logit)
        (grads,) = pullback(screen_grad)
        grads[10] = by_logit
        for row in range(PARAMS):
            here_gradient_ref[row : row + 1, columns] = grads[row].reshape(1, 1024)
        stores.append(
            pltpu.make_async_copy(
                here_gradient_ref.at[:, columns], gradient_ref.at[:, columns], store_sem.at[group]
            )
        )
        stores[-1].start()
    for store in stores:
        store.wait()
    loads[5].wait()


def shape(dims, dtype=F32):
    return jax.ShapeDtypeStruct(dims, dtype)


def call(kernel, outs, specs, out_specs, scratch, name, collective=None):
    params = {"vmem_limit_bytes": VMEM_LIMIT}
    if collective is not None:
        params.update(collective_id=collective, has_side_effects=True)
    spaces = {"v": pltpu.VMEM, "s": pltpu.SMEM, "h": pltpu.HBM}
    return pl.pallas_call(
        kernel,
        out_shape=outs,
        in_specs=[pl.BlockSpec(memory_space=spaces[kind]) for kind in specs],
        out_specs=[pl.BlockSpec(memory_space=spaces[kind]) for kind in out_specs],
        scratch_shapes=scratch,
        compiler_params=pltpu.CompilerParams(**params),
        name=name,
    )


SPLIT = (3 * (CAP // 2 * 8 + 24), 256)
SPLIT_BACK = (3 * (SEG // 2 * 8 + 24), 256)
MESSAGE = (DEVICES, 3, 128)
REQUEST = (DEVICES, 1, 128)
TABLE = (CAP, 128)
STEPS = (SEG_PAD, 128)
EIGHT = (CAP, 8, 128)
NINE = (CAP // 8, 8, 128)


IMAGE = (3, TILES, 256)


def local(params, requests, tile_slots, tile_count, tile_place, target):
    vmem = pltpu.VMEM
    sems = [pltpu.SemaphoreType.DMA] * 3
    image, back, back_ninth, owner_row, owner_col = call(
        step_kernel,
        [shape(IMAGE), shape(EIGHT), shape(NINE), shape(TABLE, I32), shape(TABLE, I32)],
        "hhhhhh",
        "hhhhh",
        [
            vmem(IMAGE, F32), vmem(EIGHT, F32), vmem(NINE, F32), vmem(TABLE, I32),
            vmem(TABLE, I32), pltpu.SemaphoreType.DMA((5,)),
            vmem((CAP, DEVICES), I32), vmem((PARAMS, OWNED), F32),
            pltpu.SMEM((TILES,), I32), pltpu.SMEM((TILES,), I32), vmem((TILES, SLOTS), I32),
            vmem(IMAGE, F32), pltpu.SemaphoreType.DMA((6,)),
            vmem(REQUEST, I32), vmem(REQUEST, I32), vmem(TABLE, I32), vmem(TABLE, I32), *sems,
            vmem(EIGHT, F32), vmem(NINE, F32), vmem(EIGHT, F32), vmem(TABLE, F32),
            vmem(SPLIT, BF16),
            vmem((2 * BLOCKS, CAP * 128), BF16), vmem((128, CAP * 128), BF16),
            vmem((SEGS * SEG + 8, 128), F32),
            vmem((2 * CAP, SEG * 128), BF16), vmem((128, SEG * 128), BF16),
            vmem(STEPS, I32), vmem(STEPS, I32), vmem(TABLE, I32), vmem(TABLE, I32),
            vmem((8, 128), I32),
            vmem(MESSAGE, F32), vmem(MESSAGE, F32), *sems, vmem(EIGHT, F32), vmem(NINE, F32),
            vmem(MESSAGE, F32), vmem(MESSAGE, F32), *sems,
            vmem((SEG, 8, 128), F32), vmem(STEPS, F32),
            vmem((SEG, 12, 8, 128), F32),
            vmem((PASSES, SEG, GROUP, 8, 128), F32), vmem((PASSES, SEG, GROUP, 8, 128), F32),
            vmem((256, 128), F32), vmem((3, 256, 128), F32), vmem((256, 128), F32),
            vmem((SEG, 9, 8, 128), F32),
            vmem((SEG, 8, 128), F32), vmem((SEG_PAD // 8, 8, 128), F32),
            vmem(EIGHT, F32), vmem(TABLE, F32), vmem(SPLIT, BF16), vmem(SPLIT_BACK, BF16),
        ],
        "step",
        0,
    )(
        requests.reshape(DEVICES, CAP).T, params, tile_count, tile_place, tile_slots,
        target.transpose(1, 0, 2),
    )
    rendered, gradient = call(
        pullback_kernel,
        [shape(IMAGE), shape((PARAMS, OWNED))],
        "hhhhhh",
        "hh",
        [
            vmem(EIGHT, F32), vmem(NINE, F32), vmem(TABLE, I32), vmem(TABLE, I32),
            vmem(EIGHT, F32), vmem(TABLE, F32), vmem(SPLIT, BF16), vmem((PARAMS, OWNED), F32),
            vmem((PARAMS, OWNED), F32), pltpu.SemaphoreType.DMA((6,)),
            pltpu.SemaphoreType.DMA((OWNED // 1024,)),
        ],
        "pullback",
    )(back, back_ninth, owner_row, owner_col, image, params)
    return rendered.transpose(1, 0, 2), gradient


def solution(mesh):
    in_specs = (
        P(None, "dev"),
        P("dev", None, None),
        P("dev", None),
        P("dev"),
        P("dev"),
        P("dev", None, None),
    )
    out_specs = (P("dev", None, None), P(None, "dev"))
    return jax.shard_map(local, mesh=mesh, in_specs=in_specs, out_specs=out_specs, check_vma=False)
```

```python
import functools

import jax
import jax.numpy as jnp
from jax import lax
from jax.experimental import pallas as pl
from jax.experimental.pallas import tpu as pltpu
from jax.sharding import PartitionSpec as P

FOCAL = 1200.0
CENTER_X = 960.0
CENTER_Y = 540.0
DILATION = 0.3
BAND_ZERO = 0.28209479177387814
BAND_ONE = 0.4886025119029199
BAND_TWO = (
    1.0925484305920792,
    -1.0925484305920792,
    0.31539156525252005,
    -1.0925484305920792,
    0.5462742152960396,
)
BAND_THREE = (
    -0.5900435899266435,
    2.890611442640554,
    -0.4570457994644658,
    0.3731763325901154,
    -0.4570457994644658,
    1.445305721320277,
    -0.5900435899266435,
)
LOG2_E = 1.4426950408889634

DEVICES = 128
INNER = 8
OUTER = DEVICES // INNER
OWNED = 5120
CAP = 40
PARAMS = 59
BLOCKS = OWNED // 128
TILES = 16
SLOTS = 512
SEG = 46
SEG_PAD = 48
SEGS = 12
GROUP = 8
PASSES = 32 // GROUP
STEP_UNROLL = 23
BACK_UNROLL = 2
SHORT_UNROLL = 23
BF16 = jnp.bfloat16
MESH_ID = pl.DeviceIdType.MESH
F32 = jnp.float32
I32 = jnp.int32
VMEM_LIMIT = 64 * 1000 * 1000


def project(rows):
    x, y, z = rows[0], rows[1], rows[2]
    scales = [jnp.exp(rows[3 + k]) for k in range(3)]
    norm = jnp.sqrt(rows[6] * rows[6] + rows[7] * rows[7] + rows[8] * rows[8] + rows[9] * rows[9])
    qw, qx, qy, qz = (rows[6 + k] / norm for k in range(4))
    rotation = [
        [1.0 - 2.0 * (qy * qy + qz * qz), 2.0 * (qx * qy - qw * qz), 2.0 * (qx * qz + qw * qy)],
        [2.0 * (qx * qy + qw * qz), 1.0 - 2.0 * (qx * qx + qz * qz), 2.0 * (qy * qz - qw * qx)],
        [2.0 * (qx * qz - qw * qy), 2.0 * (qy * qz + qw * qx), 1.0 - 2.0 * (qx * qx + qy * qy)],
    ]
    spread = [[rotation[i][k] * scales[k] for k in range(3)] for i in range(3)]
    inverse_z = 1.0 / z
    diag = FOCAL * inverse_z
    jac_xz = -FOCAL * x * inverse_z * inverse_z
    jac_yz = -FOCAL * y * inverse_z * inverse_z
    across = [diag * spread[0][k] + jac_xz * spread[2][k] for k in range(3)]
    upward = [diag * spread[1][k] + jac_yz * spread[2][k] for k in range(3)]
    cov_xx = across[0] * across[0] + across[1] * across[1] + across[2] * across[2] + DILATION
    cov_xy = across[0] * upward[0] + across[1] * upward[1] + across[2] * upward[2]
    cov_yy = upward[0] * upward[0] + upward[1] * upward[1] + upward[2] * upward[2] + DILATION
    determinant = cov_xx * cov_yy - cov_xy * cov_xy
    distance = jnp.sqrt(x * x + y * y + z * z)
    fx, fy, fz = x / distance, y / distance, z / distance
    xx, yy, zz = fx * fx, fy * fy, fz * fz
    basis = [
        None,
        -BAND_ONE * fy,
        BAND_ONE * fz,
        -BAND_ONE * fx,
        BAND_TWO[0] * fx * fy,
        BAND_TWO[1] * fy * fz,
        BAND_TWO[2] * (2.0 * zz - xx - yy),
        BAND_TWO[3] * fx * fz,
        BAND_TWO[4] * (xx - yy),
        BAND_THREE[0] * fy * (3.0 * xx - yy),
        BAND_THREE[1] * fx * fy * fz,
        BAND_THREE[2] * fy * (4.0 * zz - xx - yy),
        BAND_THREE[3] * fz * (2.0 * zz - 3.0 * xx - 3.0 * yy),
        BAND_THREE[4] * fx * (4.0 * zz - xx - yy),
        BAND_THREE[5] * fz * (xx - yy),
        BAND_THREE[6] * fx * (xx - 3.0 * yy),
    ]
    colours = []
    for channel in range(3):
        total = BAND_ZERO * rows[11 + channel]
        for k in range(1, 16):
            total = total + basis[k] * rows[11 + 3 * k + channel]
        colours.append(jnp.maximum(total + 0.5, 0.0))
    return [
        FOCAL * x * inverse_z + CENTER_X,
        FOCAL * y * inverse_z + CENTER_Y,
        cov_yy / determinant,
        -cov_xy / determinant,
        cov_xx / determinant,
        1.0 / (1.0 + jnp.exp(-rows[10])),
        *colours,
    ]


def load_rows(params_ref, columns):
    return [params_ref[row : row + 1, columns].reshape(8, 128) for row in range(PARAMS)]


def project_all(params_ref, screen_ref, ninth_ref):
    def one_group(group, carry):
        screen = project(
            load_rows(params_ref, pl.ds(pl.multiple_of(group * 1024, 1024), 1024))
        )
        for row in range(8):
            screen_ref[pl.ds(pl.multiple_of(group * 8, 8), 8), row, :] = screen[row]
        ninth_ref[group] = screen[8]
        return carry

    lax.fori_loop(0, OWNED // 1024, one_group, 0)


def repeat(count, unroll, body, state):
    def turn(index, state):
        for part in range(unroll):
            state = body(index * unroll + part, state)
        return state

    return lax.fori_loop(0, count // unroll, turn, state)


def gather(
    source_ref, ninth_ref, block_ref, lane_ref, out_ref, out_ninth_ref, split_ref,
    targets, sources, by_matmul, by_lanes,
):
    half = sources // 2
    eights = half * 8
    height = eights + 24
    width = 128 * by_matmul
    ninth = ninth_ref[...].reshape(-1, 128)
    rest = jnp.concatenate(
        [
            jnp.concatenate([ninth[0:half], ninth[half:sources]], axis=1),
            jnp.zeros((24 - half, 256), F32),
        ],
        axis=0,
    )
    main = jnp.concatenate(
        [
            source_ref[0:half].reshape(eights, 128),
            source_ref[half:sources].reshape(eights, 128),
        ],
        axis=1,
    )
    for part in range(3):
        for values, start in ((main, 0), (rest, eights)):
            rounded = values.astype(BF16)
            split_ref[part * height + start : part * height + start + values.shape[0]] = rounded
        main = main - main.astype(BF16).astype(F32)
        rest = rest - rest.astype(BF16).astype(F32)
    iota = lax.broadcasted_iota(I32, (256, width), 0).astype(F32).astype(BF16)
    sublane_rest = lax.broadcasted_iota(I32, (24, width), 0)
    sublane = lax.broadcasted_iota(I32, (8, 128), 0)

    def turn(index, carry):
        base = index * (by_matmul + by_lanes)
        rows = [pl.ds(base + k, 1) for k in range(by_matmul)]
        block = jnp.concatenate([block_ref[row, :] for row in rows], axis=1)
        lane = jnp.concatenate([lane_ref[row, :] for row in rows], axis=1)
        upper = jnp.where(block >= half, 1, 0)
        key = jnp.broadcast_to((lane + 128 * upper).astype(F32), (16, width)).astype(BF16)
        place = block - half * upper
        match = jnp.concatenate([key] * 16, axis=0) == iota
        pick = jnp.where(match, jnp.ones((), BF16), jnp.zeros((), BF16))
        parts = lax.dot_general(
            split_ref[...], pick, (((1,), (0,)), ((), ())), preferred_element_type=F32
        )
        for k in range(by_lanes):
            row = base + by_matmul + k
            lane = jnp.broadcast_to(lane_ref[pl.ds(row, 1), :], (8, 128))
            block = jnp.broadcast_to(block_ref[pl.ds(row, 1), :], (8, 128))
            total = jnp.zeros((8, 128), F32)
            for source in range(sources):
                picked = jnp.take_along_axis(
                    source_ref[source], lane, axis=1, mode="promise_in_bounds"
                )
                total = jnp.where(block == source, picked, total)
            out_ref[row] = total
            offset = block - sublane
            total = jnp.zeros((8, 128), F32)
            for source in range((sources + 7) // 8):
                picked = jnp.take_along_axis(
                    ninth_ref[source], lane, axis=1, mode="promise_in_bounds"
                )
                total = jnp.where(offset == 8 * source, picked, total)
            out_ninth_ref[pl.ds(row, 1), :] = jnp.sum(total, axis=0, keepdims=True)
        values = (parts[0:height] + parts[height : 2 * height]) + parts[2 * height : 3 * height]
        wide = jnp.broadcast_to(place, (8, width))
        total = jnp.zeros((8, width), F32)
        for source in range(half):
            total = jnp.where(wide == source, values[8 * source : 8 * source + 8], total)
        last = jnp.sum(
            jnp.where(sublane_rest == place, values[eights:height], 0.0), axis=0, keepdims=True
        )
        for k in range(by_matmul):
            out_ref[base + k] = total[:, 128 * k : 128 * k + 128]
            out_ninth_ref[pl.ds(base + k, 1), :] = last[:, 128 * k : 128 * k + 128]
        return carry

    lax.fori_loop(0, targets // (by_matmul + by_lanes), turn, 0)


def invert(block_ref, lane_ref, left_ref, right_ref, row_ref, col_ref, rows, blocks):
    iota_lane = lax.broadcasted_iota(I32, (1, 128), 1).astype(F32)
    iota_block = lax.broadcasted_iota(I32, (blocks, 128), 0)
    iota_sub = lax.broadcasted_iota(I32, (128, 128), 0)

    def one_row(row, carry):
        columns = pl.ds(pl.multiple_of(row * 128, 128), 128)
        here = iota_block == block_ref[pl.ds(row, 1), :]
        value = jnp.full((1, 128), 0.0, F32) + row.astype(F32)
        left_ref[0:blocks, columns] = jnp.where(here, value, 0.0).astype(BF16)
        left_ref[blocks : 2 * blocks, columns] = jnp.where(here, iota_lane, 0.0).astype(
            BF16
        )
        right_ref[:, columns] = jnp.where(
            iota_sub == lane_ref[pl.ds(row, 1), :], 1.0, 0.0
        ).astype(BF16)
        return carry

    repeat(rows, 2, one_row, 0)
    found = lax.dot_general(
        left_ref[...], right_ref[...], (((1,), (1,)), ((), ())), preferred_element_type=F32
    )
    row_ref[...] = (found[0:blocks] + 0.5).astype(I32)
    col_ref[...] = (found[blocks : 2 * blocks] + 0.5).astype(I32)


def pack_messages(rows_ref, ninth_ref, out_ref):
    flat = rows_ref[...].reshape(CAP * 8, 128)
    out_ref[:, 0, :] = flat[0:128].T
    out_ref[:, 1, :] = flat[128:256].T
    last = jnp.concatenate(
        [flat[256:320], ninth_ref[...], jnp.zeros((128 - 64 - CAP, 128), F32)], axis=0
    )
    out_ref[:, 2, :] = last.T


def unpack_messages(message_ref, rows_ref, ninth_ref):
    rows_ref[0:16] = message_ref[:, 0, :].T.reshape(16, 8, 128)
    rows_ref[16:32] = message_ref[:, 1, :].T.reshape(16, 8, 128)
    last = message_ref[:, 2, :].T
    rows_ref[32:40] = last[0:64].reshape(8, 8, 128)
    ninth_ref[...] = last[64 : 64 + CAP].reshape(CAP // 8, 8, 128)


def request_peers(me):
    outer, inner = lax.div(me, INNER), lax.rem(me, INNER)
    near = [outer * INNER + lax.rem(inner + turn, INNER) for turn in range(1, INNER)]
    far = [lax.rem(outer + turn, OUTER) * INNER + inner for turn in range(1, OUTER)]
    return outer, inner, near, far


def greet(me):
    barrier = pltpu.get_barrier_semaphore()
    _, _, near, far = request_peers(me)
    for peer in near + far:
        pl.semaphore_signal(barrier, inc=1, device_id=(peer,), device_id_type=MESH_ID)


def await_greetings():
    pl.semaphore_wait(pltpu.get_barrier_semaphore(), INNER + OUTER - 2)


def send_requests(request_ref, middle_ref, sems, me):
    send_sem, receive_sem, own_sem = sems
    _, inner, near, _ = request_peers(me)
    for peer in near:
        pltpu.make_async_remote_copy(
            src_ref=request_ref.at[lax.rem(peer, INNER)],
            dst_ref=middle_ref.at[inner],
            send_sem=send_sem,
            recv_sem=receive_sem,
            device_id=(peer,),
            device_id_type=MESH_ID,
        ).start()
    pltpu.make_async_copy(request_ref.at[inner], middle_ref.at[inner], own_sem).start()


def forward_requests(request_ref, middle_ref, wanted_ref, first_sems, sems, me):
    first_send, first_receive, first_own = first_sems
    send_sem, receive_sem, own_sem = sems
    outer, inner, _, far = request_peers(me)
    others = pl.ds(0, INNER - 1)
    pltpu.make_async_copy(request_ref.at[inner], middle_ref.at[inner], first_own).wait()
    pltpu.make_async_copy(middle_ref.at[others], middle_ref.at[others], first_receive).wait()
    for peer in far:
        pltpu.make_async_remote_copy(
            src_ref=middle_ref.at[:, lax.div(peer, INNER)],
            dst_ref=wanted_ref.at[outer],
            send_sem=send_sem,
            recv_sem=receive_sem,
            device_id=(peer,),
            device_id_type=MESH_ID,
        ).start()
    pltpu.make_async_copy(middle_ref.at[:, outer], wanted_ref.at[outer], own_sem).start()
    pltpu.make_async_copy(request_ref.at[others], request_ref.at[others], first_send).wait()


def await_requests(middle_ref, wanted_ref, sems, me):
    send_sem, receive_sem, own_sem = sems
    outer = lax.div(me, INNER)
    others = pl.ds(0, OUTER - 1)
    pltpu.make_async_copy(middle_ref.at[:, outer], wanted_ref.at[outer], own_sem).wait()
    pltpu.make_async_copy(wanted_ref.at[others], wanted_ref.at[others], receive_sem).wait()
    pltpu.make_async_copy(wanted_ref.at[others], wanted_ref.at[others], send_sem).wait()


def send_all(source_ref, landing_ref, send_sem, receive_sem, own_sem, me):
    def one(turn, carry):
        peer = lax.rem(me + turn, DEVICES)
        pltpu.make_async_remote_copy(
            src_ref=source_ref.at[peer],
            dst_ref=landing_ref.at[me],
            send_sem=send_sem,
            recv_sem=receive_sem,
            device_id=(peer,),
            device_id_type=MESH_ID,
        ).start()
        return carry

    lax.fori_loop(1, DEVICES, one, 0)
    pltpu.make_async_copy(source_ref.at[me], landing_ref.at[me], own_sem).start()


def await_all(source_ref, landing_ref, send_sem, receive_sem, own_sem, me):
    others = pl.ds(0, DEVICES - 1)
    pltpu.make_async_copy(source_ref.at[me], landing_ref.at[me], own_sem).wait()
    pltpu.make_async_copy(landing_ref.at[others], landing_ref.at[others], receive_sem).wait()
    pltpu.make_async_copy(source_ref.at[others], source_ref.at[others], send_sem).wait()


def wanted_tables(wanted_ref, block_ref, lane_ref):
    wanted = wanted_ref[:, :, 0, :].reshape(DEVICES, 128).astype(F32).T[0:CAP].astype(I32)
    block_ref[...] = wanted >> 7
    lane_ref[...] = wanted & 127


def lane_map(count_ref, place_ref):
    lane = lax.broadcasted_iota(I32, (1, 128), 1)
    tile = jnp.full((1, 128), -1, I32)
    segment = jnp.zeros((1, 128), I32)
    segments = jnp.zeros((1, 128), I32)
    count = jnp.zeros((1, 128), I32)
    origin_x = jnp.zeros((1, 128), I32)
    origin_y = jnp.zeros((1, 128), I32)
    base = jnp.int32(0)
    for index in range(TILES):
        listed = count_ref[index]
        place = place_ref[index]
        used = lax.div(listed + (SEG - 1), SEG)
        inside = (lane >= base) & (lane < base + used)
        place_y = lax.div(place, 120)
        tile = jnp.where(inside, index, tile)
        segment = jnp.where(inside, lane - base, segment)
        segments = jnp.where(inside, used, segments)
        count = jnp.where(inside, listed, count)
        origin_x = jnp.where(inside, 16 * (place - 120 * place_y), origin_x)
        origin_y = jnp.where(inside, 16 * place_y, origin_y)
        base = base + used
    return tile, segment, segments, count, origin_x, origin_y


def index_tables(
    count_ref, place_ref, slots_ref,
    block_ref, lane_ref, row_ref, col_ref, lanes_ref, all_ref, left_ref, right_ref,
):
    tile, segment, segments, count, origin_x, origin_y = lane_map(count_ref, place_ref)
    lanes_ref[0:1] = tile
    lanes_ref[1:2] = segment
    lanes_ref[2:3] = segments
    lanes_ref[3:4] = count
    lanes_ref[4:5] = origin_x
    lanes_ref[5:6] = origin_y
    lanes_ref[6:8] = jnp.zeros((2, 128), I32)
    slots = slots_ref[...]
    owner = ((slots.astype(F32) + 0.5) * (1.0 / CAP)).astype(I32)
    within = slots - owner * CAP
    pick = jnp.where(
        lax.broadcasted_iota(I32, (TILES, 128), 0) == tile, 1.0, 0.0
    ).astype(BF16)
    contract = (((0,), (0,)), ((), ()))
    step = lax.broadcasted_iota(I32, (SEG_PAD, 128), 0)
    live = (step < SEG) & (step + segment * SEG < count)
    for values, out, unused in ((within, block_ref, -1), (owner, lane_ref, 0)):
        all_ref[0:SLOTS] = lax.dot_general(
            values.astype(F32).astype(BF16), pick, contract, preferred_element_type=F32
        )
        all_ref[SLOTS:] = jnp.zeros_like(all_ref[SLOTS:])
        total = jnp.zeros((SEG_PAD, 128), F32)
        for part in range(SEGS):
            rows = all_ref[part * SEG : part * SEG + SEG_PAD]
            total = jnp.where(segment == part, rows, total)
        out[...] = jnp.where(live, (total + 0.5).astype(I32), unused)
    invert(block_ref, lane_ref, left_ref, right_ref, row_ref, col_ref, SEG, CAP)


def render(
    source_ref, source_ninth_ref, block_ref, lane_ref, row_ref, col_ref, lanes_ref, target_ref,
    rendered_ref, gradient_ref,
    rows_ref, ninth_ref, pre_ref, alpha_ref, weight_ref,
    trans_ref, colour_ref, behind_ref, moment_ref, grad_ref, grad_ninth_ref,
    back_ref, back_ninth_ref, split_ref, split_back_ref,
):
    gather(
        source_ref, source_ninth_ref, block_ref, lane_ref, rows_ref, ninth_ref, split_ref,
        SEG, CAP, 12, 11,
    )
    tile = lanes_ref[0:1]
    segment = lanes_ref[1:2]
    segments = lanes_ref[2:3]
    origin_x = lanes_ref[4:5].astype(F32)
    origin_y = lanes_ref[5:6].astype(F32)
    sub = lax.broadcasted_iota(I32, (8, 128), 0).astype(F32) + 0.5

    def wide(row):
        return jnp.broadcast_to(row, (8, 128))

    def prepare(step, carry):
        attrs = rows_ref[step]
        screen_x = attrs[0:1] - origin_x
        screen_y = attrs[1:2] - origin_y
        curve_x = wide(-0.5 * LOG2_E * attrs[2:3])
        curve_xy = wide(-LOG2_E * attrs[3:4])
        for half in range(2):
            delta = (sub + 8.0 * half) - wide(screen_x)
            pre_ref[step, half] = curve_x * delta * delta
            pre_ref[step, 2 + half] = curve_xy * delta
            pre_ref[step, 9 + half] = delta
        pre_ref[step, 4] = wide(screen_y)
        pre_ref[step, 5] = wide(-0.5 * LOG2_E * attrs[4:5])
        pre_ref[step, 6] = wide(attrs[5:6])
        pre_ref[step, 7] = wide(attrs[6:7])
        pre_ref[step, 8] = wide(attrs[7:8])
        pre_ref[step, 11] = wide(ninth_ref[pl.ds(step, 1), :])
        return carry

    repeat(SEG, SHORT_UNROLL, prepare, 0)

    for index in range(PASSES):
        first_v = index * (GROUP // 2) + 0.5

        def one_step(step, state):
            trans, red, green, blue = (list(part) for part in state)
            opacity, screen_y, curve_y = pre_ref[step, 6], pre_ref[step, 4], pre_ref[step, 5]
            colours = (pre_ref[step, 7], pre_ref[step, 8], pre_ref[step, 11])
            for pair in range(GROUP // 2):
                delta_y = (first_v + float(pair)) - screen_y
                bend = curve_y * delta_y * delta_y
                for half in range(2):
                    k = 2 * pair + half
                    power = pre_ref[step, half] + (bend + pre_ref[step, 2 + half] * delta_y)
                    alpha = opacity * jnp.exp2(power)
                    weight = alpha * trans[k]
                    trans[k] = trans[k] - weight
                    red[k] = red[k] + colours[0] * weight
                    green[k] = green[k] + colours[1] * weight
                    blue[k] = blue[k] + colours[2] * weight
                    alpha_ref[index, step, k] = alpha
                    weight_ref[index, step, k] = weight
            return tuple(trans), tuple(red), tuple(green), tuple(blue)

        ones = tuple(jnp.ones((8, 128), F32) for _ in range(GROUP))
        zeros = tuple(jnp.zeros((8, 128), F32) for _ in range(GROUP))
        state = repeat(SEG, STEP_UNROLL, one_step, (ones, zeros, zeros, zeros))
        for k in range(GROUP):
            rows = pl.ds((index * GROUP + k) * 8, 8)
            trans_ref[rows, :] = state[0][k]
            for channel in range(3):
                colour_ref[channel, rows, :] = state[1 + channel][k]

    through = trans_ref[...]
    start = jnp.where(segment == 0, 1.0, pltpu.roll(through, 1, 1))
    for shift in (1, 2, 4, 8):
        start = start * jnp.where(segment >= shift, pltpu.roll(start, shift, 1), 1.0)
    pick = jnp.where(lax.broadcasted_iota(I32, (TILES, 128), 0) == tile, 1.0, 0.0)
    behind = jnp.zeros((256, 128), F32)
    for channel in range(3):
        image = lax.dot_general(
            pick, colour_ref[channel] * start, (((1,), (1,)), ((), ())),
            preferred_element_type=F32, precision=lax.Precision.HIGHEST,
        )
        rendered_ref[channel] = image
        error = (image - target_ref[channel]) * (1.0 / 256.0)
        spread = lax.dot_general(
            error, pick, (((0,), (0,)), ((), ())),
            preferred_element_type=F32, precision=lax.Precision.HIGHEST,
        )
        behind = behind + spread * colour_ref[channel]
        colour_ref[channel] = spread * start
    left = segments - 1 - segment
    factor = jnp.where(left >= 1, pltpu.roll(through, 127, 1), 0.0)
    behind = jnp.where(left >= 1, pltpu.roll(behind, 127, 1), 0.0)
    for shift in (1, 2, 4, 8):
        reach = left >= shift
        behind = behind + factor * jnp.where(reach, pltpu.roll(behind, 128 - shift, 1), 0.0)
        factor = factor * jnp.where(reach, pltpu.roll(factor, 128 - shift, 1), 0.0)
    behind_ref[...] = behind * start

    for index in range(PASSES):
        first_v = index * (GROUP // 2) + 0.5
        rows = [pl.ds((index * GROUP + k) * 8, 8) for k in range(GROUP)]
        errors = [[colour_ref[channel, rows[k], :] for channel in range(3)] for k in range(GROUP)]

        def one_step(count, state):
            step = SEG - 1 - count
            state = list(state)
            screen_y = pre_ref[step, 4]
            colours = (pre_ref[step, 7], pre_ref[step, 8], pre_ref[step, 11])
            sums = [moment_ref[step, row] if index else None for row in range(9)]

            def add(row, value):
                sums[row] = value if sums[row] is None else sums[row] + value

            for pair in range(GROUP // 2):
                delta_y = (first_v + float(pair)) - screen_y
                for half in range(2):
                    k = 2 * pair + half
                    alpha = alpha_ref[index, step, k]
                    weight = weight_ref[index, step, k]
                    shade = (
                        colours[0] * errors[k][0]
                        + colours[1] * errors[k][1]
                        + colours[2] * errors[k][2]
                    )
                    gap = shade - state[k]
                    state[k] = state[k] + alpha * gap
                    slope = weight * gap
                    slope_y = slope * delta_y
                    add(3 * half, slope)
                    add(3 * half + 1, slope_y)
                    add(3 * half + 2, slope_y * delta_y)
                    for channel in range(3):
                        add(6 + channel, weight * errors[k][channel])
            for row in range(9):
                moment_ref[step, row] = sums[row]
            return tuple(state)

        repeat(
            SEG, BACK_UNROLL, one_step, tuple(behind_ref[rows[k], :] for k in range(GROUP))
        )

    def finish(step, carry):
        delta = [pre_ref[step, 9], pre_ref[step, 10]]
        sums = [moment_ref[step, row] for row in range(9)]
        flat = [sums[0], sums[3]]
        tilt = [sums[1], sums[4]]
        bend = [sums[2], sums[5]]
        side = [flat[half] * delta[half] for half in range(2)]

        def total(register):
            return jnp.sum(register, axis=0, keepdims=True)

        m00 = total(flat[0] + flat[1])
        m10 = total(side[0] + side[1])
        m01 = total(tilt[0] + tilt[1])
        m20 = total(side[0] * delta[0] + side[1] * delta[1])
        m11 = total(tilt[0] * delta[0] + tilt[1] * delta[1])
        m02 = total(bend[0] + bend[1])
        attrs = rows_ref[step]
        conic_a, conic_b, conic_c = attrs[2:3], attrs[3:4], attrs[4:5]
        grad_ref[step] = jnp.concatenate(
            [
                conic_a * m10 + conic_b * m01,
                conic_b * m10 + conic_c * m01,
                -0.5 * m20,
                -m11,
                -0.5 * m02,
                m00,
                total(sums[6]),
                total(sums[7]),
            ],
            axis=0,
        )
        ninth_ref[pl.ds(step, 1), :] = total(sums[8])
        return carry

    repeat(SEG, SHORT_UNROLL, finish, 0)
    ninth_ref[SEG:SEG_PAD] = jnp.zeros((SEG_PAD - SEG, 128), F32)
    grad_ninth_ref[...] = ninth_ref[...].reshape(SEG_PAD // 8, 8, 128)
    gather(
        grad_ref, grad_ninth_ref, row_ref, col_ref, back_ref, back_ninth_ref, split_back_ref,
        CAP, SEG, 10, 10,
    )
    pack_messages(back_ref, back_ninth_ref, gradient_ref)


def step_kernel(
    requests_ref, params_ref, count_ref, place_ref, slots_ref, target_ref,
    far_rendered_ref, far_back_ref, far_back_ninth_ref, far_owner_row_ref, far_owner_col_ref,
    rendered_ref, back_ref, back_ninth_ref, owner_row_ref, owner_col_ref, store_sem,
    here_requests_ref, here_params_ref, here_count_ref, here_place_ref, here_slots_ref,
    here_target_ref, load_sem,
    request_ref, middle_ref, wanted_ref, wanted_block_ref, wanted_lane_ref,
    near_send, near_receive, near_own, far_send, far_receive, far_own,
    screen_ref, ninth_ref, out_ref, out_ninth_ref, split_ref, left_ref, right_ref,
    all_ref, slot_left_ref, slot_right_ref, block_ref, lane_ref, row_ref, col_ref, lanes_ref,
    message_ref, landing_ref, send_sem, receive_sem, own_sem, source_ref, source_ninth_ref,
    reply_ref, reply_landing_ref, reply_send, reply_receive, reply_own,
    *render_refs,
):
    me = lax.axis_index("dev")
    loads = [
        pltpu.make_async_copy(far, near, load_sem.at[index])
        for index, (far, near) in enumerate(
            (
                (requests_ref, here_requests_ref),
                (params_ref, here_params_ref),
                (count_ref, here_count_ref),
                (place_ref, here_place_ref),
                (slots_ref, here_slots_ref),
                (target_ref, here_target_ref),
            )
        )
    ]
    for load in loads:
        load.start()
    greet(me)
    loads[0].wait()
    wide = jnp.concatenate(
        [here_requests_ref[...].astype(F32), jnp.zeros((128 - CAP, DEVICES), F32)], axis=0
    )
    by_device = wide.T.astype(I32).reshape(OUTER, INNER, 128)
    for inner in range(INNER):
        request_ref[inner, :, 0, :] = by_device[:, inner, :]
    await_greetings()
    near_sems = (near_send, near_receive, near_own)
    far_sems = (far_send, far_receive, far_own)
    send_requests(request_ref, middle_ref, near_sems, me)
    for load in loads[1:]:
        load.wait()
    project_all(here_params_ref, screen_ref, ninth_ref)
    forward_requests(request_ref, middle_ref, wanted_ref, near_sems, far_sems, me)
    index_tables(
        here_count_ref, here_place_ref, here_slots_ref,
        block_ref, lane_ref, row_ref, col_ref, lanes_ref, all_ref, slot_left_ref, slot_right_ref,
    )
    await_requests(middle_ref, wanted_ref, far_sems, me)
    wanted_tables(wanted_ref, wanted_block_ref, wanted_lane_ref)
    gather(
        screen_ref, ninth_ref, wanted_block_ref, wanted_lane_ref, out_ref, out_ninth_ref,
        split_ref, CAP, BLOCKS, 10, 10,
    )
    pack_messages(out_ref, out_ninth_ref, message_ref)
    sems = (send_sem, receive_sem, own_sem, me)
    send_all(message_ref, landing_ref, *sems)
    invert(
        wanted_block_ref, wanted_lane_ref, left_ref, right_ref, owner_row_ref, owner_col_ref,
        CAP, BLOCKS,
    )
    await_all(message_ref, landing_ref, *sems)
    unpack_messages(landing_ref, source_ref, source_ninth_ref)
    render(
        source_ref, source_ninth_ref, block_ref, lane_ref, row_ref, col_ref, lanes_ref,
        here_target_ref, rendered_ref, reply_ref, *render_refs,
    )
    reply_sems = (reply_send, reply_receive, reply_own, me)
    send_all(reply_ref, reply_landing_ref, *reply_sems)
    stores = [
        pltpu.make_async_copy(near, far, store_sem.at[index])
        for index, (near, far) in enumerate(
            (
                (rendered_ref, far_rendered_ref),
                (owner_row_ref, far_owner_row_ref),
                (owner_col_ref, far_owner_col_ref),
                (back_ref, far_back_ref),
                (back_ninth_ref, far_back_ninth_ref),
            )
        )
    ]
    for store in stores[:3]:
        store.start()
    await_all(reply_ref, reply_landing_ref, *reply_sems)
    unpack_messages(reply_landing_ref, back_ref, back_ninth_ref)
    for store in stores[3:]:
        store.start()
    for store in stores:
        store.wait()


def pullback_kernel(
    far_source_ref, far_ninth_ref, far_row_ref, far_col_ref, image_ref, params_ref,
    rendered_ref, gradient_ref,
    source_ref, source_ninth_ref, row_ref, col_ref,
    rows_ref, ninth_ref, split_ref, here_params_ref, here_gradient_ref, load_sem, store_sem,
):
    loads = [
        pltpu.make_async_copy(far, near, load_sem.at[index])
        for index, (far, near) in enumerate(
            (
                (far_source_ref, source_ref),
                (far_ninth_ref, source_ninth_ref),
                (far_row_ref, row_ref),
                (far_col_ref, col_ref),
                (params_ref, here_params_ref),
                (image_ref, rendered_ref),
            )
        )
    ]
    for load in loads:
        load.start()
    for load in loads[:4]:
        load.wait()
    gather(
        source_ref, source_ninth_ref, row_ref, col_ref, rows_ref, ninth_ref, split_ref,
        BLOCKS, CAP, 10, 10,
    )
    loads[4].wait()
    stores = []
    for group in range(OWNED // 1024):
        columns = pl.ds(group * 1024, 1024)
        eight = pl.ds(group * 8, 8)
        rows = load_rows(here_params_ref, columns)
        screen_grad = [rows_ref[eight, row, :] for row in range(8)] + [ninth_ref[eight, :]]
        screen, pullback = jax.vjp(project, rows)
        by_logit = screen_grad[5] * (1.0 / (1.0 + jnp.exp(rows[10])))
        screen_grad[5] = jnp.zeros_like(by_logit)
        (grads,) = pullback(screen_grad)
        grads[10] = by_logit
        for row in range(PARAMS):
            here_gradient_ref[row : row + 1, columns] = grads[row].reshape(1, 1024)
        stores.append(
            pltpu.make_async_copy(
                here_gradient_ref.at[:, columns], gradient_ref.at[:, columns], store_sem.at[group]
            )
        )
        stores[-1].start()
    for store in stores:
        store.wait()
    loads[5].wait()


def shape(dims, dtype=F32):
    return jax.ShapeDtypeStruct(dims, dtype)


def call(kernel, outs, specs, out_specs, scratch, name, collective=None):
    params = {"vmem_limit_bytes": VMEM_LIMIT}
    if collective is not None:
        params.update(collective_id=collective, has_side_effects=True)
    spaces = {"v": pltpu.VMEM, "s": pltpu.SMEM, "h": pltpu.HBM}
    return pl.pallas_call(
        kernel,
        out_shape=outs,
        in_specs=[pl.BlockSpec(memory_space=spaces[kind]) for kind in specs],
        out_specs=[pl.BlockSpec(memory_space=spaces[kind]) for kind in out_specs],
        scratch_shapes=scratch,
        compiler_params=pltpu.CompilerParams(**params),
        name=name,
    )


SPLIT = (3 * (CAP // 2 * 8 + 24), 256)
SPLIT_BACK = (3 * (SEG // 2 * 8 + 24), 256)
MESSAGE = (DEVICES, 3, 128)
TABLE = (CAP, 128)
STEPS = (SEG_PAD, 128)
EIGHT = (CAP, 8, 128)
NINE = (CAP // 8, 8, 128)


IMAGE = (3, TILES, 256)


def local(params, requests, tile_slots, tile_count, tile_place, target):
    vmem = pltpu.VMEM
    sems = [pltpu.SemaphoreType.DMA] * 3
    image, back, back_ninth, owner_row, owner_col = call(
        step_kernel,
        [shape(IMAGE), shape(EIGHT), shape(NINE), shape(TABLE, I32), shape(TABLE, I32)],
        "hhhhhh",
        "hhhhh",
        [
            vmem(IMAGE, F32), vmem(EIGHT, F32), vmem(NINE, F32), vmem(TABLE, I32),
            vmem(TABLE, I32), pltpu.SemaphoreType.DMA((5,)),
            vmem((CAP, DEVICES), I32), vmem((PARAMS, OWNED), F32),
            pltpu.SMEM((TILES,), I32), pltpu.SMEM((TILES,), I32), vmem((TILES, SLOTS), I32),
            vmem(IMAGE, F32), pltpu.SemaphoreType.DMA((6,)),
            vmem((INNER, OUTER, 1, 128), I32), vmem((INNER, OUTER, 1, 128), I32),
            vmem((OUTER, INNER, 1, 128), I32), vmem(TABLE, I32), vmem(TABLE, I32), *sems, *sems,
            vmem(EIGHT, F32), vmem(NINE, F32), vmem(EIGHT, F32), vmem(TABLE, F32),
            vmem(SPLIT, BF16),
            vmem((2 * BLOCKS, CAP * 128), BF16), vmem((128, CAP * 128), BF16),
            vmem((SEGS * SEG + 8, 128), F32),
            vmem((2 * CAP, SEG * 128), BF16), vmem((128, SEG * 128), BF16),
            vmem(STEPS, I32), vmem(STEPS, I32), vmem(TABLE, I32), vmem(TABLE, I32),
            vmem((8, 128), I32),
            vmem(MESSAGE, F32), vmem(MESSAGE, F32), *sems, vmem(EIGHT, F32), vmem(NINE, F32),
            vmem(MESSAGE, F32), vmem(MESSAGE, F32), *sems,
            vmem((SEG, 8, 128), F32), vmem(STEPS, F32),
            vmem((SEG, 12, 8, 128), F32),
            vmem((PASSES, SEG, GROUP, 8, 128), F32), vmem((PASSES, SEG, GROUP, 8, 128), F32),
            vmem((256, 128), F32), vmem((3, 256, 128), F32), vmem((256, 128), F32),
            vmem((SEG, 9, 8, 128), F32),
            vmem((SEG, 8, 128), F32), vmem((SEG_PAD // 8, 8, 128), F32),
            vmem(EIGHT, F32), vmem(TABLE, F32), vmem(SPLIT, BF16), vmem(SPLIT_BACK, BF16),
        ],
        "step",
        0,
    )(
        requests.reshape(DEVICES, CAP).T, params, tile_count, tile_place, tile_slots,
        target.transpose(1, 0, 2),
    )
    rendered, gradient = call(
        pullback_kernel,
        [shape(IMAGE), shape((PARAMS, OWNED))],
        "hhhhhh",
        "hh",
        [
            vmem(EIGHT, F32), vmem(NINE, F32), vmem(TABLE, I32), vmem(TABLE, I32),
            vmem(EIGHT, F32), vmem(TABLE, F32), vmem(SPLIT, BF16), vmem((PARAMS, OWNED), F32),
            vmem((PARAMS, OWNED), F32), pltpu.SemaphoreType.DMA((6,)),
            pltpu.SemaphoreType.DMA((OWNED // 1024,)),
        ],
        "pullback",
    )(back, back_ninth, owner_row, owner_col, image, params)
    return rendered.transpose(1, 0, 2), gradient


def solution(mesh):
    in_specs = (
        P(None, "dev"),
        P("dev", None, None),
        P("dev", None),
        P("dev"),
        P("dev"),
        P("dev", None, None),
    )
    out_specs = (P("dev", None, None), P(None, "dev"))
    return jax.shard_map(local, mesh=mesh, in_specs=in_specs, out_specs=out_specs, check_vma=False)
```

```python
import functools

import jax
import jax.numpy as jnp
from jax import lax
from jax.experimental import pallas as pl
from jax.experimental.pallas import tpu as pltpu
from jax.sharding import PartitionSpec as P

FOCAL = 1200.0
CENTER_X = 960.0
CENTER_Y = 540.0
DILATION = 0.3
BAND_ZERO = 0.28209479177387814
BAND_ONE = 0.4886025119029199
BAND_TWO = (
    1.0925484305920792,
    -1.0925484305920792,
    0.31539156525252005,
    -1.0925484305920792,
    0.5462742152960396,
)
BAND_THREE = (
    -0.5900435899266435,
    2.890611442640554,
    -0.4570457994644658,
    0.3731763325901154,
    -0.4570457994644658,
    1.445305721320277,
    -0.5900435899266435,
)
LOG2_E = 1.4426950408889634

DEVICES = 128
INNER = 8
OUTER = DEVICES // INNER
OWNED = 5120
CAP = 40
PARAMS = 59
BLOCKS = OWNED // 128
TILES = 16
SLOTS = 512
SEG = 46
SEG_PAD = 48
SEGS = 12
GROUP = 8
PASSES = 32 // GROUP
MIDDLE = 4
STEP_UNROLL = 23
BACK_UNROLL = 23
SHORT_UNROLL = 23
BF16 = jnp.bfloat16
MESH_ID = pl.DeviceIdType.MESH
F32 = jnp.float32
I32 = jnp.int32
VMEM_LIMIT = 64 * 1000 * 1000


def project(rows):
    x, y, z = rows[0], rows[1], rows[2]
    scales = [jnp.exp(rows[3 + k]) for k in range(3)]
    norm = jnp.sqrt(rows[6] * rows[6] + rows[7] * rows[7] + rows[8] * rows[8] + rows[9] * rows[9])
    qw, qx, qy, qz = (rows[6 + k] / norm for k in range(4))
    rotation = [
        [1.0 - 2.0 * (qy * qy + qz * qz), 2.0 * (qx * qy - qw * qz), 2.0 * (qx * qz + qw * qy)],
        [2.0 * (qx * qy + qw * qz), 1.0 - 2.0 * (qx * qx + qz * qz), 2.0 * (qy * qz - qw * qx)],
        [2.0 * (qx * qz - qw * qy), 2.0 * (qy * qz + qw * qx), 1.0 - 2.0 * (qx * qx + qy * qy)],
    ]
    spread = [[rotation[i][k] * scales[k] for k in range(3)] for i in range(3)]
    inverse_z = 1.0 / z
    diag = FOCAL * inverse_z
    jac_xz = -FOCAL * x * inverse_z * inverse_z
    jac_yz = -FOCAL * y * inverse_z * inverse_z
    across = [diag * spread[0][k] + jac_xz * spread[2][k] for k in range(3)]
    upward = [diag * spread[1][k] + jac_yz * spread[2][k] for k in range(3)]
    cov_xx = across[0] * across[0] + across[1] * across[1] + across[2] * across[2] + DILATION
    cov_xy = across[0] * upward[0] + across[1] * upward[1] + across[2] * upward[2]
    cov_yy = upward[0] * upward[0] + upward[1] * upward[1] + upward[2] * upward[2] + DILATION
    determinant = cov_xx * cov_yy - cov_xy * cov_xy
    distance = jnp.sqrt(x * x + y * y + z * z)
    fx, fy, fz = x / distance, y / distance, z / distance
    xx, yy, zz = fx * fx, fy * fy, fz * fz
    basis = [
        None,
        -BAND_ONE * fy,
        BAND_ONE * fz,
        -BAND_ONE * fx,
        BAND_TWO[0] * fx * fy,
        BAND_TWO[1] * fy * fz,
        BAND_TWO[2] * (2.0 * zz - xx - yy),
        BAND_TWO[3] * fx * fz,
        BAND_TWO[4] * (xx - yy),
        BAND_THREE[0] * fy * (3.0 * xx - yy),
        BAND_THREE[1] * fx * fy * fz,
        BAND_THREE[2] * fy * (4.0 * zz - xx - yy),
        BAND_THREE[3] * fz * (2.0 * zz - 3.0 * xx - 3.0 * yy),
        BAND_THREE[4] * fx * (4.0 * zz - xx - yy),
        BAND_THREE[5] * fz * (xx - yy),
        BAND_THREE[6] * fx * (xx - 3.0 * yy),
    ]
    colours = []
    for channel in range(3):
        total = BAND_ZERO * rows[11 + channel]
        for k in range(1, 16):
            total = total + basis[k] * rows[11 + 3 * k + channel]
        colours.append(jnp.maximum(total + 0.5, 0.0))
    return [
        FOCAL * x * inverse_z + CENTER_X,
        FOCAL * y * inverse_z + CENTER_Y,
        cov_yy / determinant,
        -cov_xy / determinant,
        cov_xx / determinant,
        1.0 / (1.0 + jnp.exp(-rows[10])),
        *colours,
    ]


def load_rows(params_ref, columns):
    return [params_ref[row : row + 1, columns].reshape(8, 128) for row in range(PARAMS)]


def project_all(params_ref, screen_ref, ninth_ref):
    def one_group(group, carry):
        screen = project(
            load_rows(params_ref, pl.ds(pl.multiple_of(group * 1024, 1024), 1024))
        )
        for row in range(8):
            screen_ref[pl.ds(pl.multiple_of(group * 8, 8), 8), row, :] = screen[row]
        ninth_ref[group] = screen[8]
        return carry

    lax.fori_loop(0, OWNED // 1024, one_group, 0)


def repeat(count, unroll, body, state):
    def turn(index, state):
        for part in range(unroll):
            state = body(index * unroll + part, state)
        return state

    return lax.fori_loop(0, count // unroll, turn, state)


def gather(
    source_ref, ninth_ref, block_ref, lane_ref, out_ref, out_ninth_ref, split_ref,
    targets, sources, by_matmul, by_lanes,
):
    half = sources // 2
    eights = half * 8
    height = eights + 24
    width = 128 * by_matmul
    ninth = ninth_ref[...].reshape(-1, 128)
    rest = jnp.concatenate(
        [
            jnp.concatenate([ninth[0:half], ninth[half:sources]], axis=1),
            jnp.zeros((24 - half, 256), F32),
        ],
        axis=0,
    )
    main = jnp.concatenate(
        [
            source_ref[0:half].reshape(eights, 128),
            source_ref[half:sources].reshape(eights, 128),
        ],
        axis=1,
    )
    for part in range(3):
        for values, start in ((main, 0), (rest, eights)):
            rounded = values.astype(BF16)
            split_ref[part * height + start : part * height + start + values.shape[0]] = rounded
        main = main - main.astype(BF16).astype(F32)
        rest = rest - rest.astype(BF16).astype(F32)
    iota = lax.broadcasted_iota(I32, (256, width), 0).astype(F32).astype(BF16)
    sublane_rest = lax.broadcasted_iota(I32, (24, width), 0)
    sublane = lax.broadcasted_iota(I32, (8, 128), 0)

    def turn(index, carry):
        base = index * (by_matmul + by_lanes)
        rows = [pl.ds(base + k, 1) for k in range(by_matmul)]
        block = jnp.concatenate([block_ref[row, :] for row in rows], axis=1)
        lane = jnp.concatenate([lane_ref[row, :] for row in rows], axis=1)
        upper = jnp.where(block >= half, 1, 0)
        key = jnp.broadcast_to((lane + 128 * upper).astype(F32), (16, width)).astype(BF16)
        place = block - half * upper
        match = jnp.concatenate([key] * 16, axis=0) == iota
        pick = jnp.where(match, jnp.ones((), BF16), jnp.zeros((), BF16))
        parts = lax.dot_general(
            split_ref[...], pick, (((1,), (0,)), ((), ())), preferred_element_type=F32
        )
        for k in range(by_lanes):
            row = base + by_matmul + k
            lane = jnp.broadcast_to(lane_ref[pl.ds(row, 1), :], (8, 128))
            block = jnp.broadcast_to(block_ref[pl.ds(row, 1), :], (8, 128))
            total = jnp.zeros((8, 128), F32)
            for source in range(sources):
                picked = jnp.take_along_axis(
                    source_ref[source], lane, axis=1, mode="promise_in_bounds"
                )
                total = jnp.where(block == source, picked, total)
            out_ref[row] = total
            offset = block - sublane
            total = jnp.zeros((8, 128), F32)
            for source in range((sources + 7) // 8):
                picked = jnp.take_along_axis(
                    ninth_ref[source], lane, axis=1, mode="promise_in_bounds"
                )
                total = jnp.where(offset == 8 * source, picked, total)
            out_ninth_ref[pl.ds(row, 1), :] = jnp.sum(total, axis=0, keepdims=True)
        values = (parts[0:height] + parts[height : 2 * height]) + parts[2 * height : 3 * height]
        wide = jnp.broadcast_to(place, (8, width))
        total = jnp.zeros((8, width), F32)
        for source in range(half):
            total = jnp.where(wide == source, values[8 * source : 8 * source + 8], total)
        last = jnp.sum(
            jnp.where(sublane_rest == place, values[eights:height], 0.0), axis=0, keepdims=True
        )
        for k in range(by_matmul):
            out_ref[base + k] = total[:, 128 * k : 128 * k + 128]
            out_ninth_ref[pl.ds(base + k, 1), :] = last[:, 128 * k : 128 * k + 128]
        return carry

    lax.fori_loop(0, targets // (by_matmul + by_lanes), turn, 0)


def invert(block_ref, lane_ref, left_ref, right_ref, row_ref, col_ref, rows, blocks):
    iota_lane = lax.broadcasted_iota(I32, (1, 128), 1).astype(F32)
    iota_block = lax.broadcasted_iota(I32, (blocks, 128), 0)
    iota_sub = lax.broadcasted_iota(I32, (128, 128), 0)

    def one_row(row, carry):
        columns = pl.ds(pl.multiple_of(row * 128, 128), 128)
        here = iota_block == block_ref[pl.ds(row, 1), :]
        value = jnp.full((1, 128), 0.0, F32) + row.astype(F32)
        left_ref[0:blocks, columns] = jnp.where(here, value, 0.0).astype(BF16)
        left_ref[blocks : 2 * blocks, columns] = jnp.where(here, iota_lane, 0.0).astype(
            BF16
        )
        right_ref[:, columns] = jnp.where(
            iota_sub == lane_ref[pl.ds(row, 1), :], 1.0, 0.0
        ).astype(BF16)
        return carry

    repeat(rows, 2, one_row, 0)
    found = lax.dot_general(
        left_ref[...], right_ref[...], (((1,), (1,)), ((), ())), preferred_element_type=F32
    )
    row_ref[...] = (found[0:blocks] + 0.5).astype(I32)
    col_ref[...] = (found[blocks : 2 * blocks] + 0.5).astype(I32)


def pack_messages(rows_ref, ninth_ref, out_ref):
    flat = rows_ref[...].reshape(CAP * 8, 128)
    out_ref[:, 0, :] = flat[0:128].T
    out_ref[:, 1, :] = flat[128:256].T
    last = jnp.concatenate(
        [flat[256:320], ninth_ref[...], jnp.zeros((128 - 64 - CAP, 128), F32)], axis=0
    )
    out_ref[:, 2, :] = last.T


def unpack_messages(message_ref, rows_ref, ninth_ref):
    rows_ref[0:16] = message_ref[:, 0, :].T.reshape(16, 8, 128)
    rows_ref[16:32] = message_ref[:, 1, :].T.reshape(16, 8, 128)
    last = message_ref[:, 2, :].T
    rows_ref[32:40] = last[0:64].reshape(8, 8, 128)
    ninth_ref[...] = last[64 : 64 + CAP].reshape(CAP // 8, 8, 128)


def request_peers(me):
    outer, inner = lax.div(me, INNER), lax.rem(me, INNER)
    near = [outer * INNER + lax.rem(inner + turn, INNER) for turn in range(1, INNER)]
    far = [lax.rem(outer + turn, OUTER) * INNER + inner for turn in range(1, OUTER)]
    return outer, inner, near, far


def greet(me):
    barrier = pltpu.get_barrier_semaphore()
    _, _, near, far = request_peers(me)
    for peer in near + far:
        pl.semaphore_signal(barrier, inc=1, device_id=(peer,), device_id_type=MESH_ID)


def await_greetings():
    pl.semaphore_wait(pltpu.get_barrier_semaphore(), INNER + OUTER - 2)


def send_requests(request_ref, middle_ref, sems, me):
    send_sem, receive_sem, own_sem = sems
    _, inner, near, _ = request_peers(me)
    for peer in near:
        pltpu.make_async_remote_copy(
            src_ref=request_ref.at[lax.rem(peer, INNER)],
            dst_ref=middle_ref.at[inner],
            send_sem=send_sem,
            recv_sem=receive_sem,
            device_id=(peer,),
            device_id_type=MESH_ID,
        ).start()
    pltpu.make_async_copy(request_ref.at[inner], middle_ref.at[inner], own_sem).start()


def forward_requests(request_ref, middle_ref, wanted_ref, first_sems, sems, me):
    first_send, first_receive, first_own = first_sems
    send_sem, receive_sem, own_sem = sems
    outer, inner, _, far = request_peers(me)
    others = pl.ds(0, INNER - 1)
    pltpu.make_async_copy(request_ref.at[inner], middle_ref.at[inner], first_own).wait()
    pltpu.make_async_copy(middle_ref.at[others], middle_ref.at[others], first_receive).wait()
    for peer in far:
        pltpu.make_async_remote_copy(
            src_ref=middle_ref.at[:, lax.div(peer, INNER)],
            dst_ref=wanted_ref.at[outer],
            send_sem=send_sem,
            recv_sem=receive_sem,
            device_id=(peer,),
            device_id_type=MESH_ID,
        ).start()
    pltpu.make_async_copy(middle_ref.at[:, outer], wanted_ref.at[outer], own_sem).start()
    pltpu.make_async_copy(request_ref.at[others], request_ref.at[others], first_send).wait()


def await_requests(middle_ref, wanted_ref, sems, me):
    send_sem, receive_sem, own_sem = sems
    outer = lax.div(me, INNER)
    others = pl.ds(0, OUTER - 1)
    pltpu.make_async_copy(middle_ref.at[:, outer], wanted_ref.at[outer], own_sem).wait()
    pltpu.make_async_copy(wanted_ref.at[others], wanted_ref.at[others], receive_sem).wait()
    pltpu.make_async_copy(wanted_ref.at[others], wanted_ref.at[others], send_sem).wait()


def far_first():
    offsets = [
        (y, x, z, core) for y in range(4) for x in range(4) for z in range(4) for core in range(2)
    ]
    hops = (0, 1, 2, 1)
    offsets.sort(key=lambda o: -(2 * (hops[o[0]] + hops[o[1]] + hops[o[2]]) + o[3]))
    return offsets[:-1]


def send_all(source_ref, landing_ref, send_sem, receive_sem, own_sem, me):
    at_y, at_x = lax.div(me, 32), lax.rem(lax.div(me, 8), 4)
    at_z, at_core = lax.rem(lax.div(me, 2), 4), lax.rem(me, 2)
    to_y = [32 * lax.rem(at_y + turn, 4) for turn in range(4)]
    to_x = [8 * lax.rem(at_x + turn, 4) for turn in range(4)]
    to_z = [2 * lax.rem(at_z + turn, 4) for turn in range(4)]
    to_core = [lax.rem(at_core + turn, 2) for turn in range(2)]
    for y, x, z, core in far_first():
        peer = to_y[y] + to_x[x] + to_z[z] + to_core[core]
        pltpu.make_async_remote_copy(
            src_ref=source_ref.at[peer],
            dst_ref=landing_ref.at[me],
            send_sem=send_sem,
            recv_sem=receive_sem,
            device_id=(peer,),
            device_id_type=MESH_ID,
        ).start()
    pltpu.make_async_copy(source_ref.at[me], landing_ref.at[me], own_sem).start()


def await_all(source_ref, landing_ref, send_sem, receive_sem, own_sem, me):
    others = pl.ds(0, DEVICES - 1)
    pltpu.make_async_copy(source_ref.at[me], landing_ref.at[me], own_sem).wait()
    pltpu.make_async_copy(landing_ref.at[others], landing_ref.at[others], receive_sem).wait()
    pltpu.make_async_copy(source_ref.at[others], source_ref.at[others], send_sem).wait()


def wanted_tables(wanted_ref, block_ref, lane_ref):
    wanted = wanted_ref[:, :, 0, :].reshape(DEVICES, 128).astype(F32).T[0:CAP].astype(I32)
    block_ref[...] = wanted >> 7
    lane_ref[...] = wanted & 127


def lane_map(count_ref, place_ref):
    lane = lax.broadcasted_iota(I32, (1, 128), 1)
    tile = jnp.full((1, 128), -1, I32)
    segment = jnp.zeros((1, 128), I32)
    segments = jnp.zeros((1, 128), I32)
    count = jnp.zeros((1, 128), I32)
    origin_x = jnp.zeros((1, 128), I32)
    origin_y = jnp.zeros((1, 128), I32)
    base = jnp.int32(0)
    for index in range(TILES):
        listed = count_ref[index]
        place = place_ref[index]
        used = lax.div(listed + (SEG - 1), SEG)
        inside = (lane >= base) & (lane < base + used)
        place_y = lax.div(place, 120)
        tile = jnp.where(inside, index, tile)
        segment = jnp.where(inside, lane - base, segment)
        segments = jnp.where(inside, used, segments)
        count = jnp.where(inside, listed, count)
        origin_x = jnp.where(inside, 16 * (place - 120 * place_y), origin_x)
        origin_y = jnp.where(inside, 16 * place_y, origin_y)
        base = base + used
    return tile, segment, segments, count, origin_x, origin_y


def index_tables(
    count_ref, place_ref, slots_ref,
    block_ref, lane_ref, row_ref, col_ref, lanes_ref, all_ref, left_ref, right_ref,
):
    tile, segment, segments, count, origin_x, origin_y = lane_map(count_ref, place_ref)
    lanes_ref[0:1] = tile
    lanes_ref[1:2] = segment
    lanes_ref[2:3] = segments
    lanes_ref[3:4] = count
    lanes_ref[4:5] = origin_x
    lanes_ref[5:6] = origin_y
    lanes_ref[6:8] = jnp.zeros((2, 128), I32)
    slots = slots_ref[...]
    owner = ((slots.astype(F32) + 0.5) * (1.0 / CAP)).astype(I32)
    within = slots - owner * CAP
    pick = jnp.where(
        lax.broadcasted_iota(I32, (TILES, 128), 0) == tile, 1.0, 0.0
    ).astype(BF16)
    contract = (((0,), (0,)), ((), ()))
    step = lax.broadcasted_iota(I32, (SEG_PAD, 128), 0)
    live = (step < SEG) & (step + segment * SEG < count)
    for values, out, unused in ((within, block_ref, -1), (owner, lane_ref, 0)):
        all_ref[0:SLOTS] = lax.dot_general(
            values.astype(F32).astype(BF16), pick, contract, preferred_element_type=F32
        )
        all_ref[SLOTS:] = jnp.zeros_like(all_ref[SLOTS:])
        total = jnp.zeros((SEG_PAD, 128), F32)
        for part in range(SEGS):
            rows = all_ref[part * SEG : part * SEG + SEG_PAD]
            total = jnp.where(segment == part, rows, total)
        out[...] = jnp.where(live, (total + 0.5).astype(I32), unused)
    invert(block_ref, lane_ref, left_ref, right_ref, row_ref, col_ref, SEG, CAP)


def render(
    source_ref, source_ninth_ref, block_ref, lane_ref, row_ref, col_ref, lanes_ref, target_ref,
    rendered_ref, gradient_ref,
    rows_ref, ninth_ref, pre_ref, alpha_ref, weight_ref,
    trans_ref, colour_ref, behind_ref, moment_ref, grad_ref, grad_ninth_ref,
    back_ref, back_ninth_ref, split_ref, split_back_ref,
):
    gather(
        source_ref, source_ninth_ref, block_ref, lane_ref, rows_ref, ninth_ref, split_ref,
        SEG, CAP, 12, 11,
    )
    tile = lanes_ref[0:1]
    segment = lanes_ref[1:2]
    segments = lanes_ref[2:3]
    origin_x = lanes_ref[4:5].astype(F32)
    origin_y = lanes_ref[5:6].astype(F32)
    sub = lax.broadcasted_iota(I32, (8, 128), 0).astype(F32) + 0.5

    def wide(row):
        return jnp.broadcast_to(row, (8, 128))

    def prepare(step, carry):
        attrs = rows_ref[step]
        screen_x = attrs[0:1] - origin_x
        screen_y = attrs[1:2] - origin_y
        curve_x = wide(-0.5 * LOG2_E * attrs[2:3])
        curve_xy = wide(-LOG2_E * attrs[3:4])
        for half in range(2):
            delta = (sub + 8.0 * half) - wide(screen_x)
            pre_ref[step, half] = curve_x * delta * delta
            pre_ref[step, 2 + half] = curve_xy * delta
            pre_ref[step, 9 + half] = delta
        pre_ref[step, 4] = wide(screen_y)
        pre_ref[step, 5] = wide(-0.5 * LOG2_E * attrs[4:5])
        pre_ref[step, 6] = wide(attrs[5:6])
        pre_ref[step, 7] = wide(attrs[6:7])
        pre_ref[step, 8] = wide(attrs[7:8])
        pre_ref[step, 11] = wide(ninth_ref[pl.ds(step, 1), :])
        return carry

    repeat(SEG, SHORT_UNROLL, prepare, 0)

    def place(index):
        half, block = index % 2, index // 2
        rows = [pl.ds((2 * (GROUP * block + k) + half) * 8, 8) for k in range(GROUP)]
        return half, GROUP * block + MIDDLE + 0.5, rows

    for index in range(PASSES):
        half, middle, rows = place(index)

        def one_step(step, state):
            trans, red, green, blue = (list(part) for part in state)
            opacity, curve_y = pre_ref[step, 6], pre_ref[step, 5]
            colours = (pre_ref[step, 7], pre_ref[step, 8], pre_ref[step, 11])
            delta_y = middle - pre_ref[step, 4]
            bend = curve_y * delta_y
            slant = pre_ref[step, 2 + half] + bend
            twice = curve_y + curve_y
            powers = [None] * GROUP
            powers[MIDDLE] = pre_ref[step, half] + slant * delta_y
            slant = slant + bend
            rise, fall = curve_y + slant, curve_y - slant
            for k in range(MIDDLE + 1, GROUP):
                powers[k] = powers[k - 1] + rise
                rise = rise + twice
            for k in range(MIDDLE - 1, -1, -1):
                powers[k] = powers[k + 1] + fall
                fall = fall + twice
            for k in range(GROUP):
                alpha = opacity * jnp.exp2(powers[k])
                weight = alpha * trans[k]
                trans[k] = trans[k] - weight
                red[k] = red[k] + colours[0] * weight
                green[k] = green[k] + colours[1] * weight
                blue[k] = blue[k] + colours[2] * weight
                alpha_ref[index, step, k] = alpha
                weight_ref[index, step, k] = weight
            return tuple(trans), tuple(red), tuple(green), tuple(blue)

        ones = tuple(jnp.ones((8, 128), F32) for _ in range(GROUP))
        zeros = tuple(jnp.zeros((8, 128), F32) for _ in range(GROUP))
        state = repeat(SEG, STEP_UNROLL, one_step, (ones, zeros, zeros, zeros))
        for k in range(GROUP):
            trans_ref[rows[k], :] = state[0][k]
            for channel in range(3):
                colour_ref[channel, rows[k], :] = state[1 + channel][k]

    through = trans_ref[...]
    start = jnp.where(segment == 0, 1.0, pltpu.roll(through, 1, 1))
    for shift in (1, 2, 4, 8):
        start = start * jnp.where(segment >= shift, pltpu.roll(start, shift, 1), 1.0)
    pick = jnp.where(lax.broadcasted_iota(I32, (TILES, 128), 0) == tile, 1.0, 0.0)
    behind = jnp.zeros((256, 128), F32)
    for channel in range(3):
        image = lax.dot_general(
            pick, colour_ref[channel] * start, (((1,), (1,)), ((), ())),
            preferred_element_type=F32, precision=lax.Precision.HIGHEST,
        )
        rendered_ref[channel] = image
        error = (image - target_ref[channel]) * (1.0 / 256.0)
        spread = lax.dot_general(
            error, pick, (((0,), (0,)), ((), ())),
            preferred_element_type=F32, precision=lax.Precision.HIGHEST,
        )
        behind = behind + spread * colour_ref[channel]
        colour_ref[channel] = spread * start
    left = segments - 1 - segment
    factor = jnp.where(left >= 1, pltpu.roll(through, 127, 1), 0.0)
    behind = jnp.where(left >= 1, pltpu.roll(behind, 127, 1), 0.0)
    for shift in (1, 2, 4, 8):
        reach = left >= shift
        behind = behind + factor * jnp.where(reach, pltpu.roll(behind, 128 - shift, 1), 0.0)
        factor = factor * jnp.where(reach, pltpu.roll(factor, 128 - shift, 1), 0.0)
    behind_ref[...] = behind * start

    for index in range(PASSES):
        half, middle, rows = place(index)
        errors = [[colour_ref[channel, rows[k], :] for channel in range(3)] for k in range(GROUP)]

        def one_step(count, state):
            step = SEG - 1 - count
            state = list(state)
            colours = (pre_ref[step, 7], pre_ref[step, 8], pre_ref[step, 11])
            slopes = [None] * GROUP
            shares = [None, None, None]
            for k in range(GROUP):
                alpha = alpha_ref[index, step, k]
                weight = weight_ref[index, step, k]
                shade = (
                    colours[0] * errors[k][0]
                    + colours[1] * errors[k][1]
                    + colours[2] * errors[k][2]
                )
                gap = shade - state[k]
                state[k] = state[k] + alpha * gap
                slopes[k] = weight * gap
                for channel in range(3):
                    part = weight * errors[k][channel]
                    shares[channel] = part if k == 0 else shares[channel] + part
            flat = tilt = bend = None
            for order in (range(GROUP - 1, MIDDLE, -1), range(MIDDLE)):
                first = second = third = None
                for k in order:
                    first = slopes[k] if first is None else first + slopes[k]
                    second = first if second is None else second + first
                    third = second if third is None else third + second
                square = (third + third) - second
                flat = first if flat is None else flat + first
                bend = square if bend is None else bend + square
                tilt = second if tilt is None else tilt - second
            flat = flat + slopes[MIDDLE]
            delta_y = middle - pre_ref[step, 4]
            moved = tilt + delta_y * flat
            bend = bend + delta_y * (tilt + moved)
            for row, value, started in (
                (3 * half, flat, index > 1),
                (3 * half + 1, moved, index > 1),
                (3 * half + 2, bend, index > 1),
                (6, shares[0], index > 0),
                (7, shares[1], index > 0),
                (8, shares[2], index > 0),
            ):
                moment_ref[step, row] = moment_ref[step, row] + value if started else value
            return tuple(state)

        repeat(
            SEG, BACK_UNROLL, one_step, tuple(behind_ref[rows[k], :] for k in range(GROUP))
        )

    def finish(step, carry):
        delta = [pre_ref[step, 9], pre_ref[step, 10]]
        sums = [moment_ref[step, row] for row in range(9)]
        flat = [sums[0], sums[3]]
        tilt = [sums[1], sums[4]]
        bend = [sums[2], sums[5]]
        side = [flat[half] * delta[half] for half in range(2)]

        def total(register):
            return jnp.sum(register, axis=0, keepdims=True)

        m00 = total(flat[0] + flat[1])
        m10 = total(side[0] + side[1])
        m01 = total(tilt[0] + tilt[1])
        m20 = total(side[0] * delta[0] + side[1] * delta[1])
        m11 = total(tilt[0] * delta[0] + tilt[1] * delta[1])
        m02 = total(bend[0] + bend[1])
        attrs = rows_ref[step]
        conic_a, conic_b, conic_c = attrs[2:3], attrs[3:4], attrs[4:5]
        grad_ref[step] = jnp.concatenate(
            [
                conic_a * m10 + conic_b * m01,
                conic_b * m10 + conic_c * m01,
                -0.5 * m20,
                -m11,
                -0.5 * m02,
                m00,
                total(sums[6]),
                total(sums[7]),
            ],
            axis=0,
        )
        ninth_ref[pl.ds(step, 1), :] = total(sums[8])
        return carry

    repeat(SEG, SHORT_UNROLL, finish, 0)
    ninth_ref[SEG:SEG_PAD] = jnp.zeros((SEG_PAD - SEG, 128), F32)
    grad_ninth_ref[...] = ninth_ref[...].reshape(SEG_PAD // 8, 8, 128)
    gather(
        grad_ref, grad_ninth_ref, row_ref, col_ref, back_ref, back_ninth_ref, split_back_ref,
        CAP, SEG, 10, 10,
    )
    pack_messages(back_ref, back_ninth_ref, gradient_ref)


def step_kernel(
    requests_ref, params_ref, count_ref, place_ref, slots_ref, target_ref,
    far_rendered_ref, far_back_ref, far_back_ninth_ref, far_owner_row_ref, far_owner_col_ref,
    rendered_ref, back_ref, back_ninth_ref, owner_row_ref, owner_col_ref, store_sem,
    here_requests_ref, here_params_ref, here_count_ref, here_place_ref, here_slots_ref,
    here_target_ref, load_sem,
    request_ref, middle_ref, wanted_ref, wanted_block_ref, wanted_lane_ref,
    near_send, near_receive, near_own, far_send, far_receive, far_own,
    screen_ref, ninth_ref, out_ref, out_ninth_ref, split_ref, left_ref, right_ref,
    all_ref, slot_left_ref, slot_right_ref, block_ref, lane_ref, row_ref, col_ref, lanes_ref,
    message_ref, landing_ref, send_sem, receive_sem, own_sem, source_ref, source_ninth_ref,
    reply_ref, reply_landing_ref, reply_send, reply_receive, reply_own,
    *render_refs,
):
    me = lax.axis_index("dev")
    loads = [
        pltpu.make_async_copy(far, near, load_sem.at[index])
        for index, (far, near) in enumerate(
            (
                (requests_ref, here_requests_ref),
                (params_ref, here_params_ref),
                (count_ref, here_count_ref),
                (place_ref, here_place_ref),
                (slots_ref, here_slots_ref),
                (target_ref, here_target_ref),
            )
        )
    ]
    for load in loads:
        load.start()
    greet(me)
    loads[0].wait()
    wide = jnp.concatenate(
        [here_requests_ref[...].astype(F32), jnp.zeros((128 - CAP, DEVICES), F32)], axis=0
    )
    by_device = wide.T.astype(I32).reshape(OUTER, INNER, 128)
    for inner in range(INNER):
        request_ref[inner, :, 0, :] = by_device[:, inner, :]
    await_greetings()
    near_sems = (near_send, near_receive, near_own)
    far_sems = (far_send, far_receive, far_own)
    send_requests(request_ref, middle_ref, near_sems, me)
    for load in loads[1:]:
        load.wait()
    project_all(here_params_ref, screen_ref, ninth_ref)
    forward_requests(request_ref, middle_ref, wanted_ref, near_sems, far_sems, me)
    index_tables(
        here_count_ref, here_place_ref, here_slots_ref,
        block_ref, lane_ref, row_ref, col_ref, lanes_ref, all_ref, slot_left_ref, slot_right_ref,
    )
    await_requests(middle_ref, wanted_ref, far_sems, me)
    wanted_tables(wanted_ref, wanted_block_ref, wanted_lane_ref)
    gather(
        screen_ref, ninth_ref, wanted_block_ref, wanted_lane_ref, out_ref, out_ninth_ref,
        split_ref, CAP, BLOCKS, 10, 10,
    )
    pack_messages(out_ref, out_ninth_ref, message_ref)
    sems = (send_sem, receive_sem, own_sem, me)
    send_all(message_ref, landing_ref, *sems)
    invert(
        wanted_block_ref, wanted_lane_ref, left_ref, right_ref, owner_row_ref, owner_col_ref,
        CAP, BLOCKS,
    )
    await_all(message_ref, landing_ref, *sems)
    unpack_messages(landing_ref, source_ref, source_ninth_ref)
    render(
        source_ref, source_ninth_ref, block_ref, lane_ref, row_ref, col_ref, lanes_ref,
        here_target_ref, rendered_ref, reply_ref, *render_refs,
    )
    reply_sems = (reply_send, reply_receive, reply_own, me)
    send_all(reply_ref, reply_landing_ref, *reply_sems)
    stores = [
        pltpu.make_async_copy(near, far, store_sem.at[index])
        for index, (near, far) in enumerate(
            (
                (rendered_ref, far_rendered_ref),
                (owner_row_ref, far_owner_row_ref),
                (owner_col_ref, far_owner_col_ref),
                (back_ref, far_back_ref),
                (back_ninth_ref, far_back_ninth_ref),
            )
        )
    ]
    for store in stores[:3]:
        store.start()
    await_all(reply_ref, reply_landing_ref, *reply_sems)
    unpack_messages(reply_landing_ref, back_ref, back_ninth_ref)
    for store in stores[3:]:
        store.start()
    for store in stores:
        store.wait()


def pullback_kernel(
    far_source_ref, far_ninth_ref, far_row_ref, far_col_ref, image_ref, params_ref,
    rendered_ref, gradient_ref,
    source_ref, source_ninth_ref, row_ref, col_ref,
    rows_ref, ninth_ref, split_ref, here_params_ref, here_gradient_ref, load_sem, store_sem,
):
    loads = [
        pltpu.make_async_copy(far, near, load_sem.at[index])
        for index, (far, near) in enumerate(
            (
                (far_source_ref, source_ref),
                (far_ninth_ref, source_ninth_ref),
                (far_row_ref, row_ref),
                (far_col_ref, col_ref),
                (params_ref, here_params_ref),
                (image_ref, rendered_ref),
            )
        )
    ]
    for load in loads:
        load.start()
    for load in loads[:4]:
        load.wait()
    gather(
        source_ref, source_ninth_ref, row_ref, col_ref, rows_ref, ninth_ref, split_ref,
        BLOCKS, CAP, 10, 10,
    )
    loads[4].wait()
    stores = []
    for group in range(OWNED // 1024):
        columns = pl.ds(group * 1024, 1024)
        eight = pl.ds(group * 8, 8)
        rows = load_rows(here_params_ref, columns)
        screen_grad = [rows_ref[eight, row, :] for row in range(8)] + [ninth_ref[eight, :]]
        screen, pullback = jax.vjp(project, rows)
        by_logit = screen_grad[5] * (1.0 / (1.0 + jnp.exp(rows[10])))
        screen_grad[5] = jnp.zeros_like(by_logit)
        (grads,) = pullback(screen_grad)
        grads[10] = by_logit
        for row in range(PARAMS):
            here_gradient_ref[row : row + 1, columns] = grads[row].reshape(1, 1024)
        stores.append(
            pltpu.make_async_copy(
                here_gradient_ref.at[:, columns], gradient_ref.at[:, columns], store_sem.at[group]
            )
        )
        stores[-1].start()
    for store in stores:
        store.wait()
    loads[5].wait()


def shape(dims, dtype=F32):
    return jax.ShapeDtypeStruct(dims, dtype)


def call(kernel, outs, specs, out_specs, scratch, name, collective=None):
    params = {"vmem_limit_bytes": VMEM_LIMIT}
    if collective is not None:
        params.update(collective_id=collective, has_side_effects=True)
    spaces = {"v": pltpu.VMEM, "s": pltpu.SMEM, "h": pltpu.HBM}
    return pl.pallas_call(
        kernel,
        out_shape=outs,
        in_specs=[pl.BlockSpec(memory_space=spaces[kind]) for kind in specs],
        out_specs=[pl.BlockSpec(memory_space=spaces[kind]) for kind in out_specs],
        scratch_shapes=scratch,
        compiler_params=pltpu.CompilerParams(**params),
        name=name,
    )


SPLIT = (3 * (CAP // 2 * 8 + 24), 256)
SPLIT_BACK = (3 * (SEG // 2 * 8 + 24), 256)
MESSAGE = (DEVICES, 3, 128)
TABLE = (CAP, 128)
STEPS = (SEG_PAD, 128)
EIGHT = (CAP, 8, 128)
NINE = (CAP // 8, 8, 128)


IMAGE = (3, TILES, 256)


def local(params, requests, tile_slots, tile_count, tile_place, target):
    vmem = pltpu.VMEM
    sems = [pltpu.SemaphoreType.DMA] * 3
    image, back, back_ninth, owner_row, owner_col = call(
        step_kernel,
        [shape(IMAGE), shape(EIGHT), shape(NINE), shape(TABLE, I32), shape(TABLE, I32)],
        "hhhhhh",
        "hhhhh",
        [
            vmem(IMAGE, F32), vmem(EIGHT, F32), vmem(NINE, F32), vmem(TABLE, I32),
            vmem(TABLE, I32), pltpu.SemaphoreType.DMA((5,)),
            vmem((CAP, DEVICES), I32), vmem((PARAMS, OWNED), F32),
            pltpu.SMEM((TILES,), I32), pltpu.SMEM((TILES,), I32), vmem((TILES, SLOTS), I32),
            vmem(IMAGE, F32), pltpu.SemaphoreType.DMA((6,)),
            vmem((INNER, OUTER, 1, 128), I32), vmem((INNER, OUTER, 1, 128), I32),
            vmem((OUTER, INNER, 1, 128), I32), vmem(TABLE, I32), vmem(TABLE, I32), *sems, *sems,
            vmem(EIGHT, F32), vmem(NINE, F32), vmem(EIGHT, F32), vmem(TABLE, F32),
            vmem(SPLIT, BF16),
            vmem((2 * BLOCKS, CAP * 128), BF16), vmem((128, CAP * 128), BF16),
            vmem((SEGS * SEG + 8, 128), F32),
            vmem((2 * CAP, SEG * 128), BF16), vmem((128, SEG * 128), BF16),
            vmem(STEPS, I32), vmem(STEPS, I32), vmem(TABLE, I32), vmem(TABLE, I32),
            vmem((8, 128), I32),
            vmem(MESSAGE, F32), vmem(MESSAGE, F32), *sems, vmem(EIGHT, F32), vmem(NINE, F32),
            vmem(MESSAGE, F32), vmem(MESSAGE, F32), *sems,
            vmem((SEG, 8, 128), F32), vmem(STEPS, F32),
            vmem((SEG, 12, 8, 128), F32),
            vmem((PASSES, SEG, GROUP, 8, 128), F32), vmem((PASSES, SEG, GROUP, 8, 128), F32),
            vmem((256, 128), F32), vmem((3, 256, 128), F32), vmem((256, 128), F32),
            vmem((SEG, 9, 8, 128), F32),
            vmem((SEG, 8, 128), F32), vmem((SEG_PAD // 8, 8, 128), F32),
            vmem(EIGHT, F32), vmem(TABLE, F32), vmem(SPLIT, BF16), vmem(SPLIT_BACK, BF16),
        ],
        "step",
        0,
    )(
        requests.reshape(DEVICES, CAP).T, params, tile_count, tile_place, tile_slots,
        target.transpose(1, 0, 2),
    )
    rendered, gradient = call(
        pullback_kernel,
        [shape(IMAGE), shape((PARAMS, OWNED))],
        "hhhhhh",
        "hh",
        [
            vmem(EIGHT, F32), vmem(NINE, F32), vmem(TABLE, I32), vmem(TABLE, I32),
            vmem(EIGHT, F32), vmem(TABLE, F32), vmem(SPLIT, BF16), vmem((PARAMS, OWNED), F32),
            vmem((PARAMS, OWNED), F32), pltpu.SemaphoreType.DMA((6,)),
            pltpu.SemaphoreType.DMA((OWNED // 1024,)),
        ],
        "pullback",
    )(back, back_ninth, owner_row, owner_col, image, params)
    return rendered.transpose(1, 0, 2), gradient


def solution(mesh):
    in_specs = (
        P(None, "dev"),
        P("dev", None, None),
        P("dev", None),
        P("dev"),
        P("dev"),
        P("dev", None, None),
    )
    out_specs = (P("dev", None, None), P(None, "dev"))
    return jax.shard_map(local, mesh=mesh, in_specs=in_specs, out_specs=out_specs, check_vma=False)
```

```python
import functools

import jax
import jax.numpy as jnp
from jax import lax
from jax.experimental import pallas as pl
from jax.experimental.pallas import tpu as pltpu
from jax.sharding import PartitionSpec as P

FOCAL = 1200.0
CENTER_X = 960.0
CENTER_Y = 540.0
DILATION = 0.3
BAND_ZERO = 0.28209479177387814
BAND_ONE = 0.4886025119029199
BAND_TWO = (
    1.0925484305920792,
    -1.0925484305920792,
    0.31539156525252005,
    -1.0925484305920792,
    0.5462742152960396,
)
BAND_THREE = (
    -0.5900435899266435,
    2.890611442640554,
    -0.4570457994644658,
    0.3731763325901154,
    -0.4570457994644658,
    1.445305721320277,
    -0.5900435899266435,
)
LOG2_E = 1.4426950408889634

DEVICES = 128
INNER = 8
OUTER = DEVICES // INNER
OWNED = 5120
CAP = 40
PARAMS = 59
BLOCKS = OWNED // 128
TILES = 16
SLOTS = 512
SEG = 46
SEG_PAD = 48
SEGS = 12
GROUP = 8
PASSES = 32 // GROUP
MIDDLE = 4
STEP_UNROLL = 23
BACK_UNROLL = 23
SHORT_UNROLL = 23
BF16 = jnp.bfloat16
MESH_ID = pl.DeviceIdType.MESH
F32 = jnp.float32
I32 = jnp.int32
VMEM_LIMIT = 64 * 1000 * 1000


def project(rows):
    x, y, z = rows[0], rows[1], rows[2]
    scales = [jnp.exp(rows[3 + k]) for k in range(3)]
    norm = jnp.sqrt(rows[6] * rows[6] + rows[7] * rows[7] + rows[8] * rows[8] + rows[9] * rows[9])
    qw, qx, qy, qz = (rows[6 + k] / norm for k in range(4))
    rotation = [
        [1.0 - 2.0 * (qy * qy + qz * qz), 2.0 * (qx * qy - qw * qz), 2.0 * (qx * qz + qw * qy)],
        [2.0 * (qx * qy + qw * qz), 1.0 - 2.0 * (qx * qx + qz * qz), 2.0 * (qy * qz - qw * qx)],
        [2.0 * (qx * qz - qw * qy), 2.0 * (qy * qz + qw * qx), 1.0 - 2.0 * (qx * qx + qy * qy)],
    ]
    spread = [[rotation[i][k] * scales[k] for k in range(3)] for i in range(3)]
    inverse_z = 1.0 / z
    diag = FOCAL * inverse_z
    jac_xz = -FOCAL * x * inverse_z * inverse_z
    jac_yz = -FOCAL * y * inverse_z * inverse_z
    across = [diag * spread[0][k] + jac_xz * spread[2][k] for k in range(3)]
    upward = [diag * spread[1][k] + jac_yz * spread[2][k] for k in range(3)]
    cov_xx = across[0] * across[0] + across[1] * across[1] + across[2] * across[2] + DILATION
    cov_xy = across[0] * upward[0] + across[1] * upward[1] + across[2] * upward[2]
    cov_yy = upward[0] * upward[0] + upward[1] * upward[1] + upward[2] * upward[2] + DILATION
    determinant = cov_xx * cov_yy - cov_xy * cov_xy
    distance = jnp.sqrt(x * x + y * y + z * z)
    fx, fy, fz = x / distance, y / distance, z / distance
    xx, yy, zz = fx * fx, fy * fy, fz * fz
    basis = [
        None,
        -BAND_ONE * fy,
        BAND_ONE * fz,
        -BAND_ONE * fx,
        BAND_TWO[0] * fx * fy,
        BAND_TWO[1] * fy * fz,
        BAND_TWO[2] * (2.0 * zz - xx - yy),
        BAND_TWO[3] * fx * fz,
        BAND_TWO[4] * (xx - yy),
        BAND_THREE[0] * fy * (3.0 * xx - yy),
        BAND_THREE[1] * fx * fy * fz,
        BAND_THREE[2] * fy * (4.0 * zz - xx - yy),
        BAND_THREE[3] * fz * (2.0 * zz - 3.0 * xx - 3.0 * yy),
        BAND_THREE[4] * fx * (4.0 * zz - xx - yy),
        BAND_THREE[5] * fz * (xx - yy),
        BAND_THREE[6] * fx * (xx - 3.0 * yy),
    ]
    colours = []
    for channel in range(3):
        total = BAND_ZERO * rows[11 + channel]
        for k in range(1, 16):
            total = total + basis[k] * rows[11 + 3 * k + channel]
        colours.append(jnp.maximum(total + 0.5, 0.0))
    return [
        FOCAL * x * inverse_z + CENTER_X,
        FOCAL * y * inverse_z + CENTER_Y,
        cov_yy / determinant,
        -cov_xy / determinant,
        cov_xx / determinant,
        1.0 / (1.0 + jnp.exp(-rows[10])),
        *colours,
    ]


def load_rows(params_ref, columns):
    return [params_ref[row : row + 1, columns].reshape(8, 128) for row in range(PARAMS)]


def project_all(params_ref, screen_ref, ninth_ref):
    def one_group(group, carry):
        screen = project(
            load_rows(params_ref, pl.ds(pl.multiple_of(group * 1024, 1024), 1024))
        )
        for row in range(8):
            screen_ref[pl.ds(pl.multiple_of(group * 8, 8), 8), row, :] = screen[row]
        ninth_ref[group] = screen[8]
        return carry

    lax.fori_loop(0, OWNED // 1024, one_group, 0)


def repeat(count, unroll, body, state):
    def turn(index, state):
        for part in range(unroll):
            state = body(index * unroll + part, state)
        return state

    return lax.fori_loop(0, count // unroll, turn, state)


def gather(
    source_ref, ninth_ref, block_ref, lane_ref, out_ref, out_ninth_ref, split_ref,
    targets, sources, by_matmul, by_lanes, parts=3,
):
    half = sources // 2
    eights = half * 8
    height = eights + 24
    width = 128 * by_matmul
    ninth = ninth_ref[...].reshape(-1, 128)
    rest = jnp.concatenate(
        [
            jnp.concatenate([ninth[0:half], ninth[half:sources]], axis=1),
            jnp.zeros((24 - half, 256), F32),
        ],
        axis=0,
    )
    main = jnp.concatenate(
        [
            source_ref[0:half].reshape(eights, 128),
            source_ref[half:sources].reshape(eights, 128),
        ],
        axis=1,
    )
    for part in range(parts):
        for values, start in ((main, 0), (rest, eights)):
            rounded = values.astype(BF16)
            split_ref[part * height + start : part * height + start + values.shape[0]] = rounded
        main = main - main.astype(BF16).astype(F32)
        rest = rest - rest.astype(BF16).astype(F32)
    iota = lax.broadcasted_iota(I32, (256, width), 0).astype(F32).astype(BF16)
    sublane_rest = lax.broadcasted_iota(I32, (24, width), 0)
    sublane = lax.broadcasted_iota(I32, (8, 128), 0)

    def turn(index, carry):
        base = index * (by_matmul + by_lanes)
        rows = [pl.ds(base + k, 1) for k in range(by_matmul)]
        block = jnp.concatenate([block_ref[row, :] for row in rows], axis=1)
        lane = jnp.concatenate([lane_ref[row, :] for row in rows], axis=1)
        upper = jnp.where(block >= half, 1, 0)
        key = jnp.broadcast_to((lane + 128 * upper).astype(F32), (16, width)).astype(BF16)
        place = block - half * upper
        match = jnp.concatenate([key] * 16, axis=0) == iota
        pick = jnp.where(match, jnp.ones((), BF16), jnp.zeros((), BF16))
        products = lax.dot_general(
            split_ref[0 : parts * height], pick, (((1,), (0,)), ((), ())), preferred_element_type=F32
        )
        for k in range(by_lanes):
            row = base + by_matmul + k
            lane = jnp.broadcast_to(lane_ref[pl.ds(row, 1), :], (8, 128))
            block = jnp.broadcast_to(block_ref[pl.ds(row, 1), :], (8, 128))
            total = jnp.zeros((8, 128), F32)
            for source in range(sources):
                picked = jnp.take_along_axis(
                    source_ref[source], lane, axis=1, mode="promise_in_bounds"
                )
                total = jnp.where(block == source, picked, total)
            out_ref[row] = total
            offset = block - sublane
            total = jnp.zeros((8, 128), F32)
            for source in range((sources + 7) // 8):
                picked = jnp.take_along_axis(
                    ninth_ref[source], lane, axis=1, mode="promise_in_bounds"
                )
                total = jnp.where(offset == 8 * source, picked, total)
            out_ninth_ref[pl.ds(row, 1), :] = jnp.sum(total, axis=0, keepdims=True)
        values = products[0:height]
        for part in range(1, parts):
            values = values + products[part * height : (part + 1) * height]
        wide = jnp.broadcast_to(place, (8, width))
        total = jnp.zeros((8, width), F32)
        for source in range(half):
            total = jnp.where(wide == source, values[8 * source : 8 * source + 8], total)
        last = jnp.sum(
            jnp.where(sublane_rest == place, values[eights:height], 0.0), axis=0, keepdims=True
        )
        for k in range(by_matmul):
            out_ref[base + k] = total[:, 128 * k : 128 * k + 128]
            out_ninth_ref[pl.ds(base + k, 1), :] = last[:, 128 * k : 128 * k + 128]
        return carry

    lax.fori_loop(0, targets // (by_matmul + by_lanes), turn, 0)


def invert(block_ref, lane_ref, left_ref, right_ref, row_ref, col_ref, rows, blocks):
    iota_lane = lax.broadcasted_iota(I32, (1, 128), 1).astype(F32)
    iota_block = lax.broadcasted_iota(I32, (blocks, 128), 0)
    iota_sub = lax.broadcasted_iota(I32, (128, 128), 0)

    def one_row(row, carry):
        columns = pl.ds(pl.multiple_of(row * 128, 128), 128)
        here = iota_block == block_ref[pl.ds(row, 1), :]
        value = jnp.full((1, 128), 0.0, F32) + row.astype(F32)
        left_ref[0:blocks, columns] = jnp.where(here, value, 0.0).astype(BF16)
        left_ref[blocks : 2 * blocks, columns] = jnp.where(here, iota_lane, 0.0).astype(
            BF16
        )
        right_ref[:, columns] = jnp.where(
            iota_sub == lane_ref[pl.ds(row, 1), :], 1.0, 0.0
        ).astype(BF16)
        return carry

    repeat(rows, 2, one_row, 0)
    found = lax.dot_general(
        left_ref[...], right_ref[...], (((1,), (1,)), ((), ())), preferred_element_type=F32
    )
    row_ref[...] = (found[0:blocks] + 0.5).astype(I32)
    col_ref[...] = (found[blocks : 2 * blocks] + 0.5).astype(I32)


def pack_messages(rows_ref, ninth_ref, out_ref):
    flat = rows_ref[...].reshape(CAP * 8, 128)
    out_ref[:, 0, :] = flat[0:128].T
    out_ref[:, 1, :] = flat[128:256].T
    last = jnp.concatenate(
        [flat[256:320], ninth_ref[...], jnp.zeros((128 - 64 - CAP, 128), F32)], axis=0
    )
    out_ref[:, 2, :] = last.T


def unpack_messages(message_ref, rows_ref, ninth_ref):
    rows_ref[0:16] = message_ref[:, 0, :].T.reshape(16, 8, 128)
    rows_ref[16:32] = message_ref[:, 1, :].T.reshape(16, 8, 128)
    last = message_ref[:, 2, :].T
    rows_ref[32:40] = last[0:64].reshape(8, 8, 128)
    ninth_ref[...] = last[64 : 64 + CAP].reshape(CAP // 8, 8, 128)


def request_peers(me):
    outer, inner = lax.div(me, INNER), lax.rem(me, INNER)
    near = [outer * INNER + lax.rem(inner + turn, INNER) for turn in range(1, INNER)]
    far = [lax.rem(outer + turn, OUTER) * INNER + inner for turn in range(1, OUTER)]
    return outer, inner, near, far


def greet(me):
    barrier = pltpu.get_barrier_semaphore()
    _, _, near, far = request_peers(me)
    for peer in near + far:
        pl.semaphore_signal(barrier, inc=1, device_id=(peer,), device_id_type=MESH_ID)


def await_greetings():
    pl.semaphore_wait(pltpu.get_barrier_semaphore(), INNER + OUTER - 2)


def send_requests(request_ref, middle_ref, sems, me):
    send_sem, receive_sem, own_sem = sems
    _, inner, near, _ = request_peers(me)
    for peer in near:
        pltpu.make_async_remote_copy(
            src_ref=request_ref.at[lax.rem(peer, INNER)],
            dst_ref=middle_ref.at[inner],
            send_sem=send_sem,
            recv_sem=receive_sem,
            device_id=(peer,),
            device_id_type=MESH_ID,
        ).start()
    pltpu.make_async_copy(request_ref.at[inner], middle_ref.at[inner], own_sem).start()


def forward_requests(request_ref, middle_ref, wanted_ref, first_sems, sems, me):
    first_send, first_receive, first_own = first_sems
    send_sem, receive_sem, own_sem = sems
    outer, inner, _, far = request_peers(me)
    others = pl.ds(0, INNER - 1)
    pltpu.make_async_copy(request_ref.at[inner], middle_ref.at[inner], first_own).wait()
    pltpu.make_async_copy(middle_ref.at[others], middle_ref.at[others], first_receive).wait()
    for peer in far:
        pltpu.make_async_remote_copy(
            src_ref=middle_ref.at[:, lax.div(peer, INNER)],
            dst_ref=wanted_ref.at[outer],
            send_sem=send_sem,
            recv_sem=receive_sem,
            device_id=(peer,),
            device_id_type=MESH_ID,
        ).start()
    pltpu.make_async_copy(middle_ref.at[:, outer], wanted_ref.at[outer], own_sem).start()
    pltpu.make_async_copy(request_ref.at[others], request_ref.at[others], first_send).wait()


def await_requests(middle_ref, wanted_ref, sems, me):
    send_sem, receive_sem, own_sem = sems
    outer = lax.div(me, INNER)
    others = pl.ds(0, OUTER - 1)
    pltpu.make_async_copy(middle_ref.at[:, outer], wanted_ref.at[outer], own_sem).wait()
    pltpu.make_async_copy(wanted_ref.at[others], wanted_ref.at[others], receive_sem).wait()
    pltpu.make_async_copy(wanted_ref.at[others], wanted_ref.at[others], send_sem).wait()


def far_first():
    offsets = [
        (y, x, z, core) for y in range(4) for x in range(4) for z in range(4) for core in range(2)
    ]
    hops = (0, 1, 2, 1)
    offsets.sort(key=lambda o: -(2 * (hops[o[0]] + hops[o[1]] + hops[o[2]]) + o[3]))
    return offsets[:-1]


def send_all(source_ref, landing_ref, send_sem, receive_sem, own_sem, me):
    at_y, at_x = lax.div(me, 32), lax.rem(lax.div(me, 8), 4)
    at_z, at_core = lax.rem(lax.div(me, 2), 4), lax.rem(me, 2)
    to_y = [32 * lax.rem(at_y + turn, 4) for turn in range(4)]
    to_x = [8 * lax.rem(at_x + turn, 4) for turn in range(4)]
    to_z = [2 * lax.rem(at_z + turn, 4) for turn in range(4)]
    to_core = [lax.rem(at_core + turn, 2) for turn in range(2)]
    for y, x, z, core in far_first():
        peer = to_y[y] + to_x[x] + to_z[z] + to_core[core]
        pltpu.make_async_remote_copy(
            src_ref=source_ref.at[peer],
            dst_ref=landing_ref.at[me],
            send_sem=send_sem,
            recv_sem=receive_sem,
            device_id=(peer,),
            device_id_type=MESH_ID,
        ).start()
    pltpu.make_async_copy(source_ref.at[me], landing_ref.at[me], own_sem).start()


def await_all(source_ref, landing_ref, send_sem, receive_sem, own_sem, me):
    others = pl.ds(0, DEVICES - 1)
    pltpu.make_async_copy(source_ref.at[me], landing_ref.at[me], own_sem).wait()
    pltpu.make_async_copy(landing_ref.at[others], landing_ref.at[others], receive_sem).wait()
    pltpu.make_async_copy(source_ref.at[others], source_ref.at[others], send_sem).wait()


def wanted_tables(wanted_ref, block_ref, lane_ref):
    wanted = wanted_ref[:, :, 0, :].reshape(DEVICES, 128).astype(F32).T[0:CAP].astype(I32)
    block_ref[...] = wanted >> 7
    lane_ref[...] = wanted & 127


def lane_map(count_ref, place_ref):
    lane = lax.broadcasted_iota(I32, (1, 128), 1)
    tile = jnp.full((1, 128), -1, I32)
    segment = jnp.zeros((1, 128), I32)
    segments = jnp.zeros((1, 128), I32)
    count = jnp.zeros((1, 128), I32)
    origin_x = jnp.zeros((1, 128), I32)
    origin_y = jnp.zeros((1, 128), I32)
    base = jnp.int32(0)
    for index in range(TILES):
        listed = count_ref[index]
        place = place_ref[index]
        used = lax.div(listed + (SEG - 1), SEG)
        inside = (lane >= base) & (lane < base + used)
        place_y = lax.div(place, 120)
        tile = jnp.where(inside, index, tile)
        segment = jnp.where(inside, lane - base, segment)
        segments = jnp.where(inside, used, segments)
        count = jnp.where(inside, listed, count)
        origin_x = jnp.where(inside, 16 * (place - 120 * place_y), origin_x)
        origin_y = jnp.where(inside, 16 * place_y, origin_y)
        base = base + used
    return tile, segment, segments, count, origin_x, origin_y


def index_tables(
    count_ref, place_ref, slots_ref,
    block_ref, lane_ref, row_ref, col_ref, lanes_ref, all_ref, left_ref, right_ref,
):
    tile, segment, segments, count, origin_x, origin_y = lane_map(count_ref, place_ref)
    lanes_ref[0:1] = tile
    lanes_ref[1:2] = segment
    lanes_ref[2:3] = segments
    lanes_ref[3:4] = count
    lanes_ref[4:5] = origin_x
    lanes_ref[5:6] = origin_y
    lanes_ref[6:8] = jnp.zeros((2, 128), I32)
    slots = slots_ref[...]
    owner = ((slots.astype(F32) + 0.5) * (1.0 / CAP)).astype(I32)
    within = slots - owner * CAP
    pick = jnp.where(
        lax.broadcasted_iota(I32, (TILES, 128), 0) == tile, 1.0, 0.0
    ).astype(BF16)
    contract = (((0,), (0,)), ((), ()))
    step = lax.broadcasted_iota(I32, (SEG_PAD, 128), 0)
    live = (step < SEG) & (step + segment * SEG < count)
    for values, out, unused in ((within, block_ref, -1), (owner, lane_ref, 0)):
        all_ref[0:SLOTS] = lax.dot_general(
            values.astype(F32).astype(BF16), pick, contract, preferred_element_type=F32
        )
        all_ref[SLOTS:] = jnp.zeros_like(all_ref[SLOTS:])
        total = jnp.zeros((SEG_PAD, 128), F32)
        for part in range(SEGS):
            rows = all_ref[part * SEG : part * SEG + SEG_PAD]
            total = jnp.where(segment == part, rows, total)
        out[...] = jnp.where(live, (total + 0.5).astype(I32), unused)
    invert(block_ref, lane_ref, left_ref, right_ref, row_ref, col_ref, SEG, CAP)


def render(
    source_ref, source_ninth_ref, block_ref, lane_ref, row_ref, col_ref, lanes_ref, target_ref,
    rendered_ref, gradient_ref,
    rows_ref, ninth_ref, pre_ref, alpha_ref, weight_ref,
    trans_ref, colour_ref, behind_ref, moment_ref, grad_ref, grad_ninth_ref,
    back_ref, back_ninth_ref, split_ref, split_back_ref,
):
    gather(
        source_ref, source_ninth_ref, block_ref, lane_ref, rows_ref, ninth_ref, split_ref,
        SEG, CAP, 12, 11,
    )
    tile = lanes_ref[0:1]
    segment = lanes_ref[1:2]
    segments = lanes_ref[2:3]
    origin_x = lanes_ref[4:5].astype(F32)
    origin_y = lanes_ref[5:6].astype(F32)
    sub = lax.broadcasted_iota(I32, (8, 128), 0).astype(F32) + 0.5

    def wide(row):
        return jnp.broadcast_to(row, (8, 128))

    def prepare(step, carry):
        attrs = rows_ref[step]
        screen_x = attrs[0:1] - origin_x
        screen_y = attrs[1:2] - origin_y
        curve_x = wide(-0.5 * LOG2_E * attrs[2:3])
        curve_xy = wide(-LOG2_E * attrs[3:4])
        for half in range(2):
            delta = (sub + 8.0 * half) - wide(screen_x)
            pre_ref[step, half] = curve_x * delta * delta
            pre_ref[step, 2 + half] = curve_xy * delta
            pre_ref[step, 9 + half] = delta
        pre_ref[step, 4] = wide(screen_y)
        pre_ref[step, 5] = wide(-0.5 * LOG2_E * attrs[4:5])
        pre_ref[step, 6] = wide(attrs[5:6])
        pre_ref[step, 7] = wide(attrs[6:7])
        pre_ref[step, 8] = wide(attrs[7:8])
        pre_ref[step, 11] = wide(ninth_ref[pl.ds(step, 1), :])
        return carry

    repeat(SEG, SHORT_UNROLL, prepare, 0)

    def place(index):
        half, block = index % 2, index // 2
        rows = [pl.ds((2 * (GROUP * block + k) + half) * 8, 8) for k in range(GROUP)]
        return half, GROUP * block + MIDDLE + 0.5, rows

    for index in range(PASSES):
        half, middle, rows = place(index)

        def one_step(step, state):
            trans, red, green, blue = (list(part) for part in state)
            opacity, curve_y = pre_ref[step, 6], pre_ref[step, 5]
            colours = (pre_ref[step, 7], pre_ref[step, 8], pre_ref[step, 11])
            delta_y = middle - pre_ref[step, 4]
            bend = curve_y * delta_y
            slant = pre_ref[step, 2 + half] + bend
            twice = curve_y + curve_y
            powers = [None] * GROUP
            powers[MIDDLE] = pre_ref[step, half] + slant * delta_y
            slant = slant + bend
            rise, fall = curve_y + slant, curve_y - slant
            for k in range(MIDDLE + 1, GROUP):
                powers[k] = powers[k - 1] + rise
                rise = rise + twice
            for k in range(MIDDLE - 1, -1, -1):
                powers[k] = powers[k + 1] + fall
                fall = fall + twice
            for k in range(GROUP):
                alpha = opacity * jnp.exp2(powers[k])
                weight = alpha * trans[k]
                trans[k] = trans[k] - weight
                red[k] = red[k] + colours[0] * weight
                green[k] = green[k] + colours[1] * weight
                blue[k] = blue[k] + colours[2] * weight
                alpha_ref[index, step, k] = alpha
                weight_ref[index, step, k] = weight
            return tuple(trans), tuple(red), tuple(green), tuple(blue)

        ones = tuple(jnp.ones((8, 128), F32) for _ in range(GROUP))
        zeros = tuple(jnp.zeros((8, 128), F32) for _ in range(GROUP))
        state = repeat(SEG, STEP_UNROLL, one_step, (ones, zeros, zeros, zeros))
        for k in range(GROUP):
            trans_ref[rows[k], :] = state[0][k]
            for channel in range(3):
                colour_ref[channel, rows[k], :] = state[1 + channel][k]

    through = trans_ref[...]
    start = jnp.where(segment == 0, 1.0, pltpu.roll(through, 1, 1))
    for shift in (1, 2, 4, 8):
        start = start * jnp.where(segment >= shift, pltpu.roll(start, shift, 1), 1.0)
    pick = jnp.where(lax.broadcasted_iota(I32, (TILES, 128), 0) == tile, 1.0, 0.0)
    colours = [colour_ref[channel] for channel in range(3)]
    images = lax.dot_general(
        pick, jnp.concatenate([colour * start for colour in colours], axis=0),
        (((1,), (1,)), ((), ())),
        preferred_element_type=F32, precision=lax.Precision.HIGHEST,
    )
    errors = []
    for channel in range(3):
        image = images[:, 256 * channel : 256 * channel + 256]
        rendered_ref[channel] = image
        errors.append((image - target_ref[channel]) * (1.0 / 256.0))
    spread = lax.dot_general(
        jnp.concatenate(errors, axis=1), pick, (((0,), (0,)), ((), ())),
        preferred_element_type=F32, precision=lax.Precision.HIGHEST,
    )
    behind = jnp.zeros((256, 128), F32)
    for channel in range(3):
        part = spread[256 * channel : 256 * channel + 256]
        behind = behind + part * colours[channel]
        colour_ref[channel] = part * start
    left = segments - 1 - segment
    factor = jnp.where(left >= 1, pltpu.roll(through, 127, 1), 0.0)
    behind = jnp.where(left >= 1, pltpu.roll(behind, 127, 1), 0.0)
    for shift in (1, 2, 4, 8):
        reach = left >= shift
        behind = behind + factor * jnp.where(reach, pltpu.roll(behind, 128 - shift, 1), 0.0)
        factor = factor * jnp.where(reach, pltpu.roll(factor, 128 - shift, 1), 0.0)
    behind_ref[...] = behind * start

    for index in range(PASSES):
        half, middle, rows = place(index)
        errors = [[colour_ref[channel, rows[k], :] for channel in range(3)] for k in range(GROUP)]

        def one_step(count, state):
            step = SEG - 1 - count
            state = list(state)
            colours = (pre_ref[step, 7], pre_ref[step, 8], pre_ref[step, 11])
            slopes = [None] * GROUP
            shares = [None, None, None]
            for k in range(GROUP):
                alpha = alpha_ref[index, step, k]
                weight = weight_ref[index, step, k]
                shade = (
                    colours[0] * errors[k][0]
                    + colours[1] * errors[k][1]
                    + colours[2] * errors[k][2]
                )
                gap = shade - state[k]
                state[k] = state[k] + alpha * gap
                slopes[k] = weight * gap
                for channel in range(3):
                    part = weight * errors[k][channel]
                    shares[channel] = part if k == 0 else shares[channel] + part
            flat = tilt = bend = None
            for order in (range(GROUP - 1, MIDDLE, -1), range(MIDDLE)):
                first = second = third = None
                for k in order:
                    first = slopes[k] if first is None else first + slopes[k]
                    second = first if second is None else second + first
                    third = second if third is None else third + second
                square = (third + third) - second
                flat = first if flat is None else flat + first
                bend = square if bend is None else bend + square
                tilt = second if tilt is None else tilt - second
            flat = flat + slopes[MIDDLE]
            delta_y = middle - pre_ref[step, 4]
            moved = tilt + delta_y * flat
            bend = bend + delta_y * (tilt + moved)
            for row, value, started in (
                (3 * half, flat, index > 1),
                (3 * half + 1, moved, index > 1),
                (3 * half + 2, bend, index > 1),
                (6, shares[0], index > 0),
                (7, shares[1], index > 0),
                (8, shares[2], index > 0),
            ):
                moment_ref[step, row] = moment_ref[step, row] + value if started else value
            return tuple(state)

        repeat(
            SEG, BACK_UNROLL, one_step, tuple(behind_ref[rows[k], :] for k in range(GROUP))
        )

    def finish(step, carry):
        delta = [pre_ref[step, 9], pre_ref[step, 10]]
        sums = [moment_ref[step, row] for row in range(9)]
        flat = [sums[0], sums[3]]
        tilt = [sums[1], sums[4]]
        bend = [sums[2], sums[5]]
        side = [flat[half] * delta[half] for half in range(2)]

        def total(register):
            return jnp.sum(register, axis=0, keepdims=True)

        m00 = total(flat[0] + flat[1])
        m10 = total(side[0] + side[1])
        m01 = total(tilt[0] + tilt[1])
        m20 = total(side[0] * delta[0] + side[1] * delta[1])
        m11 = total(tilt[0] * delta[0] + tilt[1] * delta[1])
        m02 = total(bend[0] + bend[1])
        attrs = rows_ref[step]
        conic_a, conic_b, conic_c = attrs[2:3], attrs[3:4], attrs[4:5]
        grad_ref[step] = jnp.concatenate(
            [
                conic_a * m10 + conic_b * m01,
                conic_b * m10 + conic_c * m01,
                -0.5 * m20,
                -m11,
                -0.5 * m02,
                m00,
                total(sums[6]),
                total(sums[7]),
            ],
            axis=0,
        )
        ninth_ref[pl.ds(step, 1), :] = total(sums[8])
        return carry

    repeat(SEG, SHORT_UNROLL, finish, 0)
    ninth_ref[SEG:SEG_PAD] = jnp.zeros((SEG_PAD - SEG, 128), F32)
    grad_ninth_ref[...] = ninth_ref[...].reshape(SEG_PAD // 8, 8, 128)
    gather(
        grad_ref, grad_ninth_ref, row_ref, col_ref, back_ref, back_ninth_ref, split_back_ref,
        CAP, SEG, 10, 10, 2,
    )
    pack_messages(back_ref, back_ninth_ref, gradient_ref)


def step_kernel(
    requests_ref, params_ref, count_ref, place_ref, slots_ref, target_ref,
    far_rendered_ref, reply_landing_ref, far_owner_row_ref, far_owner_col_ref,
    rendered_ref, owner_row_ref, owner_col_ref, store_sem,
    here_requests_ref, here_params_ref, here_count_ref, here_place_ref, here_slots_ref,
    here_target_ref, load_sem,
    request_ref, middle_ref, wanted_ref, wanted_block_ref, wanted_lane_ref,
    near_send, near_receive, near_own, far_send, far_receive, far_own,
    screen_ref, ninth_ref, out_ref, out_ninth_ref, split_ref, left_ref, right_ref,
    all_ref, slot_left_ref, slot_right_ref, block_ref, lane_ref, row_ref, col_ref, lanes_ref,
    message_ref, landing_ref, send_sem, receive_sem, own_sem, source_ref, source_ninth_ref,
    reply_ref, reply_send, reply_receive, reply_own,
    *render_refs,
):
    me = lax.axis_index("dev")
    loads = [
        pltpu.make_async_copy(far, near, load_sem.at[index])
        for index, (far, near) in enumerate(
            (
                (requests_ref, here_requests_ref),
                (params_ref, here_params_ref),
                (count_ref, here_count_ref),
                (place_ref, here_place_ref),
                (slots_ref, here_slots_ref),
                (target_ref, here_target_ref),
            )
        )
    ]
    for load in loads:
        load.start()
    greet(me)
    loads[0].wait()
    wide = jnp.concatenate(
        [here_requests_ref[...].astype(F32), jnp.zeros((128 - CAP, DEVICES), F32)], axis=0
    )
    by_device = wide.T.astype(I32).reshape(OUTER, INNER, 128)
    for inner in range(INNER):
        request_ref[inner, :, 0, :] = by_device[:, inner, :]
    await_greetings()
    near_sems = (near_send, near_receive, near_own)
    far_sems = (far_send, far_receive, far_own)
    send_requests(request_ref, middle_ref, near_sems, me)
    for load in loads[1:]:
        load.wait()
    project_all(here_params_ref, screen_ref, ninth_ref)
    forward_requests(request_ref, middle_ref, wanted_ref, near_sems, far_sems, me)
    index_tables(
        here_count_ref, here_place_ref, here_slots_ref,
        block_ref, lane_ref, row_ref, col_ref, lanes_ref, all_ref, slot_left_ref, slot_right_ref,
    )
    await_requests(middle_ref, wanted_ref, far_sems, me)
    wanted_tables(wanted_ref, wanted_block_ref, wanted_lane_ref)
    gather(
        screen_ref, ninth_ref, wanted_block_ref, wanted_lane_ref, out_ref, out_ninth_ref,
        split_ref, CAP, BLOCKS, 10, 10,
    )
    pack_messages(out_ref, out_ninth_ref, message_ref)
    sems = (send_sem, receive_sem, own_sem, me)
    send_all(message_ref, landing_ref, *sems)
    invert(
        wanted_block_ref, wanted_lane_ref, left_ref, right_ref, owner_row_ref, owner_col_ref,
        CAP, BLOCKS,
    )
    await_all(message_ref, landing_ref, *sems)
    unpack_messages(landing_ref, source_ref, source_ninth_ref)
    render(
        source_ref, source_ninth_ref, block_ref, lane_ref, row_ref, col_ref, lanes_ref,
        here_target_ref, rendered_ref, reply_ref, *render_refs,
    )
    reply_sems = (reply_send, reply_receive, reply_own, me)
    send_all(reply_ref, reply_landing_ref, *reply_sems)
    stores = [
        pltpu.make_async_copy(near, far, store_sem.at[index])
        for index, (near, far) in enumerate(
            (
                (rendered_ref, far_rendered_ref),
                (owner_row_ref, far_owner_row_ref),
                (owner_col_ref, far_owner_col_ref),
            )
        )
    ]
    for store in stores:
        store.start()
    await_all(reply_ref, reply_landing_ref, *reply_sems)
    for store in stores:
        store.wait()


def pullback_kernel(
    far_message_ref, far_row_ref, far_col_ref, image_ref, params_ref,
    rendered_ref, gradient_ref,
    message_ref, source_ref, source_ninth_ref, row_ref, col_ref,
    rows_ref, ninth_ref, split_ref, here_params_ref, here_gradient_ref, load_sem, store_sem,
):
    loads = [
        pltpu.make_async_copy(far, near, load_sem.at[index])
        for index, (far, near) in enumerate(
            (
                (far_message_ref, message_ref),
                (far_row_ref, row_ref),
                (far_col_ref, col_ref),
                (params_ref, here_params_ref),
                (image_ref, rendered_ref),
            )
        )
    ]
    for load in loads:
        load.start()
    for load in loads[:3]:
        load.wait()
    unpack_messages(message_ref, source_ref, source_ninth_ref)
    gather(
        source_ref, source_ninth_ref, row_ref, col_ref, rows_ref, ninth_ref, split_ref,
        BLOCKS, CAP, 10, 10, 2,
    )
    loads[3].wait()
    stores = []
    for group in range(OWNED // 1024):
        columns = pl.ds(group * 1024, 1024)
        eight = pl.ds(group * 8, 8)
        rows = load_rows(here_params_ref, columns)
        screen_grad = [rows_ref[eight, row, :] for row in range(8)] + [ninth_ref[eight, :]]
        screen, pullback = jax.vjp(project, rows)
        by_logit = screen_grad[5] * (1.0 / (1.0 + jnp.exp(rows[10])))
        screen_grad[5] = jnp.zeros_like(by_logit)
        (grads,) = pullback(screen_grad)
        grads[10] = by_logit
        for row in range(PARAMS):
            here_gradient_ref[row : row + 1, columns] = grads[row].reshape(1, 1024)
        stores.append(
            pltpu.make_async_copy(
                here_gradient_ref.at[:, columns], gradient_ref.at[:, columns], store_sem.at[group]
            )
        )
        stores[-1].start()
    for store in stores:
        store.wait()
    loads[4].wait()


def shape(dims, dtype=F32):
    return jax.ShapeDtypeStruct(dims, dtype)


def call(kernel, outs, specs, out_specs, scratch, name, collective=None):
    params = {"vmem_limit_bytes": VMEM_LIMIT}
    if collective is not None:
        params.update(collective_id=collective, has_side_effects=True)
    spaces = {"v": pltpu.VMEM, "s": pltpu.SMEM, "h": pltpu.HBM}
    return pl.pallas_call(
        kernel,
        out_shape=outs,
        in_specs=[pl.BlockSpec(memory_space=spaces[kind]) for kind in specs],
        out_specs=[pl.BlockSpec(memory_space=spaces[kind]) for kind in out_specs],
        scratch_shapes=scratch,
        compiler_params=pltpu.CompilerParams(**params),
        name=name,
    )


SPLIT = (3 * (CAP // 2 * 8 + 24), 256)
SPLIT_BACK = (3 * (SEG // 2 * 8 + 24), 256)
MESSAGE = (DEVICES, 3, 128)
TABLE = (CAP, 128)
STEPS = (SEG_PAD, 128)
EIGHT = (CAP, 8, 128)
NINE = (CAP // 8, 8, 128)


IMAGE = (3, TILES, 256)


def local(params, requests, tile_slots, tile_count, tile_place, target):
    vmem = pltpu.VMEM
    sems = [pltpu.SemaphoreType.DMA] * 3
    image, replies, owner_row, owner_col = call(
        step_kernel,
        [shape(IMAGE), shape(MESSAGE), shape(TABLE, I32), shape(TABLE, I32)],
        "hhhhhh",
        "hhhh",
        [
            vmem(IMAGE, F32), vmem(TABLE, I32), vmem(TABLE, I32), pltpu.SemaphoreType.DMA((3,)),
            vmem((CAP, DEVICES), I32), vmem((PARAMS, OWNED), F32),
            pltpu.SMEM((TILES,), I32), pltpu.SMEM((TILES,), I32), vmem((TILES, SLOTS), I32),
            vmem(IMAGE, F32), pltpu.SemaphoreType.DMA((6,)),
            vmem((INNER, OUTER, 1, 128), I32), vmem((INNER, OUTER, 1, 128), I32),
            vmem((OUTER, INNER, 1, 128), I32), vmem(TABLE, I32), vmem(TABLE, I32), *sems, *sems,
            vmem(EIGHT, F32), vmem(NINE, F32), vmem(EIGHT, F32), vmem(TABLE, F32),
            vmem(SPLIT, BF16),
            vmem((2 * BLOCKS, CAP * 128), BF16), vmem((128, CAP * 128), BF16),
            vmem((SEGS * SEG + 8, 128), F32),
            vmem((2 * CAP, SEG * 128), BF16), vmem((128, SEG * 128), BF16),
            vmem(STEPS, I32), vmem(STEPS, I32), vmem(TABLE, I32), vmem(TABLE, I32),
            vmem((8, 128), I32),
            vmem(MESSAGE, F32), vmem(MESSAGE, F32), *sems, vmem(EIGHT, F32), vmem(NINE, F32),
            vmem(MESSAGE, F32), *sems,
            vmem((SEG, 8, 128), F32), vmem(STEPS, F32),
            vmem((SEG, 12, 8, 128), F32),
            vmem((PASSES, SEG, GROUP, 8, 128), F32), vmem((PASSES, SEG, GROUP, 8, 128), F32),
            vmem((256, 128), F32), vmem((3, 256, 128), F32), vmem((256, 128), F32),
            vmem((SEG, 9, 8, 128), F32),
            vmem((SEG, 8, 128), F32), vmem((SEG_PAD // 8, 8, 128), F32),
            vmem(EIGHT, F32), vmem(TABLE, F32), vmem(SPLIT, BF16), vmem(SPLIT_BACK, BF16),
        ],
        "step",
        0,
    )(
        requests.reshape(DEVICES, CAP).T, params, tile_count, tile_place, tile_slots,
        target.transpose(1, 0, 2),
    )
    rendered, gradient = call(
        pullback_kernel,
        [shape(IMAGE), shape((PARAMS, OWNED))],
        "hhhhh",
        "hh",
        [
            vmem(MESSAGE, F32), vmem(EIGHT, F32), vmem(NINE, F32), vmem(TABLE, I32), vmem(TABLE, I32),
            vmem(EIGHT, F32), vmem(TABLE, F32), vmem(SPLIT, BF16), vmem((PARAMS, OWNED), F32),
            vmem((PARAMS, OWNED), F32), pltpu.SemaphoreType.DMA((5,)),
            pltpu.SemaphoreType.DMA((OWNED // 1024,)),
        ],
        "pullback",
    )(replies, owner_row, owner_col, image, params)
    return rendered.transpose(1, 0, 2), gradient


def solution(mesh):
    in_specs = (
        P(None, "dev"),
        P("dev", None, None),
        P("dev", None),
        P("dev"),
        P("dev"),
        P("dev", None, None),
    )
    out_specs = (P("dev", None, None), P(None, "dev"))
    return jax.shard_map(local, mesh=mesh, in_specs=in_specs, out_specs=out_specs, check_vma=False)
```

```python
import functools

import jax
import jax.numpy as jnp
from jax import lax
from jax.experimental import pallas as pl
from jax.experimental.pallas import tpu as pltpu
from jax.sharding import PartitionSpec as P

FOCAL = 1200.0
CENTER_X = 960.0
CENTER_Y = 540.0
DILATION = 0.3
BAND_ZERO = 0.28209479177387814
BAND_ONE = 0.4886025119029199
BAND_TWO = (
    1.0925484305920792,
    -1.0925484305920792,
    0.31539156525252005,
    -1.0925484305920792,
    0.5462742152960396,
)
BAND_THREE = (
    -0.5900435899266435,
    2.890611442640554,
    -0.4570457994644658,
    0.3731763325901154,
    -0.4570457994644658,
    1.445305721320277,
    -0.5900435899266435,
)
LOG2_E = 1.4426950408889634

DEVICES = 128
INNER = 8
OUTER = DEVICES // INNER
OWNED = 5120
CAP = 40
PARAMS = 59
BLOCKS = OWNED // 128
TILES = 16
SLOTS = 512
SEG = 46
SEG_PAD = 48
SEGS = 12
GROUP = 8
PASSES = 32 // GROUP
MIDDLE = 4
STEP_UNROLL = 23
BACK_UNROLL = 23
SHORT_UNROLL = 23
BF16 = jnp.bfloat16
MESH_ID = pl.DeviceIdType.MESH
F32 = jnp.float32
I32 = jnp.int32
VMEM_LIMIT = 64 * 1000 * 1000


def project(rows):
    x, y, z = rows[0], rows[1], rows[2]
    scales = [jnp.exp(rows[3 + k]) for k in range(3)]
    norm = jnp.sqrt(rows[6] * rows[6] + rows[7] * rows[7] + rows[8] * rows[8] + rows[9] * rows[9])
    qw, qx, qy, qz = (rows[6 + k] / norm for k in range(4))
    rotation = [
        [1.0 - 2.0 * (qy * qy + qz * qz), 2.0 * (qx * qy - qw * qz), 2.0 * (qx * qz + qw * qy)],
        [2.0 * (qx * qy + qw * qz), 1.0 - 2.0 * (qx * qx + qz * qz), 2.0 * (qy * qz - qw * qx)],
        [2.0 * (qx * qz - qw * qy), 2.0 * (qy * qz + qw * qx), 1.0 - 2.0 * (qx * qx + qy * qy)],
    ]
    spread = [[rotation[i][k] * scales[k] for k in range(3)] for i in range(3)]
    inverse_z = 1.0 / z
    diag = FOCAL * inverse_z
    jac_xz = -FOCAL * x * inverse_z * inverse_z
    jac_yz = -FOCAL * y * inverse_z * inverse_z
    across = [diag * spread[0][k] + jac_xz * spread[2][k] for k in range(3)]
    upward = [diag * spread[1][k] + jac_yz * spread[2][k] for k in range(3)]
    cov_xx = across[0] * across[0] + across[1] * across[1] + across[2] * across[2] + DILATION
    cov_xy = across[0] * upward[0] + across[1] * upward[1] + across[2] * upward[2]
    cov_yy = upward[0] * upward[0] + upward[1] * upward[1] + upward[2] * upward[2] + DILATION
    determinant = cov_xx * cov_yy - cov_xy * cov_xy
    distance = jnp.sqrt(x * x + y * y + z * z)
    fx, fy, fz = x / distance, y / distance, z / distance
    xx, yy, zz = fx * fx, fy * fy, fz * fz
    basis = [
        None,
        -BAND_ONE * fy,
        BAND_ONE * fz,
        -BAND_ONE * fx,
        BAND_TWO[0] * fx * fy,
        BAND_TWO[1] * fy * fz,
        BAND_TWO[2] * (2.0 * zz - xx - yy),
        BAND_TWO[3] * fx * fz,
        BAND_TWO[4] * (xx - yy),
        BAND_THREE[0] * fy * (3.0 * xx - yy),
        BAND_THREE[1] * fx * fy * fz,
        BAND_THREE[2] * fy * (4.0 * zz - xx - yy),
        BAND_THREE[3] * fz * (2.0 * zz - 3.0 * xx - 3.0 * yy),
        BAND_THREE[4] * fx * (4.0 * zz - xx - yy),
        BAND_THREE[5] * fz * (xx - yy),
        BAND_THREE[6] * fx * (xx - 3.0 * yy),
    ]
    colours = []
    for channel in range(3):
        total = BAND_ZERO * rows[11 + channel]
        for k in range(1, 16):
            total = total + basis[k] * rows[11 + 3 * k + channel]
        colours.append(jnp.maximum(total + 0.5, 0.0))
    return [
        FOCAL * x * inverse_z + CENTER_X,
        FOCAL * y * inverse_z + CENTER_Y,
        cov_yy / determinant,
        -cov_xy / determinant,
        cov_xx / determinant,
        1.0 / (1.0 + jnp.exp(-rows[10])),
        *colours,
    ]


def load_rows(params_ref, columns):
    return [params_ref[row : row + 1, columns].reshape(8, 128) for row in range(PARAMS)]


def project_all(params_ref, screen_ref, ninth_ref):
    def one_group(group, carry):
        screen = project(
            load_rows(params_ref, pl.ds(pl.multiple_of(group * 1024, 1024), 1024))
        )
        for row in range(8):
            screen_ref[pl.ds(pl.multiple_of(group * 8, 8), 8), row, :] = screen[row]
        ninth_ref[group] = screen[8]
        return carry

    lax.fori_loop(0, OWNED // 1024, one_group, 0)


def repeat(count, unroll, body, state):
    def turn(index, state):
        for part in range(unroll):
            state = body(index * unroll + part, state)
        return state

    return lax.fori_loop(0, count // unroll, turn, state)


def gather(
    source_ref, ninth_ref, block_ref, lane_ref, out_ref, out_ninth_ref, split_ref,
    targets, sources, by_matmul, by_lanes, parts=3,
):
    half = sources // 2
    eights = half * 8
    height = eights + 24
    width = 128 * by_matmul
    ninth = ninth_ref[...].reshape(-1, 128)
    rest = jnp.concatenate(
        [
            jnp.concatenate([ninth[0:half], ninth[half:sources]], axis=1),
            jnp.zeros((24 - half, 256), F32),
        ],
        axis=0,
    )
    main = jnp.concatenate(
        [
            source_ref[0:half].reshape(eights, 128),
            source_ref[half:sources].reshape(eights, 128),
        ],
        axis=1,
    )
    for part in range(parts):
        for values, start in ((main, 0), (rest, eights)):
            rounded = values.astype(BF16)
            split_ref[part * height + start : part * height + start + values.shape[0]] = rounded
        main = main - main.astype(BF16).astype(F32)
        rest = rest - rest.astype(BF16).astype(F32)
    iota = lax.broadcasted_iota(I32, (256, width), 0).astype(F32).astype(BF16)
    sublane_rest = lax.broadcasted_iota(I32, (24, width), 0)
    sublane = lax.broadcasted_iota(I32, (8, 128), 0)

    def turn(index, carry):
        base = index * (by_matmul + by_lanes)
        rows = [pl.ds(base + k, 1) for k in range(by_matmul)]
        block = jnp.concatenate([block_ref[row, :] for row in rows], axis=1)
        lane = jnp.concatenate([lane_ref[row, :] for row in rows], axis=1)
        upper = jnp.where(block >= half, 1, 0)
        key = jnp.broadcast_to((lane + 128 * upper).astype(F32), (16, width)).astype(BF16)
        place = block - half * upper
        match = jnp.concatenate([key] * 16, axis=0) == iota
        pick = jnp.where(match, jnp.ones((), BF16), jnp.zeros((), BF16))
        products = lax.dot_general(
            split_ref[0 : parts * height], pick, (((1,), (0,)), ((), ())), preferred_element_type=F32
        )
        for k in range(by_lanes):
            row = base + by_matmul + k
            lane = jnp.broadcast_to(lane_ref[pl.ds(row, 1), :], (8, 128))
            block = jnp.broadcast_to(block_ref[pl.ds(row, 1), :], (8, 128))
            total = jnp.zeros((8, 128), F32)
            for source in range(sources):
                picked = jnp.take_along_axis(
                    source_ref[source], lane, axis=1, mode="promise_in_bounds"
                )
                total = jnp.where(block == source, picked, total)
            out_ref[row] = total
            offset = block - sublane
            total = jnp.zeros((8, 128), F32)
            for source in range((sources + 7) // 8):
                picked = jnp.take_along_axis(
                    ninth_ref[source], lane, axis=1, mode="promise_in_bounds"
                )
                total = jnp.where(offset == 8 * source, picked, total)
            out_ninth_ref[pl.ds(row, 1), :] = jnp.sum(total, axis=0, keepdims=True)
        values = products[0:height]
        for part in range(1, parts):
            values = values + products[part * height : (part + 1) * height]
        wide = jnp.broadcast_to(place, (8, width))
        total = jnp.zeros((8, width), F32)
        for source in range(half):
            total = jnp.where(wide == source, values[8 * source : 8 * source + 8], total)
        last = jnp.sum(
            jnp.where(sublane_rest == place, values[eights:height], 0.0), axis=0, keepdims=True
        )
        for k in range(by_matmul):
            out_ref[base + k] = total[:, 128 * k : 128 * k + 128]
            out_ninth_ref[pl.ds(base + k, 1), :] = last[:, 128 * k : 128 * k + 128]
        return carry

    lax.fori_loop(0, targets // (by_matmul + by_lanes), turn, 0)


def invert(block_ref, lane_ref, left_ref, right_ref, row_ref, col_ref, rows, blocks):
    iota_lane = lax.broadcasted_iota(I32, (1, 128), 1).astype(F32)
    iota_block = lax.broadcasted_iota(I32, (blocks, 128), 0)
    iota_sub = lax.broadcasted_iota(I32, (128, 128), 0)

    def one_row(row, carry):
        columns = pl.ds(pl.multiple_of(row * 128, 128), 128)
        here = iota_block == block_ref[pl.ds(row, 1), :]
        value = jnp.full((1, 128), 0.0, F32) + row.astype(F32)
        left_ref[0:blocks, columns] = jnp.where(here, value, 0.0).astype(BF16)
        left_ref[blocks : 2 * blocks, columns] = jnp.where(here, iota_lane, 0.0).astype(
            BF16
        )
        right_ref[:, columns] = jnp.where(
            iota_sub == lane_ref[pl.ds(row, 1), :], 1.0, 0.0
        ).astype(BF16)
        return carry

    repeat(rows, 2, one_row, 0)
    found = lax.dot_general(
        left_ref[...], right_ref[...], (((1,), (1,)), ((), ())), preferred_element_type=F32
    )
    row_ref[...] = (found[0:blocks] + 0.5).astype(I32)
    col_ref[...] = (found[blocks : 2 * blocks] + 0.5).astype(I32)


def pack_messages(rows_ref, ninth_ref, out_ref):
    flat = rows_ref[...].reshape(CAP * 8, 128)
    out_ref[:, 0, :] = flat[0:128].T
    out_ref[:, 1, :] = flat[128:256].T
    last = jnp.concatenate(
        [flat[256:320], ninth_ref[...], jnp.zeros((128 - 64 - CAP, 128), F32)], axis=0
    )
    out_ref[:, 2, :] = last.T


def unpack_messages(message_ref, rows_ref, ninth_ref):
    rows_ref[0:16] = message_ref[:, 0, :].T.reshape(16, 8, 128)
    rows_ref[16:32] = message_ref[:, 1, :].T.reshape(16, 8, 128)
    last = message_ref[:, 2, :].T
    rows_ref[32:40] = last[0:64].reshape(8, 8, 128)
    ninth_ref[...] = last[64 : 64 + CAP].reshape(CAP // 8, 8, 128)


def request_peers(me):
    outer, inner = lax.div(me, INNER), lax.rem(me, INNER)
    near = [outer * INNER + lax.rem(inner + turn, INNER) for turn in range(1, INNER)]
    far = [lax.rem(outer + turn, OUTER) * INNER + inner for turn in range(1, OUTER)]
    return outer, inner, near, far


def greet(me):
    barrier = pltpu.get_barrier_semaphore()
    _, _, near, far = request_peers(me)
    for peer in near + far:
        pl.semaphore_signal(barrier, inc=1, device_id=(peer,), device_id_type=MESH_ID)


def await_greetings():
    pl.semaphore_wait(pltpu.get_barrier_semaphore(), INNER + OUTER - 2)


def send_requests(request_ref, middle_ref, sems, me):
    send_sem, receive_sem, own_sem = sems
    _, inner, near, _ = request_peers(me)
    for peer in near:
        pltpu.make_async_remote_copy(
            src_ref=request_ref.at[lax.rem(peer, INNER)],
            dst_ref=middle_ref.at[inner],
            send_sem=send_sem,
            recv_sem=receive_sem,
            device_id=(peer,),
            device_id_type=MESH_ID,
        ).start()
    pltpu.make_async_copy(request_ref.at[inner], middle_ref.at[inner], own_sem).start()


def forward_requests(request_ref, middle_ref, wanted_ref, first_sems, sems, me):
    first_send, first_receive, first_own = first_sems
    send_sem, receive_sem, own_sem = sems
    outer, inner, _, far = request_peers(me)
    others = pl.ds(0, INNER - 1)
    pltpu.make_async_copy(request_ref.at[inner], middle_ref.at[inner], first_own).wait()
    pltpu.make_async_copy(middle_ref.at[others], middle_ref.at[others], first_receive).wait()
    for peer in far:
        pltpu.make_async_remote_copy(
            src_ref=middle_ref.at[:, lax.div(peer, INNER)],
            dst_ref=wanted_ref.at[outer],
            send_sem=send_sem,
            recv_sem=receive_sem,
            device_id=(peer,),
            device_id_type=MESH_ID,
        ).start()
    pltpu.make_async_copy(middle_ref.at[:, outer], wanted_ref.at[outer], own_sem).start()
    pltpu.make_async_copy(request_ref.at[others], request_ref.at[others], first_send).wait()


def await_requests(middle_ref, wanted_ref, sems, me):
    send_sem, receive_sem, own_sem = sems
    outer = lax.div(me, INNER)
    others = pl.ds(0, OUTER - 1)
    pltpu.make_async_copy(middle_ref.at[:, outer], wanted_ref.at[outer], own_sem).wait()
    pltpu.make_async_copy(wanted_ref.at[others], wanted_ref.at[others], receive_sem).wait()
    pltpu.make_async_copy(wanted_ref.at[others], wanted_ref.at[others], send_sem).wait()


def far_first():
    offsets = [
        (y, x, z, core) for y in range(4) for x in range(4) for z in range(4) for core in range(2)
    ]
    hops = (0, 1, 2, 1)
    offsets.sort(key=lambda o: -(2 * (hops[o[0]] + hops[o[1]] + hops[o[2]]) + o[3]))
    return offsets[:-1]


def send_all(source_ref, landing_ref, send_sem, receive_sem, own_sem, me):
    at_y, at_x = lax.div(me, 32), lax.rem(lax.div(me, 8), 4)
    at_z, at_core = lax.rem(lax.div(me, 2), 4), lax.rem(me, 2)
    to_y = [32 * lax.rem(at_y + turn, 4) for turn in range(4)]
    to_x = [8 * lax.rem(at_x + turn, 4) for turn in range(4)]
    to_z = [2 * lax.rem(at_z + turn, 4) for turn in range(4)]
    to_core = [lax.rem(at_core + turn, 2) for turn in range(2)]
    for y, x, z, core in far_first():
        peer = to_y[y] + to_x[x] + to_z[z] + to_core[core]
        pltpu.make_async_remote_copy(
            src_ref=source_ref.at[peer],
            dst_ref=landing_ref.at[me],
            send_sem=send_sem,
            recv_sem=receive_sem,
            device_id=(peer,),
            device_id_type=MESH_ID,
        ).start()
    pltpu.make_async_copy(source_ref.at[me], landing_ref.at[me], own_sem).start()


def await_all(source_ref, landing_ref, send_sem, receive_sem, own_sem, me):
    others = pl.ds(0, DEVICES - 1)
    pltpu.make_async_copy(source_ref.at[me], landing_ref.at[me], own_sem).wait()
    pltpu.make_async_copy(landing_ref.at[others], landing_ref.at[others], receive_sem).wait()
    pltpu.make_async_copy(source_ref.at[others], source_ref.at[others], send_sem).wait()


def wanted_tables(wanted_ref, block_ref, lane_ref):
    wanted = wanted_ref[:, :, 0, :].reshape(DEVICES, 128).astype(F32).T[0:CAP].astype(I32)
    block_ref[...] = wanted >> 7
    lane_ref[...] = wanted & 127


def lane_map(count_ref, place_ref):
    lane = lax.broadcasted_iota(I32, (1, 128), 1)
    tile = jnp.full((1, 128), -1, I32)
    segment = jnp.zeros((1, 128), I32)
    segments = jnp.zeros((1, 128), I32)
    count = jnp.zeros((1, 128), I32)
    origin_x = jnp.zeros((1, 128), I32)
    origin_y = jnp.zeros((1, 128), I32)
    base = jnp.int32(0)
    for index in range(TILES):
        listed = count_ref[index]
        place = place_ref[index]
        used = lax.div(listed + (SEG - 1), SEG)
        inside = (lane >= base) & (lane < base + used)
        place_y = lax.div(place, 120)
        tile = jnp.where(inside, index, tile)
        segment = jnp.where(inside, lane - base, segment)
        segments = jnp.where(inside, used, segments)
        count = jnp.where(inside, listed, count)
        origin_x = jnp.where(inside, 16 * (place - 120 * place_y), origin_x)
        origin_y = jnp.where(inside, 16 * place_y, origin_y)
        base = base + used
    return tile, segment, segments, count, origin_x, origin_y


def index_tables(
    count_ref, place_ref, slots_ref,
    block_ref, lane_ref, row_ref, col_ref, lanes_ref, all_ref, left_ref, right_ref,
):
    tile, segment, segments, count, origin_x, origin_y = lane_map(count_ref, place_ref)
    lanes_ref[0:1] = tile
    lanes_ref[1:2] = segment
    lanes_ref[2:3] = segments
    lanes_ref[3:4] = count
    lanes_ref[4:5] = origin_x
    lanes_ref[5:6] = origin_y
    lanes_ref[6:8] = jnp.zeros((2, 128), I32)
    slots = slots_ref[...]
    owner = ((slots.astype(F32) + 0.5) * (1.0 / CAP)).astype(I32)
    within = slots - owner * CAP
    pick = jnp.where(
        lax.broadcasted_iota(I32, (TILES, 128), 0) == tile, 1.0, 0.0
    ).astype(BF16)
    contract = (((0,), (0,)), ((), ()))
    step = lax.broadcasted_iota(I32, (SEG_PAD, 128), 0)
    live = (step < SEG) & (step + segment * SEG < count)
    for values, out, unused in ((within, block_ref, -1), (owner, lane_ref, 0)):
        all_ref[0:SLOTS] = lax.dot_general(
            values.astype(F32).astype(BF16), pick, contract, preferred_element_type=F32
        )
        all_ref[SLOTS:] = jnp.zeros_like(all_ref[SLOTS:])
        total = jnp.zeros((SEG_PAD, 128), F32)
        for part in range(SEGS):
            rows = all_ref[part * SEG : part * SEG + SEG_PAD]
            total = jnp.where(segment == part, rows, total)
        out[...] = jnp.where(live, (total + 0.5).astype(I32), unused)
    invert(block_ref, lane_ref, left_ref, right_ref, row_ref, col_ref, SEG, CAP)


def render(
    source_ref, source_ninth_ref, block_ref, lane_ref, row_ref, col_ref, lanes_ref, target_ref,
    rendered_ref, gradient_ref,
    rows_ref, ninth_ref, pre_ref, alpha_ref, weight_ref,
    trans_ref, colour_ref, behind_ref, moment_ref, grad_ref, grad_ninth_ref,
    back_ref, back_ninth_ref, split_ref, split_back_ref,
):
    gather(
        source_ref, source_ninth_ref, block_ref, lane_ref, rows_ref, ninth_ref, split_ref,
        SEG, CAP, 12, 11,
    )
    tile = lanes_ref[0:1]
    segment = lanes_ref[1:2]
    segments = lanes_ref[2:3]
    origin_x = lanes_ref[4:5].astype(F32)
    origin_y = lanes_ref[5:6].astype(F32)
    sub = lax.broadcasted_iota(I32, (8, 128), 0).astype(F32) + 0.5

    def wide(row):
        return jnp.broadcast_to(row, (8, 128))

    def prepare(step, carry):
        attrs = rows_ref[step]
        screen_x = attrs[0:1] - origin_x
        screen_y = attrs[1:2] - origin_y
        curve_x = wide(-0.5 * LOG2_E * attrs[2:3])
        curve_xy = wide(-LOG2_E * attrs[3:4])
        for half in range(2):
            delta = (sub + 8.0 * half) - wide(screen_x)
            pre_ref[step, half] = curve_x * delta * delta
            pre_ref[step, 2 + half] = curve_xy * delta
            pre_ref[step, 9 + half] = delta
        pre_ref[step, 4] = wide(screen_y)
        pre_ref[step, 5] = wide(-0.5 * LOG2_E * attrs[4:5])
        pre_ref[step, 6] = wide(attrs[5:6])
        pre_ref[step, 7] = wide(attrs[6:7])
        pre_ref[step, 8] = wide(attrs[7:8])
        pre_ref[step, 11] = wide(ninth_ref[pl.ds(step, 1), :])
        return carry

    repeat(SEG, SHORT_UNROLL, prepare, 0)

    def place(index):
        half, block = index % 2, index // 2
        rows = [pl.ds((2 * (GROUP * block + k) + half) * 8, 8) for k in range(GROUP)]
        return half, GROUP * block + MIDDLE + 0.5, rows

    for index in range(PASSES):
        half, middle, rows = place(index)

        def one_step(step, state):
            trans, red, green, blue = (list(part) for part in state)
            opacity, curve_y = pre_ref[step, 6], pre_ref[step, 5]
            colours = (pre_ref[step, 7], pre_ref[step, 8], pre_ref[step, 11])
            delta_y = middle - pre_ref[step, 4]
            bend = curve_y * delta_y
            slant = pre_ref[step, 2 + half] + bend
            twice = curve_y + curve_y
            powers = [None] * GROUP
            powers[MIDDLE] = pre_ref[step, half] + slant * delta_y
            slant = slant + bend
            rise, fall = curve_y + slant, curve_y - slant
            for k in range(MIDDLE + 1, GROUP):
                powers[k] = powers[k - 1] + rise
                rise = rise + twice
            for k in range(MIDDLE - 1, -1, -1):
                powers[k] = powers[k + 1] + fall
                fall = fall + twice
            for k in range(GROUP):
                alpha = opacity * jnp.exp2(powers[k])
                weight = alpha * trans[k]
                trans[k] = trans[k] - weight
                red[k] = red[k] + colours[0] * weight
                green[k] = green[k] + colours[1] * weight
                blue[k] = blue[k] + colours[2] * weight
                alpha_ref[index, step, k] = alpha
                weight_ref[index, step, k] = weight
            return tuple(trans), tuple(red), tuple(green), tuple(blue)

        ones = tuple(jnp.ones((8, 128), F32) for _ in range(GROUP))
        zeros = tuple(jnp.zeros((8, 128), F32) for _ in range(GROUP))
        state = repeat(SEG, STEP_UNROLL, one_step, (ones, zeros, zeros, zeros))
        for k in range(GROUP):
            trans_ref[rows[k], :] = state[0][k]
            for channel in range(3):
                colour_ref[channel, rows[k], :] = state[1 + channel][k]

    through = trans_ref[...]
    start = jnp.where(segment == 0, 1.0, pltpu.roll(through, 1, 1))
    for shift in (1, 2, 4, 8):
        start = start * jnp.where(segment >= shift, pltpu.roll(start, shift, 1), 1.0)
    pick = jnp.where(lax.broadcasted_iota(I32, (TILES, 128), 0) == tile, 1.0, 0.0)
    colours = [colour_ref[channel] for channel in range(3)]
    images = lax.dot_general(
        pick, jnp.concatenate([colour * start for colour in colours], axis=0),
        (((1,), (1,)), ((), ())),
        preferred_element_type=F32, precision=lax.Precision.HIGHEST,
    )
    errors = []
    for channel in range(3):
        image = images[:, 256 * channel : 256 * channel + 256]
        rendered_ref[channel] = image
        errors.append((image - target_ref[channel]) * (1.0 / 256.0))
    spread = lax.dot_general(
        jnp.concatenate(errors, axis=1), pick, (((0,), (0,)), ((), ())),
        preferred_element_type=F32, precision=lax.Precision.HIGHEST,
    )
    behind = jnp.zeros((256, 128), F32)
    for channel in range(3):
        part = spread[256 * channel : 256 * channel + 256]
        behind = behind + part * colours[channel]
        colour_ref[channel] = part * start
    left = segments - 1 - segment
    factor = jnp.where(left >= 1, pltpu.roll(through, 127, 1), 0.0)
    behind = jnp.where(left >= 1, pltpu.roll(behind, 127, 1), 0.0)
    for shift in (1, 2, 4, 8):
        reach = left >= shift
        behind = behind + factor * jnp.where(reach, pltpu.roll(behind, 128 - shift, 1), 0.0)
        factor = factor * jnp.where(reach, pltpu.roll(factor, 128 - shift, 1), 0.0)
    behind_ref[...] = behind * start

    for index in range(PASSES):
        half, middle, rows = place(index)
        errors = [[colour_ref[channel, rows[k], :] for channel in range(3)] for k in range(GROUP)]

        def one_step(count, state):
            step = SEG - 1 - count
            state = list(state)
            colours = (pre_ref[step, 7], pre_ref[step, 8], pre_ref[step, 11])
            slopes = [None] * GROUP
            shares = [None, None, None]
            for k in range(GROUP):
                alpha = alpha_ref[index, step, k]
                weight = weight_ref[index, step, k]
                shade = (
                    colours[0] * errors[k][0]
                    + colours[1] * errors[k][1]
                    + colours[2] * errors[k][2]
                )
                gap = shade - state[k]
                state[k] = state[k] + alpha * gap
                slopes[k] = weight * gap
                for channel in range(3):
                    part = weight * errors[k][channel]
                    shares[channel] = part if k == 0 else shares[channel] + part
            flat = tilt = bend = None
            for order in (range(GROUP - 1, MIDDLE, -1), range(MIDDLE)):
                first = second = third = None
                for k in order:
                    first = slopes[k] if first is None else first + slopes[k]
                    second = first if second is None else second + first
                    third = second if third is None else third + second
                square = (third + third) - second
                flat = first if flat is None else flat + first
                bend = square if bend is None else bend + square
                tilt = second if tilt is None else tilt - second
            flat = flat + slopes[MIDDLE]
            delta_y = middle - pre_ref[step, 4]
            moved = tilt + delta_y * flat
            bend = bend + delta_y * (tilt + moved)
            for row, value, started in (
                (3 * half, flat, index > 1),
                (3 * half + 1, moved, index > 1),
                (3 * half + 2, bend, index > 1),
                (6, shares[0], index > 0),
                (7, shares[1], index > 0),
                (8, shares[2], index > 0),
            ):
                moment_ref[step, row] = moment_ref[step, row] + value if started else value
            return tuple(state)

        repeat(
            SEG, BACK_UNROLL, one_step, tuple(behind_ref[rows[k], :] for k in range(GROUP))
        )

    def finish(step, carry):
        delta = [pre_ref[step, 9], pre_ref[step, 10]]
        sums = [moment_ref[step, row] for row in range(9)]
        flat = [sums[0], sums[3]]
        tilt = [sums[1], sums[4]]
        bend = [sums[2], sums[5]]
        side = [flat[half] * delta[half] for half in range(2)]

        def total(register):
            return jnp.sum(register, axis=0, keepdims=True)

        m00 = total(flat[0] + flat[1])
        m10 = total(side[0] + side[1])
        m01 = total(tilt[0] + tilt[1])
        m20 = total(side[0] * delta[0] + side[1] * delta[1])
        m11 = total(tilt[0] * delta[0] + tilt[1] * delta[1])
        m02 = total(bend[0] + bend[1])
        attrs = rows_ref[step]
        conic_a, conic_b, conic_c = attrs[2:3], attrs[3:4], attrs[4:5]
        grad_ref[step] = jnp.concatenate(
            [
                conic_a * m10 + conic_b * m01,
                conic_b * m10 + conic_c * m01,
                -0.5 * m20,
                -m11,
                -0.5 * m02,
                m00,
                total(sums[6]),
                total(sums[7]),
            ],
            axis=0,
        )
        ninth_ref[pl.ds(step, 1), :] = total(sums[8])
        return carry

    repeat(SEG, SHORT_UNROLL, finish, 0)
    ninth_ref[SEG:SEG_PAD] = jnp.zeros((SEG_PAD - SEG, 128), F32)
    grad_ninth_ref[...] = ninth_ref[...].reshape(SEG_PAD // 8, 8, 128)
    gather(
        grad_ref, grad_ninth_ref, row_ref, col_ref, back_ref, back_ninth_ref, split_back_ref,
        CAP, SEG, 14, 6, 2,
    )
    pack_messages(back_ref, back_ninth_ref, gradient_ref)


def step_kernel(
    requests_ref, params_ref, count_ref, place_ref, slots_ref, target_ref,
    far_rendered_ref, reply_landing_ref, far_owner_row_ref, far_owner_col_ref,
    rendered_ref, owner_row_ref, owner_col_ref, store_sem,
    here_requests_ref, here_params_ref, here_count_ref, here_place_ref, here_slots_ref,
    here_target_ref, load_sem,
    request_ref, middle_ref, wanted_ref, wanted_block_ref, wanted_lane_ref,
    near_send, near_receive, near_own, far_send, far_receive, far_own,
    screen_ref, ninth_ref, out_ref, out_ninth_ref, split_ref, left_ref, right_ref,
    all_ref, slot_left_ref, slot_right_ref, block_ref, lane_ref, row_ref, col_ref, lanes_ref,
    message_ref, landing_ref, send_sem, receive_sem, own_sem, source_ref, source_ninth_ref,
    reply_ref, reply_send, reply_receive, reply_own,
    *render_refs,
):
    me = lax.axis_index("dev")
    loads = [
        pltpu.make_async_copy(far, near, load_sem.at[index])
        for index, (far, near) in enumerate(
            (
                (requests_ref, here_requests_ref),
                (params_ref, here_params_ref),
                (count_ref, here_count_ref),
                (place_ref, here_place_ref),
                (slots_ref, here_slots_ref),
                (target_ref, here_target_ref),
            )
        )
    ]
    for load in loads:
        load.start()
    greet(me)
    loads[0].wait()
    wide = jnp.concatenate(
        [here_requests_ref[...].astype(F32), jnp.zeros((128 - CAP, DEVICES), F32)], axis=0
    )
    by_device = wide.T.astype(I32).reshape(OUTER, INNER, 128)
    for inner in range(INNER):
        request_ref[inner, :, 0, :] = by_device[:, inner, :]
    await_greetings()
    near_sems = (near_send, near_receive, near_own)
    far_sems = (far_send, far_receive, far_own)
    send_requests(request_ref, middle_ref, near_sems, me)
    for load in loads[1:]:
        load.wait()
    project_all(here_params_ref, screen_ref, ninth_ref)
    forward_requests(request_ref, middle_ref, wanted_ref, near_sems, far_sems, me)
    index_tables(
        here_count_ref, here_place_ref, here_slots_ref,
        block_ref, lane_ref, row_ref, col_ref, lanes_ref, all_ref, slot_left_ref, slot_right_ref,
    )
    await_requests(middle_ref, wanted_ref, far_sems, me)
    wanted_tables(wanted_ref, wanted_block_ref, wanted_lane_ref)
    gather(
        screen_ref, ninth_ref, wanted_block_ref, wanted_lane_ref, out_ref, out_ninth_ref,
        split_ref, CAP, BLOCKS, 10, 10,
    )
    pack_messages(out_ref, out_ninth_ref, message_ref)
    sems = (send_sem, receive_sem, own_sem, me)
    send_all(message_ref, landing_ref, *sems)
    invert(
        wanted_block_ref, wanted_lane_ref, left_ref, right_ref, owner_row_ref, owner_col_ref,
        CAP, BLOCKS,
    )
    await_all(message_ref, landing_ref, *sems)
    unpack_messages(landing_ref, source_ref, source_ninth_ref)
    render(
        source_ref, source_ninth_ref, block_ref, lane_ref, row_ref, col_ref, lanes_ref,
        here_target_ref, rendered_ref, reply_ref, *render_refs,
    )
    reply_sems = (reply_send, reply_receive, reply_own, me)
    send_all(reply_ref, reply_landing_ref, *reply_sems)
    stores = [
        pltpu.make_async_copy(near, far, store_sem.at[index])
        for index, (near, far) in enumerate(
            (
                (rendered_ref, far_rendered_ref),
                (owner_row_ref, far_owner_row_ref),
                (owner_col_ref, far_owner_col_ref),
            )
        )
    ]
    for store in stores:
        store.start()
    await_all(reply_ref, reply_landing_ref, *reply_sems)
    for store in stores:
        store.wait()


def pullback_kernel(
    far_message_ref, far_row_ref, far_col_ref, image_ref, params_ref,
    rendered_ref, gradient_ref,
    message_ref, source_ref, source_ninth_ref, row_ref, col_ref,
    rows_ref, ninth_ref, split_ref, here_params_ref, here_gradient_ref, load_sem, store_sem,
):
    loads = [
        pltpu.make_async_copy(far, near, load_sem.at[index])
        for index, (far, near) in enumerate(
            (
                (far_message_ref, message_ref),
                (far_row_ref, row_ref),
                (far_col_ref, col_ref),
                (params_ref, here_params_ref),
                (image_ref, rendered_ref),
            )
        )
    ]
    for load in loads:
        load.start()
    for load in loads[:3]:
        load.wait()
    unpack_messages(message_ref, source_ref, source_ninth_ref)
    gather(
        source_ref, source_ninth_ref, row_ref, col_ref, rows_ref, ninth_ref, split_ref,
        BLOCKS, CAP, 12, 8, 2,
    )
    loads[3].wait()
    stores = []
    for group in range(OWNED // 1024):
        columns = pl.ds(group * 1024, 1024)
        eight = pl.ds(group * 8, 8)
        rows = load_rows(here_params_ref, columns)
        screen_grad = [rows_ref[eight, row, :] for row in range(8)] + [ninth_ref[eight, :]]
        screen, pullback = jax.vjp(project, rows)
        by_logit = screen_grad[5] * (1.0 / (1.0 + jnp.exp(rows[10])))
        screen_grad[5] = jnp.zeros_like(by_logit)
        (grads,) = pullback(screen_grad)
        grads[10] = by_logit
        for row in range(PARAMS):
            here_gradient_ref[row : row + 1, columns] = grads[row].reshape(1, 1024)
        stores.append(
            pltpu.make_async_copy(
                here_gradient_ref.at[:, columns], gradient_ref.at[:, columns], store_sem.at[group]
            )
        )
        stores[-1].start()
    for store in stores:
        store.wait()
    loads[4].wait()


def shape(dims, dtype=F32):
    return jax.ShapeDtypeStruct(dims, dtype)


def call(kernel, outs, specs, out_specs, scratch, name, collective=None):
    params = {"vmem_limit_bytes": VMEM_LIMIT}
    if collective is not None:
        params.update(collective_id=collective, has_side_effects=True)
    spaces = {"v": pltpu.VMEM, "s": pltpu.SMEM, "h": pltpu.HBM}
    return pl.pallas_call(
        kernel,
        out_shape=outs,
        in_specs=[pl.BlockSpec(memory_space=spaces[kind]) for kind in specs],
        out_specs=[pl.BlockSpec(memory_space=spaces[kind]) for kind in out_specs],
        scratch_shapes=scratch,
        compiler_params=pltpu.CompilerParams(**params),
        name=name,
    )


SPLIT = (3 * (CAP // 2 * 8 + 24), 256)
SPLIT_BACK = (3 * (SEG // 2 * 8 + 24), 256)
MESSAGE = (DEVICES, 3, 128)
TABLE = (CAP, 128)
STEPS = (SEG_PAD, 128)
EIGHT = (CAP, 8, 128)
NINE = (CAP // 8, 8, 128)


IMAGE = (3, TILES, 256)


def local(params, requests, tile_slots, tile_count, tile_place, target):
    vmem = pltpu.VMEM
    sems = [pltpu.SemaphoreType.DMA] * 3
    image, replies, owner_row, owner_col = call(
        step_kernel,
        [shape(IMAGE), shape(MESSAGE), shape(TABLE, I32), shape(TABLE, I32)],
        "hhhhhh",
        "hhhh",
        [
            vmem(IMAGE, F32), vmem(TABLE, I32), vmem(TABLE, I32), pltpu.SemaphoreType.DMA((3,)),
            vmem((CAP, DEVICES), I32), vmem((PARAMS, OWNED), F32),
            pltpu.SMEM((TILES,), I32), pltpu.SMEM((TILES,), I32), vmem((TILES, SLOTS), I32),
            vmem(IMAGE, F32), pltpu.SemaphoreType.DMA((6,)),
            vmem((INNER, OUTER, 1, 128), I32), vmem((INNER, OUTER, 1, 128), I32),
            vmem((OUTER, INNER, 1, 128), I32), vmem(TABLE, I32), vmem(TABLE, I32), *sems, *sems,
            vmem(EIGHT, F32), vmem(NINE, F32), vmem(EIGHT, F32), vmem(TABLE, F32),
            vmem(SPLIT, BF16),
            vmem((2 * BLOCKS, CAP * 128), BF16), vmem((128, CAP * 128), BF16),
            vmem((SEGS * SEG + 8, 128), F32),
            vmem((2 * CAP, SEG * 128), BF16), vmem((128, SEG * 128), BF16),
            vmem(STEPS, I32), vmem(STEPS, I32), vmem(TABLE, I32), vmem(TABLE, I32),
            vmem((8, 128), I32),
            vmem(MESSAGE, F32), vmem(MESSAGE, F32), *sems, vmem(EIGHT, F32), vmem(NINE, F32),
            vmem(MESSAGE, F32), *sems,
            vmem((SEG, 8, 128), F32), vmem(STEPS, F32),
            vmem((SEG, 12, 8, 128), F32),
            vmem((PASSES, SEG, GROUP, 8, 128), F32), vmem((PASSES, SEG, GROUP, 8, 128), F32),
            vmem((256, 128), F32), vmem((3, 256, 128), F32), vmem((256, 128), F32),
            vmem((SEG, 9, 8, 128), F32),
            vmem((SEG, 8, 128), F32), vmem((SEG_PAD // 8, 8, 128), F32),
            vmem(EIGHT, F32), vmem(TABLE, F32), vmem(SPLIT, BF16), vmem(SPLIT_BACK, BF16),
        ],
        "step",
        0,
    )(
        requests.reshape(DEVICES, CAP).T, params, tile_count, tile_place, tile_slots,
        target.transpose(1, 0, 2),
    )
    rendered, gradient = call(
        pullback_kernel,
        [shape(IMAGE), shape((PARAMS, OWNED))],
        "hhhhh",
        "hh",
        [
            vmem(MESSAGE, F32), vmem(EIGHT, F32), vmem(NINE, F32), vmem(TABLE, I32), vmem(TABLE, I32),
            vmem(EIGHT, F32), vmem(TABLE, F32), vmem(SPLIT, BF16), vmem((PARAMS, OWNED), F32),
            vmem((PARAMS, OWNED), F32), pltpu.SemaphoreType.DMA((5,)),
            pltpu.SemaphoreType.DMA((OWNED // 1024,)),
        ],
        "pullback",
    )(replies, owner_row, owner_col, image, params)
    return rendered.transpose(1, 0, 2), gradient


def solution(mesh):
    in_specs = (
        P(None, "dev"),
        P("dev", None, None),
        P("dev", None),
        P("dev"),
        P("dev"),
        P("dev", None, None),
    )
    out_specs = (P("dev", None, None), P(None, "dev"))
    return jax.shard_map(local, mesh=mesh, in_specs=in_specs, out_specs=out_specs, check_vma=False)
```
